32 devices in a mesh: blk: 4 (over y, x), seg: 8 (over z, core).
Axes of the slice: x: 2, y: 2, z: 4, core: 2. Of those that a mesh axis runs over, the one named last changes fastest.
Arguments:
- spectra: bfloat16 [8, 2, 2048, 2048], P('seg', None, 'blk'), may hold values from -6 to 6
- window_count: int32 [8], P('seg'), may hold values from 1 to 2, as said below
- tile_owner: int32 [4, 48], P('blk'), may hold values from 0 to 7, as said below
- phases: float32 [2, 128, 256], replicated, may hold values from -3.140625 to 3.140625
Outputs:
- tile_power: float32 [4, 8, 8, 2, 256], P('blk', 'seg')
The draws below stay inside these ranges and needn't reach their ends.
Inputs may be any that keep to these rules, and one draw needn't show every extreme that they name: `window_count`: the largest value, 2, occurs in every draw. `tile_owner`: in each row no segment index occurs more than 8 times, and some index occurs exactly 8 times.
All inputs are finite; a program needn't handle non-finite values.
Results may differ from the reference program's by a relative error of at most 0.004.
Values may be sent and summed in bfloat16 or wider, within the bound.
No kernel may reach another device: no remote copies, remote signals or barrier semaphores. Data moves between devices by JAX's collectives and lax.ppermute only.
A program may use at most 128 MiB of HBM per device.

```python
import math
import jax
import jax.numpy as jnp
from jax import lax

CH_DEV = 512
TILE = 128
FREQ = 1024
BANDS = 2
VEL = 256
CAP = 8
WIN = 2
FB = 512
SEGS = 8
BLOCKS = 4
CHANNELS = 2048
QUAD = 4
TCOL = 48


def draw_window_count(key, part):
    first_key, second_key = jax.random.split(jax.random.fold_in(key, 11))
    counted = jax.random.randint(first_key, (SEGS,), 1, WIN + 1)
    chosen = jax.random.randint(second_key, (), 0, SEGS)
    return jnp.where(jnp.arange(SEGS) == chosen, WIN, counted).astype(jnp.int32)


def draw_tile_owner(key, part):
    slot_count = SEGS * CAP

    def one_column(column_key):
        first_key, second_key, third_key = jax.random.split(column_key, 3)
        order_ids = jax.random.permutation(first_key, slot_count)
        position = jnp.argsort(order_ids)
        full_owner = jax.random.randint(second_key, (), 0, SEGS)
        score = position + jnp.where(jnp.arange(slot_count) // CAP == full_owner, 0, slot_count)
        chosen = jnp.argsort(score)[:TCOL]
        tile_perm = jax.random.permutation(third_key, TCOL)
        owners = jnp.zeros((TCOL,), jnp.int32).at[tile_perm].set((chosen // CAP).astype(jnp.int32))
        return owners
    column_keys = jax.random.split(jax.random.fold_in(key, 23), BLOCKS)
    return jax.vmap(one_column)(column_keys).astype(jnp.int32)


def levels(own_key, shape, cuts, smallest, top_value):
    loudness, own = 1.0, jax.random.fold_in(own_key, 6)
    for dim, shards_of in cuts:
        draws = jnp.exp(jax.random.uniform(jax.random.fold_in(own, dim), (shards_of,), jnp.float32, smallest / len(cuts), top_value / len(cuts)))
        loudness = loudness * jnp.repeat(draws, shape[dim] // shards_of).reshape([-1 if axis == dim else 1 for axis in range(len(shape))])
    return loudness


def bell_draw(rng, extent, scale, reach, shards=(), held_as=jnp.bfloat16):
    factor_of = levels(rng, extent, shards, -0.22, 0.18) if shards else 1.0
    result = jax.random.normal(rng, extent, jnp.float32) * scale * factor_of
    return jnp.minimum(jnp.maximum(result, -reach), reach).astype(held_as)


def setup_inputs(seed: int = 0) -> dict:
    seeds = jax.random.split(jax.random.key(seed), 5)
    spectra = bell_draw(seeds[0], (SEGS, WIN, CHANNELS, 2 * FREQ), 1.0, 6.0, ((0, 8), (2, 4)))
    window_count = draw_window_count(jax.random.fold_in(seeds[4], 71), 0)
    tile_owner = draw_tile_owner(jax.random.fold_in(seeds[4], 71), 0)
    phases = jnp.clip(jax.random.uniform(seeds[3], (BANDS, TILE, VEL), jnp.float32, -3.140625, 3.140625), -3.140625, 3.140625)
    return {"spectra": spectra, "window_count": window_count, "tile_owner": tile_owner, "phases": phases}


def prepare(segment_data, counted):
    spectrum = segment_data.astype(jnp.float32).reshape(WIN, CHANNELS, BANDS, 2, FB)
    scaling = lax.rsqrt(lax.optimization_barrier(jnp.mean(spectrum * spectrum, axis=(2, 3, 4))) + 1e-05)
    live_mask = (jnp.arange(WIN, dtype=jnp.int32) < counted).astype(jnp.float32)
    return (spectrum * scaling[:, :, None, None, None] * live_mask[:, None, None, None, None]).astype(jnp.bfloat16)

def correlate(resident, visiting, weight):
    flipped = jnp.stack([-visiting[:, :, :, 1], visiting[:, :, :, 0]], axis=3)
    both_parts = jnp.stack([visiting, flipped], axis=1)
    left_side = resident.astype(jnp.float32).reshape(WIN, QUAD, TILE, BANDS, 2 * FB)
    right_side = both_parts.astype(jnp.float32).reshape(WIN, 2, QUAD, TILE, BANDS, 2 * FB)
    product = jnp.einsum('wqibk,wpsjbk->qsbipj', left_side, right_side, precision=lax.Precision.HIGHEST)
    return (product * weight).astype(jnp.bfloat16).reshape(QUAD * QUAD, BANDS, TILE, 2 * TILE)

def disperse(stacked, phases):
    norm_factor = 1.0 / math.sqrt(TILE)
    cosine = (jnp.cos(phases) * norm_factor).astype(jnp.bfloat16)
    sine_part = (jnp.sin(phases) * norm_factor).astype(jnp.bfloat16)
    upper = jnp.concatenate([cosine, sine_part], axis=2)
    lower = jnp.concatenate([-sine_part, cosine], axis=2)
    matrix = jnp.concatenate([upper, lower], axis=1).astype(jnp.float32)
    field = jnp.einsum('nbij,bjv->nbiv', stacked.astype(jnp.float32), matrix, precision=lax.Precision.HIGHEST)
    squared = field * field
    energy = squared[..., :VEL] + squared[..., VEL:]
    return lax.optimization_barrier(jnp.mean(energy, axis=2))

def slot_table(owner_row, segments):
    count_tiles = owner_row.shape[0]
    order_ids = jnp.arange(count_tiles, dtype=jnp.int32)
    same_owner = owner_row[:, None] == owner_row[None, :]
    earlier = order_ids[None, :] < order_ids[:, None]
    rank_of = lax.optimization_barrier(jnp.sum(jnp.where(same_owner & earlier, 1, 0), axis=1)).astype(jnp.int32)
    slot_ids = owner_row * CAP + rank_of
    grid_ids = jnp.arange(segments * CAP, dtype=jnp.int32)
    matches = grid_ids[:, None] == slot_ids[None, :]
    tile_of_slot = lax.optimization_barrier(jnp.sum(jnp.where(matches, order_ids[None, :], 0), axis=1)).astype(jnp.int32)
    filled = jnp.any(matches, axis=1)
    return (tile_of_slot, filled)

def reference(spectra, window_count, tile_owner, phases):

    def one_block(block_index):

        def add_segment(segment, running):
            segment_data = lax.dynamic_index_in_dim(spectra, segment, 0, keepdims=False)
            counted = lax.dynamic_index_in_dim(window_count, segment, 0, keepdims=False)
            whitened = prepare(segment_data, counted)
            weight = 1.0 / (counted.astype(jnp.float32) * math.sqrt(FB * SEGS))
            resident = lax.dynamic_slice_in_dim(whitened, (block_index * CH_DEV).astype(jnp.int32), CH_DEV, 1)
            pieces = []
            for shift_step in range(BLOCKS // 2 + 1):
                start = ((block_index + shift_step) % BLOCKS * CH_DEV).astype(jnp.int32)
                visiting = lax.dynamic_slice_in_dim(whitened, start, CH_DEV, 1)
                pieces.append(correlate(resident, visiting, weight))
            return running + jnp.concatenate(pieces, axis=0).astype(jnp.float32)
        initial = jnp.zeros((TCOL, BANDS, TILE, 2 * TILE), jnp.float32)
        stacked = lax.fori_loop(0, SEGS, add_segment, initial).astype(jnp.bfloat16)
        powers = disperse(stacked, phases)
        owner_row = lax.dynamic_index_in_dim(tile_owner, block_index, 0, keepdims=False)
        tile_of_slot, filled = slot_table(owner_row, SEGS)
        placed = jnp.take(powers, tile_of_slot, axis=0) * filled[:, None, None].astype(jnp.float32)
        return placed.reshape(SEGS, CAP, BANDS, VEL)
    return lax.map(one_block, jnp.arange(BLOCKS, dtype=jnp.int32))
```

```python
import functools
import math

import jax
import jax.numpy as jnp
import numpy as np
from jax import lax
from jax.experimental import pallas as pl
from jax.experimental.pallas import tpu as pltpu
from jax.sharding import PartitionSpec as P

TILE = 128
BANDS = 2
CAP = 8
FB = 512
QUAD = 4
VMEM_LIMIT = 48 * 1024 * 1024


def from_behind(array, axis, by):
    devices = lax.axis_size(axis)
    return lax.ppermute(array, axis, [(i, (i + by) % devices) for i in range(devices)])


def prepare(segment_data, counted):
    windows = segment_data.shape[0]
    channels = segment_data.shape[1]
    spectrum = segment_data.astype(jnp.float32).reshape(windows, channels, BANDS, 2, FB)
    scaling = lax.rsqrt(jnp.mean(spectrum * spectrum, axis=(2, 3, 4)) + 1e-05)
    live_mask = (jnp.arange(windows, dtype=jnp.int32) < counted).astype(jnp.float32)
    return (
        spectrum * scaling[:, :, None, None, None] * live_mask[:, None, None, None, None]
    ).astype(jnp.bfloat16)


def correlate(resident, visiting, weight):
    windows = resident.shape[0]
    flipped = jnp.stack([-visiting[:, :, :, 1], visiting[:, :, :, 0]], axis=3)
    both_parts = jnp.stack([visiting, flipped], axis=1)
    left_side = resident.reshape(windows, QUAD, TILE, BANDS, 2 * FB)
    right_side = both_parts.reshape(windows, 2, QUAD, TILE, BANDS, 2 * FB)
    product = jnp.einsum(
        "wqibk,wpsjbk->qsbipj", left_side, right_side, preferred_element_type=jnp.float32
    )
    return (product * weight).astype(jnp.bfloat16).reshape(QUAD * QUAD, BANDS, TILE, 2 * TILE)


def phase_matrix(phases):
    norm_factor = 1.0 / math.sqrt(TILE)
    cosine = (jnp.cos(phases) * norm_factor).astype(jnp.bfloat16)
    sine_part = (jnp.sin(phases) * norm_factor).astype(jnp.bfloat16)
    upper = jnp.concatenate([cosine, sine_part], axis=2)
    lower = jnp.concatenate([-sine_part, cosine], axis=2)
    return jnp.concatenate([upper, lower], axis=1)


def disperse(stacked, phases):
    velocity_count = phases.shape[2]
    matrix = phase_matrix(phases)
    field = jnp.einsum("nbij,bjv->nbiv", stacked, matrix, preferred_element_type=jnp.float32)
    squared = field * field
    energy = squared[..., :velocity_count] + squared[..., velocity_count:]
    return jnp.mean(energy, axis=2)


def slot_table(owner_row, segments):
    count_tiles = owner_row.shape[0]
    order_ids = jnp.arange(count_tiles, dtype=jnp.int32)
    same_owner = owner_row[:, None] == owner_row[None, :]
    earlier = order_ids[None, :] < order_ids[:, None]
    rank_of = jnp.sum(jnp.where(same_owner & earlier, 1, 0), axis=1).astype(jnp.int32)
    slot_ids = owner_row * CAP + rank_of
    grid_ids = jnp.arange(segments * CAP, dtype=jnp.int32)
    matches = grid_ids[:, None] == slot_ids[None, :]
    tile_of_slot = jnp.sum(jnp.where(matches, order_ids[None, :], 0), axis=1)
    filled = jnp.any(matches, axis=1)
    return (tile_of_slot, filled)


def my_slots(owner_row, segments):
    tile_of_slot, filled = slot_table(owner_row, segments)
    my_start = lax.axis_index("seg") * CAP
    mine = lax.dynamic_slice_in_dim(tile_of_slot, my_start, CAP, 0)
    mine_filled = lax.dynamic_slice_in_dim(filled, my_start, CAP, 0)
    return mine, mine_filled


def ring_body(spectra, window_count, tile_owner, phases):
    blocks = lax.axis_size("blk")
    segments = lax.axis_size("seg")
    counted = window_count[0]
    whitened = prepare(spectra[0], counted)
    weight = 1.0 / (counted.astype(jnp.float32) * math.sqrt(FB * segments))
    pieces = [correlate(whitened, whitened, weight)]
    moving = whitened
    for shift_step in range(1, blocks // 2 + 1):
        moving = from_behind(moving, "blk", -1)
        pieces.append(correlate(whitened, moving, weight))
    all_tiles = jnp.concatenate(pieces, axis=0)
    share_rows = (
        lax.psum_scatter(all_tiles, "seg", scatter_dimension=0, tiled=True)
        .astype(jnp.float32)
        .astype(jnp.bfloat16)
    )
    share_power = disperse(share_rows, phases)
    every_power = lax.all_gather(share_power, "seg", axis=0, tiled=True)
    mine, mine_filled = my_slots(tile_owner[0], segments)
    response = jnp.take(every_power, mine, axis=0) * mine_filled[:, None, None].astype(jnp.float32)
    return response[None, None]


UNITS = 2 * QUAD
X_SWAP = [(0, 1), (1, 0), (2, 3), (3, 2)]
Y_SWAP = [(0, 2), (2, 0), (1, 3), (3, 1)]
DIAGONAL = [(0, 3), (3, 0), (1, 2), (2, 1)]
X_EXTRA = [(1, 0), (2, 3)]
Y_EXTRA = [(2, 0), (1, 3)]
BAND_TO_X = np.array([0, 1, 0, 1], np.int32)
BAND_TO_Y = np.array([1, 1, 0, 0], np.int32)
BAND_EXTRA = np.array([0, 0, 1, 1], np.int32)
BAND_FROM_X = BAND_TO_X[[1, 0, 3, 2]]
BAND_FROM_Y = BAND_TO_Y[[2, 3, 0, 1]]
OWN_AT, PAIR_AT, TURNED_AT, CORNER_AT, POWER_ROWS = 0, QUAD, 2 * QUAD, 3 * QUAD, 3 * QUAD + 2


def corner_plan():
    plan = np.zeros((4, UNITS, 5), np.int32)
    for n in range(UNITS):
        m = n - QUAD
        plan[0, n] = (2, 0, 1, n, 0) if m < 0 else (0, m & 1, 3, m >> 1, 1)
        plan[3, n] = (3, 0, 0, n, 0) if m < 0 else (1, m & 1, 2, m >> 1, 1)
        plan[1, n] = (1, n >> 2, 0, n & 3, 0)
        plan[2, n] = (0, n >> 2, 1, n & 3, 1)
    return plan


def source_table():
    table = np.full((4, 3 * QUAD * QUAD, BANDS), -1, np.int64)

    def put(block, step, p, q, band, chip, unit, row):
        at = (unit * 4 + (chip ^ block)) * POWER_ROWS + row
        table[block, (step * QUAD + p) * QUAD + q, band] = at

    for chip in range(4):
        for unit in range(UNITS):
            q = unit % QUAD
            for p in range(QUAD):
                put(chip, 0, p, q, unit // QUAD, chip, unit, OWN_AT + p)
                if unit < QUAD:
                    band = BAND_FROM_X[chip]
                    if chip % 2 == 0:
                        put(chip, 1, p, q, band, chip, unit, PAIR_AT + p)
                    else:
                        put(chip ^ 1, 1, q, p, band, chip, unit, TURNED_AT + p)
                else:
                    band = BAND_FROM_Y[chip]
                    put(chip, 2, p, q, band, chip, unit, PAIR_AT + p)
                    put(chip ^ 2, 2, q, p, band, chip, unit, TURNED_AT + p)
            for i in range(2):
                if chip in (1, 2):
                    put(3, 1, 2 * (unit >> 2) + i, q, chip - 1, chip, unit, CORNER_AT + i)
                elif unit < QUAD:
                    put(1, 1, (2 if chip == 3 else 0) + i, q, 0, chip, unit, CORNER_AT + i)
                else:
                    m = unit - QUAD
                    at_q = (m >> 1) + (2 if chip == 0 else 0)
                    put(1, 1, 2 * (m & 1) + i, at_q, 1, chip, unit, CORNER_AT + i)
    assert table.min() >= 0
    return table.astype(np.int32)


CORNERS = corner_plan()
SOURCES = source_table()


def params():
    return pltpu.CompilerParams(vmem_limit_bytes=VMEM_LIMIT)


def whiten_kernel(info, spectra, whole, to_x, to_y, extra_x, extra_y):
    step = pl.program_id(0)
    windows = spectra.shape[0]
    half = pl.num_programs(0) // 2
    for w in range(windows):
        values = spectra[w].astype(jnp.float32)
        scaling = lax.rsqrt(jnp.mean(values * values, axis=1, keepdims=True) + 1e-05)
        scaling = scaling * jnp.where(w < info[0], 1.0, 0.0)
        out = (values * scaling).astype(jnp.bfloat16)
        width = out.shape[1] // BANDS
        for band in range(BANDS):
            whole[band, w] = out[:, band * width : (band + 1) * width]
    to_x[...] = whole[info[1]]
    to_y[...] = whole[info[2]]

    @pl.when(step < half)
    def _():
        extra_x[...] = whole[info[3]]

    @pl.when(step >= half)
    def _():
        extra_y[...] = whole[info[3]]


def whiten(spectra, info):
    windows, channels, width = spectra.shape
    band_width = width // BANDS
    steps = channels // TILE
    half = steps // 2
    band_block = (windows, TILE, band_width)
    full = jax.ShapeDtypeStruct((windows, channels, band_width), jnp.bfloat16)
    part = jax.ShapeDtypeStruct((windows, channels // 2, band_width), jnp.bfloat16)
    return pl.pallas_call(
        whiten_kernel,
        grid_spec=pltpu.PrefetchScalarGridSpec(
            num_scalar_prefetch=1,
            grid=(steps,),
            in_specs=[pl.BlockSpec((windows, TILE, width), lambda i, s: (0, i, 0))],
            out_specs=[
                pl.BlockSpec((BANDS,) + band_block, lambda i, s: (0, 0, i, 0)),
                pl.BlockSpec(band_block, lambda i, s: (0, i, 0)),
                pl.BlockSpec(band_block, lambda i, s: (0, i, 0)),
                pl.BlockSpec(band_block, lambda i, s: (0, jnp.minimum(i, half - 1), 0)),
                pl.BlockSpec(band_block, lambda i, s: (0, jnp.maximum(i - half, 0), 0)),
            ],
        ),
        out_shape=[
            jax.ShapeDtypeStruct((BANDS, windows, channels, band_width), jnp.bfloat16),
            full,
            full,
            part,
            part,
        ],
        compiler_params=params(),
        cost_estimate=pl.CostEstimate(
            flops=8 * spectra.size, bytes_accessed=14 * 2**20, transcendentals=0
        ),
    )(info, spectra)


def product(left, right, weight):
    total = None
    for w in range(len(left)):
        r = right[w]
        width = r.shape[1] // 2
        turned = jnp.concatenate([-r[:, width:], r[:, :width]], axis=1)
        both = jnp.concatenate([r, turned], axis=0)
        part = lax.dot_general(
            left[w], both, (((1,), (1,)), ((), ())), preferred_element_type=jnp.float32
        )
        total = part if total is None else total + part
    return (total * weight).astype(jnp.bfloat16)


def own_kernel(info, weight, left, right, out):
    windows = left.shape[1]
    out[0] = product(
        [left[0, w] for w in range(windows)], [right[0, w] for w in range(windows)], weight[0]
    )


def pair_kernel(info, weight, left, from_x, from_y, out, held):
    windows = left.shape[1]
    is_x = info[pl.program_id(0)] < QUAD

    @pl.when(is_x)
    def _():
        held[...] = from_x[...]

    @pl.when(jnp.logical_not(is_x))
    def _():
        held[...] = from_y[...]

    out[0] = product(
        [left[0, w] for w in range(windows)], [held[w] for w in range(windows)], weight[0]
    )


def corner_kernel(info, weight, from_x, from_y, extra_x, extra_y, out, left, right):
    windows = left.shape[0]
    at = 5 * info[pl.program_id(0)] + UNITS
    rows = left.shape[1]
    for pick, ref in enumerate((from_x, from_y, extra_x, extra_y)):

        @pl.when(info[at] == pick)
        def _():
            left[...] = ref[:, pl.ds(pl.multiple_of(info[at + 1] * rows, rows), rows), :]

        @pl.when(info[at + 2] == pick)
        def _():
            right[...] = ref[:, pl.ds(pl.multiple_of(info[at + 3] * TILE, TILE), TILE), :]

    out[0] = product(
        [left[w] for w in range(windows)], [right[w] for w in range(windows)], weight[0]
    )


def unit_call(kernel, info, weight, arrays, specs, count, rows, scratch):
    windows, width = arrays[0].shape[-3], arrays[0].shape[-1]
    return pl.pallas_call(
        kernel,
        grid_spec=pltpu.PrefetchScalarGridSpec(
            num_scalar_prefetch=2,
            grid=(count,),
            in_specs=specs,
            out_specs=pl.BlockSpec((1, rows, 2 * TILE), lambda i, s, t: (i, 0, 0)),
            scratch_shapes=scratch,
        ),
        out_shape=jax.ShapeDtypeStruct((count, rows, 2 * TILE), jnp.bfloat16),
        compiler_params=params(),
        cost_estimate=pl.CostEstimate(
            flops=2 * count * windows * rows * width * 2 * TILE,
            bytes_accessed=6 * 2**20,
            transcendentals=0,
        ),
    )(info, weight, *arrays)


def own_units(units, weight, whole):
    bands, windows, channels, width = whole.shape
    specs = [
        pl.BlockSpec((1, windows, channels, width), lambda i, s, t: (s[i] // QUAD, 0, 0, 0)),
        pl.BlockSpec((1, windows, TILE, width), lambda i, s, t: (s[i] // QUAD, 0, s[i] % QUAD, 0)),
    ]
    return unit_call(
        own_kernel, units, weight, (whole, whole), specs, units.shape[0], channels, []
    )


def pair_units(units, bands, weight, whole, from_x, from_y):
    _, windows, channels, width = whole.shape
    count = units.shape[0]
    info = jnp.concatenate([units, bands])
    tile = (windows, TILE, width)
    specs = [
        pl.BlockSpec(
            (1, windows, channels, width),
            lambda i, s, t: (jnp.where(s[i] < QUAD, s[count], s[count + 1]), 0, 0, 0),
        ),
        pl.BlockSpec(tile, lambda i, s, t: (0, s[i] % QUAD, 0)),
        pl.BlockSpec(tile, lambda i, s, t: (0, s[i] % QUAD, 0)),
    ]
    scratch = [pltpu.VMEM(tile, jnp.bfloat16)]
    return unit_call(
        pair_kernel, info, weight, (whole, from_x, from_y), specs, count, channels, scratch
    )


def corner_units(units, plan, weight, from_x, from_y, extra_x, extra_y):
    windows, channels, width = from_x.shape
    count = units.shape[0]
    info = jnp.concatenate([units, jnp.zeros((UNITS - count,), jnp.int32), plan.reshape(-1)])
    arrays = (from_x, from_y, extra_x, extra_y)
    specs = [pl.BlockSpec(a.shape, lambda i, s, t: (0, 0, 0)) for a in arrays]
    rows = channels // 2
    scratch = [
        pltpu.VMEM((windows, rows, width), jnp.bfloat16),
        pltpu.VMEM((windows, TILE, width), jnp.bfloat16),
    ]
    return unit_call(corner_kernel, info, weight, arrays, specs, count, rows, scratch)


def pair_sum_kernel(kept, got, *outs):
    for r, out in enumerate(outs):
        out[...] = (kept[r].astype(jnp.float32) + got[r].astype(jnp.float32)).astype(jnp.bfloat16)


def pair_sum(kept, got):
    shape = jax.ShapeDtypeStruct(kept.shape[1:], jnp.bfloat16)
    return pl.pallas_call(
        pair_sum_kernel,
        out_shape=[shape] * kept.shape[0],
        compiler_params=params(),
        cost_estimate=pl.CostEstimate(
            flops=kept.size, bytes_accessed=6 * kept.size, transcendentals=0
        ),
    )(kept, got)


def power_kernel(turn, info, matrix, *refs):
    parts, out = refs[:-1], refs[-1]
    total = parts[0][...].astype(jnp.float32)
    for part in parts[1:]:
        total = total + part[...].astype(jnp.float32)
    stacked = total.astype(jnp.bfloat16)
    table = matrix[info[0]]
    tiles = stacked.shape[0] // TILE
    velocities = table.shape[1] // 2

    def powers(rows):
        field = lax.dot_general(
            rows, table, (((1,), (0,)), ((), ())), preferred_element_type=jnp.float32
        )
        squared = field * field
        energy = squared[:, :velocities] + squared[:, velocities:]
        return [
            jnp.sum(energy[t * TILE : (t + 1) * TILE], axis=0, keepdims=True) * (1.0 / TILE)
            for t in range(tiles)
        ]

    found = powers(stacked)
    if turn:
        rounded = stacked.astype(jnp.float32)
        turned = []
        for t in range(tiles):
            tile = rounded[t * TILE : (t + 1) * TILE]
            turned.append(jnp.concatenate([tile[:, :TILE].T, -tile[:, TILE:].T], axis=1))
        found += powers(jnp.concatenate(turned, axis=0).astype(jnp.bfloat16))
    for t, row in enumerate(found):
        out[t : t + 1, :] = row


def power_of(parts, matrix, band, turn):
    tiles = parts[0].shape[0] // TILE
    velocities = matrix.shape[2] // 2
    vmem = pl.BlockSpec(memory_space=pltpu.VMEM)
    return pl.pallas_call(
        functools.partial(power_kernel, turn),
        in_specs=[pl.BlockSpec(memory_space=pltpu.SMEM)] + [vmem] * (1 + len(parts)),
        out_shape=jax.ShapeDtypeStruct((tiles * (2 if turn else 1), velocities), jnp.float32),
        compiler_params=params(),
        cost_estimate=pl.CostEstimate(
            flops=4 * parts[0].size * velocities,
            bytes_accessed=2 * parts[0].size * len(parts),
            transcendentals=0,
        ),
    )(band, matrix, *parts)


def grid_body(spectra, window_count, tile_owner, phases):
    segments = lax.axis_size("seg")
    layers = segments // 2
    chip = lax.axis_index("blk")
    me = lax.axis_index("seg")
    layer, core = me // 2, me % 2
    pick = lambda table: jnp.asarray(table)[chip]
    counted = window_count[0]
    weight = (1.0 / (counted.astype(jnp.float32) * math.sqrt(FB * segments))).reshape(1)
    info = jnp.stack([counted, pick(BAND_TO_X), pick(BAND_TO_Y), pick(BAND_EXTRA)])
    whole, to_x, to_y, extra_x, extra_y = whiten(spectra[0], info)
    from_x = lax.ppermute(to_x, "blk", X_SWAP)
    from_y = lax.ppermute(to_y, "blk", Y_SWAP)
    extra_x, extra_y, from_x, from_y = lax.optimization_barrier(
        (extra_x, extra_y, from_x, from_y)
    )
    got_x = lax.ppermute(extra_x, "blk", X_EXTRA)
    got_y = lax.ppermute(extra_y, "blk", Y_EXTRA)
    matrix = phase_matrix(phases)
    mine, mine_filled = my_slots(tile_owner[0], segments)

    ahead = (layer + jnp.arange(layers, dtype=jnp.int32)) % layers
    kept_units = 2 * ahead + core
    sent_units = 2 * ahead + 1 - core

    def reduce(make):
        sent = make(sent_units)
        got = lax.ppermute(sent, "seg", [(i, i ^ 1) for i in range(segments)])
        sums = pair_sum(make(kept_units), got)
        parts = [sums[0]]
        for r in range(1, layers):
            parts.append(
                lax.ppermute(sums[r], "seg", [(i, (i + 2 * r) % segments) for i in range(segments)])
            )
        return parts

    own = reduce(lambda units: own_units(units, weight, whole))
    pair_bands = jnp.stack([pick(BAND_FROM_X), pick(BAND_FROM_Y)])
    pair = reduce(lambda units: pair_units(units, pair_bands, weight, whole, from_x, from_y))
    plan = pick(CORNERS)
    corner = reduce(
        lambda units: corner_units(units, plan, weight, from_x, from_y, got_x, got_y)
    )
    own_power = power_of(own, matrix, (me // QUAD).reshape(1), False)
    pair_power = power_of(pair, matrix, pair_bands[me // QUAD].reshape(1), True)
    corner_power = power_of(corner, matrix, plan[me, 4].reshape(1), False)
    powers = jnp.concatenate([own_power, pair_power, corner_power], axis=0)
    there = [powers] + [lax.ppermute(powers, "blk", swap) for swap in (X_SWAP, Y_SWAP, DIAGONAL)]
    every = lax.all_gather(jnp.stack(there), "seg", axis=0)
    velocities = every.shape[-1]
    rows = pick(SOURCES)[mine]
    response = jnp.take(every.reshape(-1, velocities), rows, axis=0)
    response = response * mine_filled[:, None, None].astype(jnp.float32)
    return response[None, None]


def solution(mesh):
    placed = (P("seg", None, "blk", None), P("seg"), P("blk", None), P())
    fits = mesh.shape["blk"] == 4 and mesh.shape["seg"] == UNITS
    return jax.shard_map(
        grid_body if fits else ring_body,
        mesh=mesh,
        in_specs=placed,
        out_specs=P("blk", "seg", None, None, None),
        check_vma=False,
    )
```

```python
import functools
import math

import jax
import jax.numpy as jnp
import numpy as np
from jax import lax
from jax.experimental import pallas as pl
from jax.experimental.pallas import tpu as pltpu
from jax.sharding import PartitionSpec as P

TILE = 128
BANDS = 2
CAP = 8
FB = 512
QUAD = 4
VMEM_LIMIT = 48 * 1024 * 1024


def from_behind(array, axis, by):
    devices = lax.axis_size(axis)
    return lax.ppermute(array, axis, [(i, (i + by) % devices) for i in range(devices)])


def prepare(segment_data, counted):
    windows = segment_data.shape[0]
    channels = segment_data.shape[1]
    spectrum = segment_data.astype(jnp.float32).reshape(windows, channels, BANDS, 2, FB)
    scaling = lax.rsqrt(jnp.mean(spectrum * spectrum, axis=(2, 3, 4)) + 1e-05)
    live_mask = (jnp.arange(windows, dtype=jnp.int32) < counted).astype(jnp.float32)
    return (
        spectrum * scaling[:, :, None, None, None] * live_mask[:, None, None, None, None]
    ).astype(jnp.bfloat16)


def correlate(resident, visiting, weight):
    windows = resident.shape[0]
    flipped = jnp.stack([-visiting[:, :, :, 1], visiting[:, :, :, 0]], axis=3)
    both_parts = jnp.stack([visiting, flipped], axis=1)
    left_side = resident.reshape(windows, QUAD, TILE, BANDS, 2 * FB)
    right_side = both_parts.reshape(windows, 2, QUAD, TILE, BANDS, 2 * FB)
    product = jnp.einsum(
        "wqibk,wpsjbk->qsbipj", left_side, right_side, preferred_element_type=jnp.float32
    )
    return (product * weight).astype(jnp.bfloat16).reshape(QUAD * QUAD, BANDS, TILE, 2 * TILE)


def phase_matrix(phases):
    norm_factor = 1.0 / math.sqrt(TILE)
    cosine = (jnp.cos(phases) * norm_factor).astype(jnp.bfloat16)
    sine_part = (jnp.sin(phases) * norm_factor).astype(jnp.bfloat16)
    upper = jnp.concatenate([cosine, sine_part], axis=2)
    lower = jnp.concatenate([-sine_part, cosine], axis=2)
    return jnp.concatenate([upper, lower], axis=1)


def disperse(stacked, phases):
    velocity_count = phases.shape[2]
    matrix = phase_matrix(phases)
    field = jnp.einsum("nbij,bjv->nbiv", stacked, matrix, preferred_element_type=jnp.float32)
    squared = field * field
    energy = squared[..., :velocity_count] + squared[..., velocity_count:]
    return jnp.mean(energy, axis=2)


def slot_table(owner_row, segments):
    count_tiles = owner_row.shape[0]
    order_ids = jnp.arange(count_tiles, dtype=jnp.int32)
    same_owner = owner_row[:, None] == owner_row[None, :]
    earlier = order_ids[None, :] < order_ids[:, None]
    rank_of = jnp.sum(jnp.where(same_owner & earlier, 1, 0), axis=1).astype(jnp.int32)
    slot_ids = owner_row * CAP + rank_of
    grid_ids = jnp.arange(segments * CAP, dtype=jnp.int32)
    matches = grid_ids[:, None] == slot_ids[None, :]
    tile_of_slot = jnp.sum(jnp.where(matches, order_ids[None, :], 0), axis=1)
    filled = jnp.any(matches, axis=1)
    return (tile_of_slot, filled)


def my_slots(owner_row, segments):
    tile_of_slot, filled = slot_table(owner_row, segments)
    my_start = lax.axis_index("seg") * CAP
    mine = lax.dynamic_slice_in_dim(tile_of_slot, my_start, CAP, 0)
    mine_filled = lax.dynamic_slice_in_dim(filled, my_start, CAP, 0)
    return mine, mine_filled


def ring_body(spectra, window_count, tile_owner, phases):
    blocks = lax.axis_size("blk")
    segments = lax.axis_size("seg")
    counted = window_count[0]
    whitened = prepare(spectra[0], counted)
    weight = 1.0 / (counted.astype(jnp.float32) * math.sqrt(FB * segments))
    pieces = [correlate(whitened, whitened, weight)]
    moving = whitened
    for shift_step in range(1, blocks // 2 + 1):
        moving = from_behind(moving, "blk", -1)
        pieces.append(correlate(whitened, moving, weight))
    all_tiles = jnp.concatenate(pieces, axis=0)
    share_rows = (
        lax.psum_scatter(all_tiles, "seg", scatter_dimension=0, tiled=True)
        .astype(jnp.float32)
        .astype(jnp.bfloat16)
    )
    share_power = disperse(share_rows, phases)
    every_power = lax.all_gather(share_power, "seg", axis=0, tiled=True)
    mine, mine_filled = my_slots(tile_owner[0], segments)
    response = jnp.take(every_power, mine, axis=0) * mine_filled[:, None, None].astype(jnp.float32)
    return response[None, None]


CHIPS = 4
UNITS = 2 * QUAD
LAYERS = UNITS // 2
X_SWAP = [(0, 1), (1, 0), (2, 3), (3, 2)]
Y_SWAP = [(0, 2), (2, 0), (1, 3), (3, 1)]
X_EXTRA = [(1, 0), (2, 3)]
Y_EXTRA = [(2, 0), (1, 3)]
X_CORNER = [(0, 1), (2, 3)]
Y_CORNER = [(3, 1), (1, 3)]
BAND_FROM_X = [1, 0, 1, 0]
BAND_FROM_Y = [0, 0, 1, 1]
SENT_AT, KEPT_AT, BANDS_AT, MINE_AT, CORNER_AT = 0, LAYERS, 2 * LAYERS, 2 * LAYERS + 2, 2 * LAYERS + 5
INFO = CORNER_AT + 3 * UNITS
OWN_ROW, PAIR_ROW, EARLY_ROWS = 0, QUAD, 3 * QUAD


def corner_plan(chip, n):
    m = n - QUAD
    if chip == 0:
        return (4, 2 + (n >> 1), n & 1, 0) if m < 0 else (m & 1, 5, m >> 1, 1)
    if chip == 3:
        return (5, n >> 1, n & 1, 0) if m < 0 else (2 + (m & 1), 4, m >> 1, 1)
    q = n & 3
    if chip == 1:
        return (2 + (n >> 2), q >> 1, q & 1, 0)
    return (n >> 2, 2 + (q >> 1), q & 1, 1)


def pair_plan(n, part):
    return n >> 2, 2 * part + ((n >> 1) & 1), n & 1


def index_rows():
    rows = np.zeros((CHIPS, UNITS, INFO), np.int32)
    for chip in range(CHIPS):
        for me in range(UNITS):
            row = rows[chip, me]
            layer, core = me // 2, me % 2
            for r in range(LAYERS):
                unit = 2 * ((layer + r) % LAYERS)
                row[SENT_AT + r] = unit + 1 - core
                row[KEPT_AT + r] = unit + core
            bands = (BAND_FROM_X[chip], BAND_FROM_Y[chip])
            row[BANDS_AT : BANDS_AT + 2] = bands
            row[MINE_AT : MINE_AT + 3] = (me // QUAD, bands[me >> 2], corner_plan(chip, me)[3])
            for n in range(UNITS):
                row[CORNER_AT + 3 * n : CORNER_AT + 3 * n + 3] = corner_plan(chip, n)[:3]
    return rows


def source_rows():
    tiles = 3 * QUAD * QUAD
    early = np.full((CHIPS, UNITS, tiles, BANDS), -1, np.int32)
    corner = np.full((CHIPS, UNITS, tiles, BANDS), -1, np.int32)

    def put(block, step, p, q, band, chip, unit, row):
        tile = (step * QUAD + p) * QUAD + q
        for me in range(UNITS):
            r = (me // 2 - unit // 2) % LAYERS
            other = (me ^ unit) & 1
            hop = chip ^ block
            early[block, me, tile, band] = ((r * 2 + other) * 3 + hop) * EARLY_ROWS + row

    def put_corner(block, p, q, band, chip, unit, row):
        tile = (QUAD + p) * QUAD + q
        for me in range(UNITS):
            r = (me // 2 - unit // 2) % LAYERS
            other = (me ^ unit) & 1
            along_y = (chip, block) in Y_CORNER
            corner[block, me, tile, band] = ((r * 2 + other) * 2 + along_y) * 2 + row

    for chip in range(CHIPS):
        for n in range(UNITS):
            for p in range(QUAD):
                put(chip, 0, p, n % QUAD, n // QUAD, chip, n, OWN_ROW + p)
            for part in range(2):
                along_y, q, half = pair_plan(n, part)
                band = (BAND_FROM_X[chip], BAND_FROM_Y[chip])[along_y]
                for i in range(2):
                    p = 2 * half + i
                    direct = PAIR_ROW + 4 * part + i
                    if along_y:
                        put(chip, 2, p, q, band, chip, n, direct)
                        put(chip ^ 2, 2, q, p, band, chip, n, direct + 2)
                    elif chip % 2 == 0:
                        put(chip, 1, p, q, band, chip, n, direct)
                    else:
                        put(chip ^ 1, 1, q, p, band, chip, n, direct + 2)
            for i in range(2):
                m = n - QUAD
                if chip in (1, 2):
                    put_corner(3, 2 * (n >> 2) + i, n & 3, chip - 1, chip, n, i)
                elif m < 0:
                    put_corner(1, (2 if chip == 3 else 0) + i, n, 0, chip, n, i)
                else:
                    put_corner(1, 2 * (m & 1) + i, (m >> 1) + (2 if chip == 0 else 0), 1, chip, n, i)
    assert ((early >= 0) != (corner >= 0)).all()
    return np.stack([early, corner], axis=-1)


INDEX_ROWS = index_rows()
SOURCE_ROWS = source_rows()


def params():
    return pltpu.CompilerParams(vmem_limit_bytes=VMEM_LIMIT)


def whiten_kernel(counted, spectra, *refs):
    whole, to_x, to_y, extra = refs[-4:]
    windows = spectra.shape[0]
    chip = lax.axis_index("blk")
    for w in range(windows):
        values = spectra[w].astype(jnp.float32)
        scaling = lax.rsqrt(jnp.mean(values * values, axis=1, keepdims=True) + 1e-05)
        scaling = scaling * jnp.where(w < counted[0], 1.0, 0.0)
        out = (values * scaling).astype(jnp.bfloat16)
        width = out.shape[1] // BANDS
        for band in range(BANDS):
            whole[band, w] = out[:, band * width : (band + 1) * width]
    to_x[...] = whole[chip % 2]
    to_y[...] = whole[1 - chip // 2]
    extra[...] = whole[chip // 2]


def whiten(spectra, counted, half, before):
    windows, channels, width = spectra.shape
    band_width = width // BANDS
    rows = TILE // 2
    steps = channels // 2 // rows
    part_block = pl.BlockSpec((windows, rows, band_width), lambda i: (0, i, 0))
    part = jax.ShapeDtypeStruct((windows, channels // 2, band_width), jnp.bfloat16)
    return pl.pallas_call(
        whiten_kernel,
        grid=(steps,),
        in_specs=[
            pl.BlockSpec(memory_space=pltpu.SMEM),
            pl.BlockSpec((windows, rows, width), lambda i: (0, half * steps + i, 0)),
        ]
        + [pl.BlockSpec(memory_space=pl.ANY)] * len(before),
        out_specs=[
            pl.BlockSpec(
                (BANDS, windows, rows, band_width), lambda i: (0, 0, half * steps + i, 0)
            ),
            part_block,
            part_block,
            part_block,
        ],
        out_shape=[
            jax.ShapeDtypeStruct((BANDS, windows, channels, band_width), jnp.bfloat16),
            part,
            part,
            part,
        ],
        input_output_aliases={2: 0} if before else {},
        compiler_params=params(),
        cost_estimate=pl.CostEstimate(
            flops=4 * spectra.size, bytes_accessed=7 * 2**20, transcendentals=0
        ),
    )(counted, spectra, *before)


def product(left, right, weight):
    total = None
    for rows, columns in zip(left, right):
        width = columns.shape[1] // 2
        turned = jnp.concatenate([-columns[:, width:], columns[:, :width]], axis=1)
        both = jnp.concatenate([columns, turned], axis=0)
        part = lax.dot_general(
            rows, both, (((1,), (1,)), ((), ())), preferred_element_type=jnp.float32
        )
        total = part if total is None else total + part
    return (total * weight).astype(jnp.bfloat16)


def own_kernel(info, weight, left, right, out):
    windows = left.shape[1]
    out[0] = product(
        [left[0, w] for w in range(windows)], [right[0, w] for w in range(windows)], weight[0]
    )


def pair_kernel(base, info, weight, left, from_x, from_y, out, held):
    windows = left.shape[1]
    is_x = info[base + pl.program_id(0)] < QUAD

    @pl.when(is_x)
    def _():
        held[...] = from_x[...]

    @pl.when(jnp.logical_not(is_x))
    def _():
        held[...] = from_y[...]

    out[0] = product(
        [left[0, w] for w in range(windows)], [held[w] for w in range(windows)], weight[0]
    )


def corner_kernel(base, info, weight, *refs):
    arrays, (out, left, right) = refs[:-3], refs[-3:]
    windows = left.shape[0]
    at = CORNER_AT + 3 * info[base + pl.program_id(0)]
    for number, ref in enumerate(arrays):

        @pl.when(info[at] == number)
        def _():
            left[...] = ref[...]

        @pl.when(info[at + 1] == number)
        def _():
            right[...] = ref[:, pl.ds(pl.multiple_of(info[at + 2] * TILE, TILE), TILE), :]

    out[0] = product(
        [left[w] for w in range(windows)], [right[w] for w in range(windows)], weight[0]
    )


def unit_call(kernel, info, weight, arrays, specs, rows, scratch):
    windows, width = arrays[0].shape[-3], arrays[0].shape[-1]
    return pl.pallas_call(
        kernel,
        grid_spec=pltpu.PrefetchScalarGridSpec(
            num_scalar_prefetch=2,
            grid=(LAYERS,),
            in_specs=specs,
            out_specs=pl.BlockSpec((1, rows, 2 * TILE), lambda i, s, t: (i, 0, 0)),
            scratch_shapes=scratch,
        ),
        out_shape=jax.ShapeDtypeStruct((LAYERS, rows, 2 * TILE), jnp.bfloat16),
        compiler_params=params(),
        cost_estimate=pl.CostEstimate(
            flops=2 * LAYERS * windows * rows * width * 2 * TILE,
            bytes_accessed=6 * 2**20,
            transcendentals=0,
        ),
    )(info, weight, *arrays)


def own_units(base, info, weight, whole):
    bands, windows, channels, width = whole.shape

    def band(i, s):
        return s[base + i] // QUAD

    specs = [
        pl.BlockSpec((1, windows, channels, width), lambda i, s, t: (band(i, s), 0, 0, 0)),
        pl.BlockSpec(
            (1, windows, TILE, width), lambda i, s, t: (band(i, s), 0, s[base + i] % QUAD, 0)
        ),
    ]
    return unit_call(own_kernel, info, weight, (whole, whole), specs, channels, [])


def pair_units(base, info, weight, whole, from_x, from_y):
    bands, windows, channels, width = whole.shape
    half = channels // 2
    tile = (windows, TILE, width)

    def left(i, s, t):
        unit = s[base + i]
        return (jnp.where(unit < QUAD, s[BANDS_AT], s[BANDS_AT + 1]), 0, unit % 2, 0)

    def right(i, s, t):
        return (0, s[base + i] // 2 % 2, 0)

    specs = [
        pl.BlockSpec((1, windows, half, width), left),
        pl.BlockSpec(tile, right),
        pl.BlockSpec(tile, right),
    ]
    return unit_call(
        functools.partial(pair_kernel, base),
        info,
        weight,
        (whole, from_x, from_y),
        specs,
        half,
        [pltpu.VMEM(tile, jnp.bfloat16)],
    )


def corner_units(base, info, weight, *arrays):
    windows, half, width = arrays[0].shape
    specs = [pl.BlockSpec(a.shape, lambda i, s, t: (0, 0, 0)) for a in arrays]
    scratch = [
        pltpu.VMEM((windows, half, width), jnp.bfloat16),
        pltpu.VMEM((windows, TILE, width), jnp.bfloat16),
    ]
    return unit_call(
        functools.partial(corner_kernel, base), info, weight, arrays, specs, half, scratch
    )


def pair_sum_kernel(kept, got, *outs):
    for r, out in enumerate(outs):
        out[...] = (kept[r].astype(jnp.float32) + got[r].astype(jnp.float32)).astype(jnp.bfloat16)


def pair_sum(kept, got):
    shape = jax.ShapeDtypeStruct(kept.shape[1:], jnp.bfloat16)
    return pl.pallas_call(
        pair_sum_kernel,
        out_shape=[shape] * kept.shape[0],
        compiler_params=params(),
        cost_estimate=pl.CostEstimate(
            flops=kept.size, bytes_accessed=6 * kept.size, transcendentals=0
        ),
    )(kept, got)


def layer_sum(parts):
    total = parts[0][...].astype(jnp.float32)
    for part in parts[1:]:
        total = total + part[...].astype(jnp.float32)
    return total.astype(jnp.bfloat16)


def tile_powers(rows, table):
    velocities = table.shape[1] // 2
    field = lax.dot_general(
        rows, table, (((1,), (0,)), ((), ())), preferred_element_type=jnp.float32
    )
    squared = field * field
    energy = squared[:, :velocities] + squared[:, velocities:]
    return [
        jnp.sum(energy[t : t + TILE], axis=0, keepdims=True) * (1.0 / TILE)
        for t in range(0, rows.shape[0], TILE)
    ]


def transposed(stacked):
    rounded = stacked.astype(jnp.float32)
    turned = []
    for t in range(0, stacked.shape[0], TILE):
        tile = rounded[t : t + TILE]
        turned.append(jnp.concatenate([tile[:, :TILE].T, -tile[:, TILE:].T], axis=1))
    return jnp.concatenate(turned, axis=0).astype(jnp.bfloat16)


def early_power_kernel(info, matrix, *refs):
    out = refs[-1]
    found = tile_powers(layer_sum(refs[:LAYERS]), matrix[info[MINE_AT]])
    table = matrix[info[MINE_AT + 1]]
    for first in (LAYERS, 2 * LAYERS):
        stacked = layer_sum(refs[first : first + LAYERS])
        found += tile_powers(stacked, table) + tile_powers(transposed(stacked), table)
    for t, row in enumerate(found):
        out[t : t + 1, :] = row


def corner_power_kernel(info, matrix, *refs):
    out = refs[-1]
    for t, row in enumerate(tile_powers(layer_sum(refs[:-1]), matrix[info[MINE_AT + 2]])):
        out[t : t + 1, :] = row


def powers_of(kernel, rows, info, matrix, parts):
    velocities = matrix.shape[2] // 2
    vmem = pl.BlockSpec(memory_space=pltpu.VMEM)
    return pl.pallas_call(
        kernel,
        in_specs=[pl.BlockSpec(memory_space=pltpu.SMEM)] + [vmem] * (1 + len(parts)),
        out_shape=jax.ShapeDtypeStruct((rows, velocities), jnp.float32),
        compiler_params=params(),
        cost_estimate=pl.CostEstimate(
            flops=8 * TILE * TILE * rows * velocities,
            bytes_accessed=2 * sum(p.size for p in parts),
            transcendentals=0,
        ),
    )(info, matrix, *parts)


def across(array, hops):
    return lax.ppermute(array, "blk", hops)


def across_cores(array, hops):
    pairs = [(UNITS * a + s, UNITS * b + (s ^ 1)) for a, b in hops for s in range(UNITS)]
    return lax.ppermute(array, ("blk", "seg"), pairs)


def other_core(array):
    return lax.ppermute(array, "seg", [(i, i ^ 1) for i in range(UNITS)])


def layers_on(array, r):
    return lax.ppermute(array, "seg", [(i, (i + 2 * r) % UNITS) for i in range(UNITS)])


def from_layers(array):
    return jnp.stack([array] + [layers_on(array, r) for r in range(1, LAYERS)])


def grid_body(spectra, window_count, tile_owner, phases):
    chip = lax.axis_index("blk")
    me = lax.axis_index("seg")
    first = whiten(spectra[0], window_count, 0, ())
    x0, y0 = across(first[1], X_SWAP), across(first[2], Y_SWAP)
    whole, to_x, to_y, extra_y = whiten(spectra[0], window_count, 1, (first[0],))
    x1, y1 = across(to_x, X_SWAP), across(to_y, Y_SWAP)
    extra_x = across(first[3], X_EXTRA)
    extra_y = across(extra_y, Y_EXTRA)

    info = jnp.asarray(INDEX_ROWS)[chip, me]
    weight = (1.0 / (window_count.astype(jnp.float32) * math.sqrt(FB * UNITS)))
    matrix = phase_matrix(phases)
    mine, mine_filled = my_slots(tile_owner[0], UNITS)
    sources = jnp.asarray(SOURCE_ROWS)[chip, me][mine]

    def reduce(make, weight):
        got = other_core(make(SENT_AT, info, weight))
        sums = pair_sum(make(KEPT_AT, info, weight), got)
        return [sums[0]] + [layers_on(sums[r], r) for r in range(1, LAYERS)], sums

    own, done = reduce(lambda *a: own_units(*a, whole), weight)
    weight, *_ = lax.optimization_barrier((weight, *done))
    pair0, done = reduce(lambda *a: pair_units(*a, whole, x0, y0), weight)
    weight, *_ = lax.optimization_barrier((weight, *done))
    pair1, done = reduce(lambda *a: pair_units(*a, whole, x1, y1), weight)
    early = powers_of(early_power_kernel, EARLY_ROWS, info, matrix, own + pair0 + pair1)
    weight, *_ = lax.optimization_barrier((weight, early, *done))
    corner, _ = reduce(
        lambda *a: corner_units(*a, x0, x1, y0, y1, extra_x, extra_y), weight
    )
    near = jnp.stack([early, across(early, X_SWAP), across(early, Y_SWAP)])
    every = from_layers(jnp.stack([near, other_core(near)]))
    last = powers_of(corner_power_kernel, 2, info, matrix, corner)
    every_last = from_layers(
        jnp.stack(
            [
                across(last, X_CORNER),
                across(last, Y_CORNER),
                across_cores(last, X_CORNER),
                across_cores(last, Y_CORNER),
            ]
        )
    )
    velocities = early.shape[-1]
    response = jnp.take(every.reshape(-1, velocities), jnp.maximum(sources[..., 0], 0), axis=0)
    response_last = jnp.take(
        every_last.reshape(-1, velocities), jnp.maximum(sources[..., 1], 0), axis=0
    )
    response = jnp.where(sources[..., 1:2] >= 0, response_last, response)
    response = response * mine_filled[:, None, None].astype(jnp.float32)
    return response[None, None]


def solution(mesh):
    placed = (P("seg", None, "blk", None), P("seg"), P("blk", None), P())
    fits = mesh.shape["blk"] == CHIPS and mesh.shape["seg"] == UNITS
    return jax.shard_map(
        grid_body if fits else ring_body,
        mesh=mesh,
        in_specs=placed,
        out_specs=P("blk", "seg", None, None, None),
        check_vma=False,
    )
```

```python
import functools
import math

import jax
import jax.numpy as jnp
import numpy as np
from jax import lax
from jax.experimental import pallas as pl
from jax.experimental.pallas import tpu as pltpu
from jax.sharding import PartitionSpec as P

TILE = 128
BANDS = 2
CAP = 8
FB = 512
QUAD = 4
VMEM_LIMIT = 20 * 1024 * 1024
WHITEN_LIMIT = 44 * 1024 * 1024


def from_behind(array, axis, by):
    devices = lax.axis_size(axis)
    return lax.ppermute(array, axis, [(i, (i + by) % devices) for i in range(devices)])


def prepare(segment_data, counted):
    windows = segment_data.shape[0]
    channels = segment_data.shape[1]
    spectrum = segment_data.astype(jnp.float32).reshape(windows, channels, BANDS, 2, FB)
    scaling = lax.rsqrt(jnp.mean(spectrum * spectrum, axis=(2, 3, 4)) + 1e-05)
    live_mask = (jnp.arange(windows, dtype=jnp.int32) < counted).astype(jnp.float32)
    return (
        spectrum * scaling[:, :, None, None, None] * live_mask[:, None, None, None, None]
    ).astype(jnp.bfloat16)


def correlate(resident, visiting, weight):
    windows = resident.shape[0]
    flipped = jnp.stack([-visiting[:, :, :, 1], visiting[:, :, :, 0]], axis=3)
    both_parts = jnp.stack([visiting, flipped], axis=1)
    left_side = resident.reshape(windows, QUAD, TILE, BANDS, 2 * FB)
    right_side = both_parts.reshape(windows, 2, QUAD, TILE, BANDS, 2 * FB)
    product = jnp.einsum(
        "wqibk,wpsjbk->qsbipj", left_side, right_side, preferred_element_type=jnp.float32
    )
    return (product * weight).astype(jnp.bfloat16).reshape(QUAD * QUAD, BANDS, TILE, 2 * TILE)


def phase_matrix(phases):
    norm_factor = 1.0 / math.sqrt(TILE)
    cosine = (jnp.cos(phases) * norm_factor).astype(jnp.bfloat16)
    sine_part = (jnp.sin(phases) * norm_factor).astype(jnp.bfloat16)
    upper = jnp.concatenate([cosine, sine_part], axis=2)
    lower = jnp.concatenate([-sine_part, cosine], axis=2)
    return jnp.concatenate([upper, lower], axis=1)


def disperse(stacked, phases):
    velocity_count = phases.shape[2]
    matrix = phase_matrix(phases)
    field = jnp.einsum("nbij,bjv->nbiv", stacked, matrix, preferred_element_type=jnp.float32)
    squared = field * field
    energy = squared[..., :velocity_count] + squared[..., velocity_count:]
    return jnp.mean(energy, axis=2)


def slot_table(owner_row, segments):
    count_tiles = owner_row.shape[0]
    order_ids = jnp.arange(count_tiles, dtype=jnp.int32)
    same_owner = owner_row[:, None] == owner_row[None, :]
    earlier = order_ids[None, :] < order_ids[:, None]
    rank_of = jnp.sum(jnp.where(same_owner & earlier, 1, 0), axis=1).astype(jnp.int32)
    slot_ids = owner_row * CAP + rank_of
    grid_ids = jnp.arange(segments * CAP, dtype=jnp.int32)
    matches = grid_ids[:, None] == slot_ids[None, :]
    tile_of_slot = jnp.sum(jnp.where(matches, order_ids[None, :], 0), axis=1)
    filled = jnp.any(matches, axis=1)
    return (tile_of_slot, filled)


def my_slots(owner_row, segments):
    tile_of_slot, filled = slot_table(owner_row, segments)
    my_start = lax.axis_index("seg") * CAP
    mine = lax.dynamic_slice_in_dim(tile_of_slot, my_start, CAP, 0)
    mine_filled = lax.dynamic_slice_in_dim(filled, my_start, CAP, 0)
    return mine, mine_filled


def ring_body(spectra, window_count, tile_owner, phases):
    blocks = lax.axis_size("blk")
    segments = lax.axis_size("seg")
    counted = window_count[0]
    whitened = prepare(spectra[0], counted)
    weight = 1.0 / (counted.astype(jnp.float32) * math.sqrt(FB * segments))
    pieces = [correlate(whitened, whitened, weight)]
    moving = whitened
    for shift_step in range(1, blocks // 2 + 1):
        moving = from_behind(moving, "blk", -1)
        pieces.append(correlate(whitened, moving, weight))
    all_tiles = jnp.concatenate(pieces, axis=0)
    share_rows = (
        lax.psum_scatter(all_tiles, "seg", scatter_dimension=0, tiled=True)
        .astype(jnp.float32)
        .astype(jnp.bfloat16)
    )
    share_power = disperse(share_rows, phases)
    every_power = lax.all_gather(share_power, "seg", axis=0, tiled=True)
    mine, mine_filled = my_slots(tile_owner[0], segments)
    response = jnp.take(every_power, mine, axis=0) * mine_filled[:, None, None].astype(jnp.float32)
    return response[None, None]


CHIPS = 4
UNITS = 2 * QUAD
LAYERS = UNITS // 2
X_SWAP = [(0, 1), (1, 0), (2, 3), (3, 2)]
Y_SWAP = [(0, 2), (2, 0), (1, 3), (3, 1)]
X_EXTRA = [(1, 0), (2, 3)]
Y_EXTRA = [(2, 0), (1, 3)]
X_CORNER = [(0, 1), (2, 3)]
Y_CORNER = [(3, 1), (1, 3)]
BAND_FROM_X = [1, 0, 1, 0]
BAND_FROM_Y = [0, 0, 1, 1]
SENT_AT, KEPT_AT, BANDS_AT, MINE_AT, CORNER_AT = 0, LAYERS, 2 * LAYERS, 2 * LAYERS + 2, 2 * LAYERS + 5
INFO = CORNER_AT + 4 * UNITS
OWN_ROW, PAIR_ROW, EARLY_ROWS = 0, QUAD, 3 * QUAD


def corner_plan(chip, n):
    m = n - QUAD
    if chip == 0:
        return (2, 0, 1, n, 0) if m < 0 else (0, m & 1, 3, m >> 1, 1)
    if chip == 3:
        return (3, 0, 0, n, 0) if m < 0 else (1, m & 1, 2, m >> 1, 1)
    return (1, n >> 2, 0, n & 3, 0) if chip == 1 else (0, n >> 2, 1, n & 3, 1)


def index_rows():
    rows = np.zeros((CHIPS, UNITS, INFO), np.int32)
    for chip in range(CHIPS):
        for me in range(UNITS):
            row = rows[chip, me]
            layer, core = me // 2, me % 2
            for r in range(LAYERS):
                unit = 2 * ((layer + r) % LAYERS)
                row[SENT_AT + r] = unit + 1 - core
                row[KEPT_AT + r] = unit + core
            bands = (BAND_FROM_X[chip], BAND_FROM_Y[chip])
            row[BANDS_AT : BANDS_AT + 2] = bands
            row[MINE_AT : MINE_AT + 3] = (me // QUAD, bands[me >> 2], corner_plan(chip, me)[4])
            for n in range(UNITS):
                row[CORNER_AT + 4 * n : CORNER_AT + 4 * n + 4] = corner_plan(chip, n)[:4]
    return rows


def source_rows():
    tiles = 3 * QUAD * QUAD
    early = np.full((CHIPS, UNITS, tiles, BANDS), -1, np.int32)
    corner = np.full((CHIPS, UNITS, tiles, BANDS), -1, np.int32)

    def put(block, step, p, q, band, chip, unit, row):
        tile = (step * QUAD + p) * QUAD + q
        for me in range(UNITS):
            r = (me // 2 - unit // 2) % LAYERS
            other = (me ^ unit) & 1
            hop = chip ^ block
            early[block, me, tile, band] = ((r * 2 + other) * 3 + hop) * EARLY_ROWS + row

    def put_corner(block, p, q, band, chip, unit, row):
        tile = (QUAD + p) * QUAD + q
        for me in range(UNITS):
            r = (me // 2 - unit // 2) % LAYERS
            other = (me ^ unit) & 1
            along_y = (chip, block) in Y_CORNER
            corner[block, me, tile, band] = ((r * 2 + other) * 2 + along_y) * 2 + row

    for chip in range(CHIPS):
        for n in range(UNITS):
            for p in range(QUAD):
                put(chip, 0, p, n % QUAD, n // QUAD, chip, n, OWN_ROW + p)
            q = n % QUAD
            band = (BAND_FROM_X[chip], BAND_FROM_Y[chip])[n // QUAD]
            for p in range(QUAD):
                direct, turned = PAIR_ROW + p, PAIR_ROW + QUAD + p
                if n >= QUAD:
                    put(chip, 2, p, q, band, chip, n, direct)
                    put(chip ^ 2, 2, q, p, band, chip, n, turned)
                elif chip % 2 == 0:
                    put(chip, 1, p, q, band, chip, n, direct)
                else:
                    put(chip ^ 1, 1, q, p, band, chip, n, turned)
            for i in range(2):
                m = n - QUAD
                if chip in (1, 2):
                    put_corner(3, 2 * (n >> 2) + i, n & 3, chip - 1, chip, n, i)
                elif m < 0:
                    put_corner(1, (2 if chip == 3 else 0) + i, n, 0, chip, n, i)
                else:
                    put_corner(1, 2 * (m & 1) + i, (m >> 1) + (2 if chip == 0 else 0), 1, chip, n, i)
    assert ((early >= 0) != (corner >= 0)).all()
    return np.stack([early, corner], axis=-1)


INDEX_ROWS = index_rows()
SOURCE_ROWS = source_rows()


SMALL = pl.CostEstimate(flops=1000, bytes_accessed=1000, transcendentals=0)


def params(limit=VMEM_LIMIT):
    return pltpu.CompilerParams(vmem_limit_bytes=limit)


def whiten_kernel(counted, spectra, whole, to_x, to_y, extra_x, extra_y):
    step = pl.program_id(0)
    half = pl.num_programs(0) // 2
    windows = spectra.shape[0]
    chip = lax.axis_index("blk")
    for w in range(windows):
        values = spectra[w].astype(jnp.float32)
        scaling = lax.rsqrt(jnp.mean(values * values, axis=1, keepdims=True) + 1e-05)
        scaling = scaling * jnp.where(w < counted[0], 1.0, 0.0)
        out = (values * scaling).astype(jnp.bfloat16)
        width = out.shape[1] // BANDS
        for band in range(BANDS):
            whole[band, w] = out[:, band * width : (band + 1) * width]
    to_x[...] = whole[chip % 2]
    to_y[...] = whole[1 - chip // 2]

    @pl.when(step < half)
    def _():
        extra_x[...] = whole[chip // 2]

    @pl.when(step >= half)
    def _():
        extra_y[...] = whole[chip // 2]


def whiten(spectra, counted):
    windows, channels, width = spectra.shape
    band_width = width // BANDS
    steps = channels // TILE
    half = steps // 2
    block = (windows, TILE, band_width)
    full = jax.ShapeDtypeStruct((windows, channels, band_width), jnp.bfloat16)
    part = jax.ShapeDtypeStruct((windows, channels // 2, band_width), jnp.bfloat16)
    return pl.pallas_call(
        whiten_kernel,
        grid=(steps,),
        in_specs=[
            pl.BlockSpec(memory_space=pltpu.SMEM),
            pl.BlockSpec((windows, TILE, width), lambda i: (0, i, 0)),
        ],
        out_specs=[
            pl.BlockSpec((BANDS,) + block, lambda i: (0, 0, i, 0)),
            pl.BlockSpec(block, lambda i: (0, i, 0)),
            pl.BlockSpec(block, lambda i: (0, i, 0)),
            pl.BlockSpec(block, lambda i: (0, jnp.minimum(i, half - 1), 0)),
            pl.BlockSpec(block, lambda i: (0, jnp.maximum(i - half, 0), 0)),
        ],
        out_shape=[
            jax.ShapeDtypeStruct((BANDS, windows, channels, band_width), jnp.bfloat16),
            full,
            full,
            part,
            part,
        ],
        compiler_params=params(WHITEN_LIMIT),
        cost_estimate=SMALL,
    )(counted, spectra)


def product(left, right, weight):
    total = None
    for rows, columns in zip(left, right):
        width = columns.shape[1] // 2
        turned = jnp.concatenate([-columns[:, width:], columns[:, :width]], axis=1)
        both = jnp.concatenate([columns, turned], axis=0)
        part = lax.dot_general(
            rows, both, (((1,), (1,)), ((), ())), preferred_element_type=jnp.float32
        )
        total = part if total is None else total + part
    return (total * weight).astype(jnp.bfloat16)


def own_kernel(info, weight, left, right, out):
    windows = left.shape[1]
    out[0] = product(
        [left[0, w] for w in range(windows)], [right[0, w] for w in range(windows)], weight[0]
    )


def pair_kernel(base, info, weight, left, from_x, from_y, out, held):
    windows = left.shape[1]
    is_x = info[base + pl.program_id(0)] < QUAD

    @pl.when(is_x)
    def _():
        held[...] = from_x[...]

    @pl.when(jnp.logical_not(is_x))
    def _():
        held[...] = from_y[...]

    out[0] = product(
        [left[0, w] for w in range(windows)], [held[w] for w in range(windows)], weight[0]
    )


def corner_kernel(base, info, weight, *refs):
    arrays, (out, left, right) = refs[:-3], refs[-3:]
    windows = left.shape[0]
    at = CORNER_AT + 4 * info[base + pl.program_id(0)]
    rows = left.shape[1]
    for number, ref in enumerate(arrays):

        @pl.when(info[at] == number)
        def _():
            left[...] = ref[:, pl.ds(pl.multiple_of(info[at + 1] * rows, rows), rows), :]

        @pl.when(info[at + 2] == number)
        def _():
            right[...] = ref[:, pl.ds(pl.multiple_of(info[at + 3] * TILE, TILE), TILE), :]

    out[0] = product(
        [left[w] for w in range(windows)], [right[w] for w in range(windows)], weight[0]
    )


def unit_call(kernel, info, weight, arrays, specs, rows, scratch):
    windows, width = arrays[0].shape[-3], arrays[0].shape[-1]
    return pl.pallas_call(
        kernel,
        grid_spec=pltpu.PrefetchScalarGridSpec(
            num_scalar_prefetch=2,
            grid=(LAYERS,),
            in_specs=specs,
            out_specs=pl.BlockSpec((1, rows, 2 * TILE), lambda i, s, t: (i, 0, 0)),
            scratch_shapes=scratch,
        ),
        out_shape=jax.ShapeDtypeStruct((LAYERS, rows, 2 * TILE), jnp.bfloat16),
        compiler_params=params(),
        cost_estimate=SMALL,
    )(info, weight, *arrays)


def own_units(base, info, weight, whole):
    bands, windows, channels, width = whole.shape

    def band(i, s):
        return s[base + i] // QUAD

    specs = [
        pl.BlockSpec((1, windows, channels, width), lambda i, s, t: (band(i, s), 0, 0, 0)),
        pl.BlockSpec(
            (1, windows, TILE, width), lambda i, s, t: (band(i, s), 0, s[base + i] % QUAD, 0)
        ),
    ]
    return unit_call(own_kernel, info, weight, (whole, whole), specs, channels, [])


def pair_units(base, info, weight, whole, from_x, from_y):
    bands, windows, channels, width = whole.shape
    tile = (windows, TILE, width)

    def left(i, s, t):
        return (jnp.where(s[base + i] < QUAD, s[BANDS_AT], s[BANDS_AT + 1]), 0, 0, 0)

    def right(i, s, t):
        return (0, s[base + i] % QUAD, 0)

    specs = [
        pl.BlockSpec((1, windows, channels, width), left),
        pl.BlockSpec(tile, right),
        pl.BlockSpec(tile, right),
    ]
    return unit_call(
        functools.partial(pair_kernel, base),
        info,
        weight,
        (whole, from_x, from_y),
        specs,
        channels,
        [pltpu.VMEM(tile, jnp.bfloat16)],
    )


def corner_units(base, info, weight, *arrays):
    windows, channels, width = arrays[0].shape
    half = channels // 2
    specs = [pl.BlockSpec(a.shape, lambda i, s, t: (0, 0, 0)) for a in arrays]
    scratch = [
        pltpu.VMEM((windows, half, width), jnp.bfloat16),
        pltpu.VMEM((windows, TILE, width), jnp.bfloat16),
    ]
    return unit_call(
        functools.partial(corner_kernel, base), info, weight, arrays, specs, half, scratch
    )


def pair_sum_kernel(kept, got, *outs):
    for r, out in enumerate(outs):
        out[...] = (kept[r].astype(jnp.float32) + got[r].astype(jnp.float32)).astype(jnp.bfloat16)


def pair_sum(kept, got):
    shape = jax.ShapeDtypeStruct(kept.shape[1:], jnp.bfloat16)
    return pl.pallas_call(
        pair_sum_kernel,
        out_shape=[shape] * kept.shape[0],
        compiler_params=params(),
        cost_estimate=SMALL,
    )(kept, got)


def layer_sum(parts):
    total = parts[0][...].astype(jnp.float32)
    for part in parts[1:]:
        total = total + part[...].astype(jnp.float32)
    return total.astype(jnp.bfloat16)


def tile_powers(rows, table):
    velocities = table.shape[1] // 2
    field = lax.dot_general(
        rows, table, (((1,), (0,)), ((), ())), preferred_element_type=jnp.float32
    )
    squared = field * field
    energy = squared[:, :velocities] + squared[:, velocities:]
    return [
        jnp.sum(energy[t : t + TILE], axis=0, keepdims=True) * (1.0 / TILE)
        for t in range(0, rows.shape[0], TILE)
    ]


def transposed(stacked):
    rounded = stacked.astype(jnp.float32)
    turned = []
    for t in range(0, stacked.shape[0], TILE):
        tile = rounded[t : t + TILE]
        turned.append(jnp.concatenate([tile[:, :TILE].T, -tile[:, TILE:].T], axis=1))
    return jnp.concatenate(turned, axis=0).astype(jnp.bfloat16)


def early_power_kernel(info, matrix, *refs):
    out = refs[-1]
    found = tile_powers(layer_sum(refs[:LAYERS]), matrix[info[MINE_AT]])
    table = matrix[info[MINE_AT + 1]]
    stacked = layer_sum(refs[LAYERS : 2 * LAYERS])
    found += tile_powers(stacked, table) + tile_powers(transposed(stacked), table)
    for t, row in enumerate(found):
        out[t : t + 1, :] = row


def corner_power_kernel(info, matrix, *refs):
    out = refs[-1]
    for t, row in enumerate(tile_powers(layer_sum(refs[:-1]), matrix[info[MINE_AT + 2]])):
        out[t : t + 1, :] = row


def powers_of(kernel, rows, info, matrix, parts):
    velocities = matrix.shape[2] // 2
    vmem = pl.BlockSpec(memory_space=pltpu.VMEM)
    return pl.pallas_call(
        kernel,
        in_specs=[pl.BlockSpec(memory_space=pltpu.SMEM)] + [vmem] * (1 + len(parts)),
        out_shape=jax.ShapeDtypeStruct((rows, velocities), jnp.float32),
        compiler_params=params(),
        cost_estimate=SMALL,
    )(info, matrix, *parts)


def across(array, hops):
    return lax.ppermute(array, "blk", hops)


def across_cores(array, hops):
    pairs = [(UNITS * a + s, UNITS * b + (s ^ 1)) for a, b in hops for s in range(UNITS)]
    return lax.ppermute(array, ("blk", "seg"), pairs)


def other_core(array):
    return lax.ppermute(array, "seg", [(i, i ^ 1) for i in range(UNITS)])


def layers_on(array, r):
    return lax.ppermute(array, "seg", [(i, (i + 2 * r) % UNITS) for i in range(UNITS)])


def from_layers(array):
    return jnp.stack([array] + [layers_on(array, r) for r in range(1, LAYERS)])


def grid_body(spectra, window_count, tile_owner, phases):
    chip = lax.axis_index("blk")
    me = lax.axis_index("seg")
    whole, to_x, to_y, extra_x, extra_y = whiten(spectra[0], window_count)
    from_x, from_y = across(to_x, X_SWAP), across(to_y, Y_SWAP)
    extra_x, extra_y = across(extra_x, X_EXTRA), across(extra_y, Y_EXTRA)
    info = jnp.asarray(INDEX_ROWS)[chip, me]
    weight = (1.0 / (window_count.astype(jnp.float32) * math.sqrt(FB * UNITS)))
    matrix = phase_matrix(phases)
    mine, mine_filled = my_slots(tile_owner[0], UNITS)
    sources = jnp.asarray(SOURCE_ROWS)[chip, me][mine]

    def reduce(make, weight):
        got = other_core(make(SENT_AT, info, weight))
        sums = pair_sum(make(KEPT_AT, info, weight), got)
        return [sums[0]] + [layers_on(sums[r], r) for r in range(1, LAYERS)], sums

    own, _ = reduce(lambda *a: own_units(*a, whole), weight)
    weight, *_ = lax.optimization_barrier((weight, *own))
    pair, _ = reduce(lambda *a: pair_units(*a, whole, from_x, from_y), weight)
    weight, *_ = lax.optimization_barrier((weight, *pair))
    corner, done = reduce(lambda *a: corner_units(*a, from_x, from_y, extra_x, extra_y), weight)
    info_later, *_ = lax.optimization_barrier((info, *done))
    early = powers_of(early_power_kernel, EARLY_ROWS, info_later, matrix, own + pair)
    near = jnp.stack([early, across(early, X_SWAP), across(early, Y_SWAP)])
    every = from_layers(jnp.stack([near, other_core(near)]))
    last = powers_of(corner_power_kernel, 2, info, matrix, corner)
    every_last = from_layers(
        jnp.stack(
            [
                across(last, X_CORNER),
                across(last, Y_CORNER),
                across_cores(last, X_CORNER),
                across_cores(last, Y_CORNER),
            ]
        )
    )
    velocities = early.shape[-1]
    response = jnp.take(every.reshape(-1, velocities), jnp.maximum(sources[..., 0], 0), axis=0)
    response_last = jnp.take(
        every_last.reshape(-1, velocities), jnp.maximum(sources[..., 1], 0), axis=0
    )
    response = jnp.where(sources[..., 1:2] >= 0, response_last, response)
    response = response * mine_filled[:, None, None].astype(jnp.float32)
    return response[None, None]


def solution(mesh):
    placed = (P("seg", None, "blk", None), P("seg"), P("blk", None), P())
    fits = mesh.shape["blk"] == CHIPS and mesh.shape["seg"] == UNITS
    return jax.shard_map(
        grid_body if fits else ring_body,
        mesh=mesh,
        in_specs=placed,
        out_specs=P("blk", "seg", None, None, None),
        check_vma=False,
    )
```

```python
import functools
import math

import jax
import jax.numpy as jnp
import numpy as np
from jax import lax
from jax.experimental import pallas as pl
from jax.experimental.pallas import tpu as pltpu
from jax.sharding import PartitionSpec as P

TILE = 128
BANDS = 2
CAP = 8
FB = 512
QUAD = 4
VMEM_LIMIT = 16 * 1024 * 1024


def from_behind(array, axis, by):
    devices = lax.axis_size(axis)
    return lax.ppermute(array, axis, [(i, (i + by) % devices) for i in range(devices)])


def prepare(segment_data, counted):
    windows = segment_data.shape[0]
    channels = segment_data.shape[1]
    spectrum = segment_data.astype(jnp.float32).reshape(windows, channels, BANDS, 2, FB)
    scaling = lax.rsqrt(jnp.mean(spectrum * spectrum, axis=(2, 3, 4)) + 1e-05)
    live_mask = (jnp.arange(windows, dtype=jnp.int32) < counted).astype(jnp.float32)
    return (
        spectrum * scaling[:, :, None, None, None] * live_mask[:, None, None, None, None]
    ).astype(jnp.bfloat16)


def correlate(resident, visiting, weight):
    windows = resident.shape[0]
    flipped = jnp.stack([-visiting[:, :, :, 1], visiting[:, :, :, 0]], axis=3)
    both_parts = jnp.stack([visiting, flipped], axis=1)
    left_side = resident.reshape(windows, QUAD, TILE, BANDS, 2 * FB)
    right_side = both_parts.reshape(windows, 2, QUAD, TILE, BANDS, 2 * FB)
    product = jnp.einsum(
        "wqibk,wpsjbk->qsbipj", left_side, right_side, preferred_element_type=jnp.float32
    )
    return (product * weight).astype(jnp.bfloat16).reshape(QUAD * QUAD, BANDS, TILE, 2 * TILE)


def phase_matrix(phases):
    norm_factor = 1.0 / math.sqrt(TILE)
    cosine = (jnp.cos(phases) * norm_factor).astype(jnp.bfloat16)
    sine_part = (jnp.sin(phases) * norm_factor).astype(jnp.bfloat16)
    upper = jnp.concatenate([cosine, sine_part], axis=2)
    lower = jnp.concatenate([-sine_part, cosine], axis=2)
    return jnp.concatenate([upper, lower], axis=1)


def disperse(stacked, phases):
    velocity_count = phases.shape[2]
    matrix = phase_matrix(phases)
    field = jnp.einsum("nbij,bjv->nbiv", stacked, matrix, preferred_element_type=jnp.float32)
    squared = field * field
    energy = squared[..., :velocity_count] + squared[..., velocity_count:]
    return jnp.mean(energy, axis=2)


def slot_table(owner_row, segments):
    count_tiles = owner_row.shape[0]
    order_ids = jnp.arange(count_tiles, dtype=jnp.int32)
    same_owner = owner_row[:, None] == owner_row[None, :]
    earlier = order_ids[None, :] < order_ids[:, None]
    rank_of = jnp.sum(jnp.where(same_owner & earlier, 1, 0), axis=1).astype(jnp.int32)
    slot_ids = owner_row * CAP + rank_of
    grid_ids = jnp.arange(segments * CAP, dtype=jnp.int32)
    matches = grid_ids[:, None] == slot_ids[None, :]
    tile_of_slot = jnp.sum(jnp.where(matches, order_ids[None, :], 0), axis=1)
    filled = jnp.any(matches, axis=1)
    return (tile_of_slot, filled)


def my_slots(owner_row, segments):
    tile_of_slot, filled = slot_table(owner_row, segments)
    my_start = lax.axis_index("seg") * CAP
    mine = lax.dynamic_slice_in_dim(tile_of_slot, my_start, CAP, 0)
    mine_filled = lax.dynamic_slice_in_dim(filled, my_start, CAP, 0)
    return mine, mine_filled


def ring_body(spectra, window_count, tile_owner, phases):
    blocks = lax.axis_size("blk")
    segments = lax.axis_size("seg")
    counted = window_count[0]
    whitened = prepare(spectra[0], counted)
    weight = 1.0 / (counted.astype(jnp.float32) * math.sqrt(FB * segments))
    pieces = [correlate(whitened, whitened, weight)]
    moving = whitened
    for shift_step in range(1, blocks // 2 + 1):
        moving = from_behind(moving, "blk", -1)
        pieces.append(correlate(whitened, moving, weight))
    all_tiles = jnp.concatenate(pieces, axis=0)
    share_rows = (
        lax.psum_scatter(all_tiles, "seg", scatter_dimension=0, tiled=True)
        .astype(jnp.float32)
        .astype(jnp.bfloat16)
    )
    share_power = disperse(share_rows, phases)
    every_power = lax.all_gather(share_power, "seg", axis=0, tiled=True)
    mine, mine_filled = my_slots(tile_owner[0], segments)
    response = jnp.take(every_power, mine, axis=0) * mine_filled[:, None, None].astype(jnp.float32)
    return response[None, None]


CHIPS = 4
UNITS = 2 * QUAD
LAYERS = UNITS // 2
X_SWAP = [(0, 1), (1, 0), (2, 3), (3, 2)]
Y_SWAP = [(0, 2), (2, 0), (1, 3), (3, 1)]
X_EXTRA = [(1, 0), (2, 3)]
Y_EXTRA = [(2, 0), (1, 3)]
X_CORNER = [(0, 1), (2, 3)]
Y_CORNER = [(3, 1), (1, 3)]
BAND_FROM_X = [1, 0, 1, 0]
BAND_FROM_Y = [0, 0, 1, 1]
OWN_ROW, PAIR_ROW, EARLY_ROWS = 0, QUAD, 3 * QUAD


def source_rows():
    tiles = 3 * QUAD * QUAD
    early = np.full((CHIPS, UNITS, tiles, BANDS), -1, np.int32)
    corner = np.full((CHIPS, UNITS, tiles, BANDS), -1, np.int32)

    def put(block, step, p, q, band, chip, unit, row):
        tile = (step * QUAD + p) * QUAD + q
        for me in range(UNITS):
            r = (me // 2 - unit // 2) % LAYERS
            other = (me ^ unit) & 1
            hop = chip ^ block
            early[block, me, tile, band] = ((r * 2 + other) * 3 + hop) * EARLY_ROWS + row

    def put_corner(block, p, q, band, chip, unit, row):
        tile = (QUAD + p) * QUAD + q
        for me in range(UNITS):
            r = (me // 2 - unit // 2) % LAYERS
            other = (me ^ unit) & 1
            along_y = (chip, block) in Y_CORNER
            corner[block, me, tile, band] = ((r * 2 + other) * 2 + along_y) * 2 + row

    for chip in range(CHIPS):
        for n in range(UNITS):
            for p in range(QUAD):
                put(chip, 0, p, n % QUAD, n // QUAD, chip, n, OWN_ROW + p)
            q = n % QUAD
            band = (BAND_FROM_X[chip], BAND_FROM_Y[chip])[n // QUAD]
            for p in range(QUAD):
                direct, turned = PAIR_ROW + p, PAIR_ROW + QUAD + p
                if n >= QUAD:
                    put(chip, 2, p, q, band, chip, n, direct)
                    put(chip ^ 2, 2, q, p, band, chip, n, turned)
                elif chip % 2 == 0:
                    put(chip, 1, p, q, band, chip, n, direct)
                else:
                    put(chip ^ 1, 1, q, p, band, chip, n, turned)
            for i in range(2):
                m = n - QUAD
                if chip in (1, 2):
                    put_corner(3, 2 * (n >> 2) + i, n & 3, chip - 1, chip, n, i)
                elif m < 0:
                    put_corner(1, (2 if chip == 3 else 0) + i, n, 0, chip, n, i)
                else:
                    put_corner(1, 2 * (m & 1) + i, (m >> 1) + (2 if chip == 0 else 0), 1, chip, n, i)
    assert ((early >= 0) != (corner >= 0)).all()
    return np.stack([early, corner], axis=-1)


SOURCE_ROWS = source_rows()


SMALL = pl.CostEstimate(flops=1000, bytes_accessed=1000, transcendentals=0)


def in_hbm(arrays):
    return [pltpu.with_memory_space_constraint(a, pltpu.HBM) for a in arrays]


def hbm_like(shape):
    return pltpu.HBM(shape, jnp.bfloat16)


def params(limit=VMEM_LIMIT):
    return pltpu.CompilerParams(vmem_limit_bytes=limit)


def whiten_kernel(counted, spectra, whole, to_x, to_y, extra_x, extra_y):
    step = pl.program_id(0)
    half = pl.num_programs(0) // 2
    windows = spectra.shape[0]
    chip = lax.axis_index("blk")
    rows = pl.ds(pl.multiple_of(step * spectra.shape[1], spectra.shape[1]), spectra.shape[1])
    for w in range(windows):
        values = spectra[w].astype(jnp.float32)
        scaling = lax.rsqrt(jnp.mean(values * values, axis=1, keepdims=True) + 1e-05)
        scaling = scaling * jnp.where(w < counted[0], 1.0, 0.0)
        out = (values * scaling).astype(jnp.bfloat16)
        width = out.shape[1] // BANDS
        for band in range(BANDS):
            whole[band, w, rows] = out[:, band * width : (band + 1) * width]
    to_x[...] = whole[chip % 2, :, rows]
    to_y[...] = whole[1 - chip // 2, :, rows]

    @pl.when(step < half)
    def _():
        extra_x[...] = whole[chip // 2, :, rows]

    @pl.when(step >= half)
    def _():
        extra_y[...] = whole[chip // 2, :, rows]


def whiten(spectra, counted):
    windows, channels, width = spectra.shape
    band_width = width // BANDS
    steps = channels // TILE
    half = steps // 2
    block = (windows, TILE, band_width)
    full = hbm_like((windows, channels, band_width))
    part = hbm_like((windows, channels // 2, band_width))
    return pl.pallas_call(
        whiten_kernel,
        grid=(steps,),
        in_specs=[
            pl.BlockSpec(memory_space=pltpu.SMEM),
            pl.BlockSpec((windows, TILE, width), lambda i: (0, i, 0)),
        ],
        out_specs=[
            pl.BlockSpec(memory_space=pltpu.VMEM),
            pl.BlockSpec(block, lambda i: (0, i, 0)),
            pl.BlockSpec(block, lambda i: (0, i, 0)),
            pl.BlockSpec(block, lambda i: (0, jnp.minimum(i, half - 1), 0)),
            pl.BlockSpec(block, lambda i: (0, jnp.maximum(i - half, 0), 0)),
        ],
        out_shape=[
            pltpu.VMEM((BANDS, windows, channels, band_width), jnp.bfloat16),
            full,
            full,
            part,
            part,
        ],
        compiler_params=params(),
        cost_estimate=SMALL,
    )(counted, *in_hbm([spectra]))


def product(left, right, weight):
    total = None
    for rows, columns in zip(left, right):
        width = columns.shape[1] // 2
        turned = jnp.concatenate([-columns[:, width:], columns[:, :width]], axis=1)
        both = jnp.concatenate([columns, turned], axis=0)
        part = lax.dot_general(
            rows, both, (((1,), (1,)), ((), ())), preferred_element_type=jnp.float32
        )
        total = part if total is None else total + part
    return (total * weight).astype(jnp.bfloat16)


def tile_rows(tile):
    return pl.ds(pl.multiple_of(tile * TILE, TILE), TILE)


def each_unit(out):
    core = lax.axis_index("seg") % 2
    for other, ref in enumerate(out):
        for layer in range(LAYERS):
            yield layer, (1 - core if other else core), ref.at[layer]


def own_kernel(weight, whole, *out):
    for layer, core, ref in each_unit(out):
        band, q = layer // 2, 2 * (layer % 2) + core
        windows = range(whole.shape[1])
        ref[...] = product(
            [whole[band, w] for w in windows],
            [whole[band, w, tile_rows(q)] for w in windows],
            weight[0],
        )


def pair_kernel(weight, whole, from_x, from_y, *out):
    chip = lax.axis_index("blk")
    bands = (1 - chip % 2, chip // 2)
    for layer, core, ref in each_unit(out):
        along = layer // 2
        arrived, q = (from_x, from_y)[along], 2 * (layer % 2) + core
        windows = range(whole.shape[1])
        ref[...] = product(
            [whole[bands[along], w] for w in windows],
            [arrived[w, tile_rows(q)] for w in windows],
            weight[0],
        )


def corner_kernel(weight, from_x, from_y, extra_x, extra_y, *out):
    chip = lax.axis_index("blk")
    windows = range(from_x.shape[0])
    half = from_x.shape[1] // 2

    def multiply(left, left_half, right, tile, ref):
        rows = pl.ds(pl.multiple_of(left_half * half, half), half)
        ref[...] = product(
            [left[w, rows] for w in windows], [right[w, tile_rows(tile)] for w in windows], weight[0]
        )

    def split(one, two, extra_one, extra_two):
        for layer, core, ref in each_unit(out):
            if layer < LAYERS // 2:
                multiply(extra_one, 0, two, 2 * layer + core, ref)
            else:
                multiply(one, core, extra_two, layer - LAYERS // 2, ref)

    def joined(one, two):
        for layer, core, ref in each_unit(out):
            multiply(one, layer // 2, two, 2 * (layer % 2) + core, ref)

    pl.when(chip == 0)(lambda: split(from_x, from_y, extra_x, extra_y))
    pl.when(chip == 1)(lambda: joined(from_y, from_x))
    pl.when(chip == 2)(lambda: joined(from_x, from_y))
    pl.when(chip == 3)(lambda: split(from_y, from_x, extra_y, extra_x))


def in_vmem(count):
    return [pl.BlockSpec(memory_space=pltpu.VMEM)] * count


def unit_call(kernel, rows, weight, *arrays):
    out = jax.ShapeDtypeStruct((LAYERS, rows, 2 * TILE), jnp.bfloat16)
    return pl.pallas_call(
        kernel,
        in_specs=[pl.BlockSpec(memory_space=pltpu.SMEM)] + in_vmem(len(arrays)),
        out_specs=in_vmem(2),
        out_shape=[out, out],
        compiler_params=params(),
        cost_estimate=SMALL,
    )(weight, *arrays)


def pair_sum_kernel(kept, got, *outs):
    layer = lax.axis_index("seg") // 2
    for r, out in enumerate(outs):
        at = lax.rem(layer + r, LAYERS)
        out[...] = (kept[at].astype(jnp.float32) + got[at].astype(jnp.float32)).astype(jnp.bfloat16)


def pair_sum(kept, got):
    shape = jax.ShapeDtypeStruct(kept.shape[1:], jnp.bfloat16)
    return pl.pallas_call(
        pair_sum_kernel,
        in_specs=in_vmem(2),
        out_specs=in_vmem(LAYERS),
        out_shape=[shape] * LAYERS,
        compiler_params=params(),
        cost_estimate=SMALL,
    )(kept, got)


def layer_sum(parts):
    total = parts[0][...].astype(jnp.float32)
    for part in parts[1:]:
        total = total + part[...].astype(jnp.float32)
    return total.astype(jnp.bfloat16)


def tile_powers(rows, table):
    velocities = table.shape[1] // 2
    field = lax.dot_general(
        rows, table, (((1,), (0,)), ((), ())), preferred_element_type=jnp.float32
    )
    squared = field * field
    energy = squared[:, :velocities] + squared[:, velocities:]
    return [
        jnp.sum(energy[t : t + TILE], axis=0, keepdims=True) * (1.0 / TILE)
        for t in range(0, rows.shape[0], TILE)
    ]


def transposed(stacked):
    rounded = stacked.astype(jnp.float32)
    turned = []
    for t in range(0, stacked.shape[0], TILE):
        tile = rounded[t : t + TILE]
        turned.append(jnp.concatenate([tile[:, :TILE].T, -tile[:, TILE:].T], axis=1))
    return jnp.concatenate(turned, axis=0).astype(jnp.bfloat16)


def power_kernel(group, matrix, *refs):
    out = refs[-1]
    chip, me = lax.axis_index("blk"), lax.axis_index("seg")
    if group == "own":
        band = me // QUAD
    elif group == "pair":
        band = jnp.where(me < QUAD, 1 - chip % 2, chip // 2)
    else:
        band = jnp.where((chip == 1) | (chip == 2), chip - 1, me // QUAD)
    stacked = layer_sum(refs[:-1])
    table = matrix[band]
    found = tile_powers(stacked, table)
    if group == "pair":
        found += tile_powers(transposed(stacked), table)
    for t, row in enumerate(found):
        out[t : t + 1, :] = row


def powers_of(group, matrix, parts):
    velocities = matrix.shape[2] // 2
    rows = parts[0].shape[0] // TILE * (2 if group == "pair" else 1)
    return pl.pallas_call(
        functools.partial(power_kernel, group),
        in_specs=in_vmem(1 + len(parts)),
        out_specs=in_vmem(1)[0],
        out_shape=jax.ShapeDtypeStruct((rows, velocities), jnp.float32),
        compiler_params=params(),
        cost_estimate=SMALL,
    )(matrix, *parts)


def across(array, hops):
    return lax.ppermute(array, "blk", hops)


def across_cores(array, hops):
    pairs = [(UNITS * a + s, UNITS * b + (s ^ 1)) for a, b in hops for s in range(UNITS)]
    return lax.ppermute(array, ("blk", "seg"), pairs)


def other_core(array):
    return lax.ppermute(array, "seg", [(i, i ^ 1) for i in range(UNITS)])


def layers_on(array, r):
    return lax.ppermute(array, "seg", [(i, (i + 2 * r) % UNITS) for i in range(UNITS)])


def from_layers(array):
    return jnp.stack([array] + [layers_on(array, r) for r in range(1, LAYERS)])


def grid_body(spectra, window_count, tile_owner, phases):
    chip = lax.axis_index("blk")
    me = lax.axis_index("seg")
    whole, to_x, to_y, extra_x, extra_y = whiten(spectra[0], window_count)
    from_x, from_y = across(to_x, X_SWAP), across(to_y, Y_SWAP)
    extra_x, extra_y = across(extra_x, X_EXTRA), across(extra_y, Y_EXTRA)
    weight = 1.0 / (window_count.astype(jnp.float32) * math.sqrt(FB * UNITS))
    matrix = phase_matrix(phases)
    mine, mine_filled = my_slots(tile_owner[0], UNITS)
    sources = jnp.asarray(SOURCE_ROWS)[chip, me][mine]
    channels = whole.shape[2]

    def reduce(kernel, rows, weight, *arrays):
        kept, sent = unit_call(kernel, rows, weight, *arrays)
        sums = pair_sum(kept, other_core(sent))
        return [sums[0]] + [layers_on(sums[r], r) for r in range(1, LAYERS)]

    own = powers_of("own", matrix, reduce(own_kernel, channels, weight, whole))
    weight, own = lax.optimization_barrier((weight, own))
    pair = reduce(pair_kernel, channels, weight, whole, from_x, from_y)
    pair = powers_of("pair", matrix, pair)
    weight, pair = lax.optimization_barrier((weight, pair))
    corner = reduce(
        corner_kernel, channels // 2, weight, from_x, from_y, extra_x, extra_y
    )
    early = jnp.concatenate([own, pair], axis=0)
    near = jnp.stack([early, across(early, X_SWAP), across(early, Y_SWAP)])
    every = from_layers(jnp.stack([near, other_core(near)]))
    last = powers_of("corner", matrix, corner)
    every_last = from_layers(
        jnp.stack(
            [
                across(last, X_CORNER),
                across(last, Y_CORNER),
                across_cores(last, X_CORNER),
                across_cores(last, Y_CORNER),
            ]
        )
    )
    velocities = early.shape[-1]
    response = jnp.take(every.reshape(-1, velocities), jnp.maximum(sources[..., 0], 0), axis=0)
    response_last = jnp.take(
        every_last.reshape(-1, velocities), jnp.maximum(sources[..., 1], 0), axis=0
    )
    response = jnp.where(sources[..., 1:2] >= 0, response_last, response)
    response = response * mine_filled[:, None, None].astype(jnp.float32)
    return response[None, None]


def solution(mesh):
    placed = (P("seg", None, "blk", None), P("seg"), P("blk", None), P())
    fits = mesh.shape["blk"] == CHIPS and mesh.shape["seg"] == UNITS
    return jax.shard_map(
        grid_body if fits else ring_body,
        mesh=mesh,
        in_specs=placed,
        out_specs=P("blk", "seg", None, None, None),
        check_vma=False,
    )
```

```python
import functools
import math

import jax
import jax.numpy as jnp
import numpy as np
from jax import lax
from jax.experimental import pallas as pl
from jax.experimental.pallas import tpu as pltpu
from jax.sharding import PartitionSpec as P

TILE = 128
BANDS = 2
CAP = 8
FB = 512
QUAD = 4
VMEM_LIMIT = 8 * 1024 * 1024
WHITEN_LIMIT = 16 * 1024 * 1024


def from_behind(array, axis, by):
    devices = lax.axis_size(axis)
    return lax.ppermute(array, axis, [(i, (i + by) % devices) for i in range(devices)])


def prepare(segment_data, counted):
    windows = segment_data.shape[0]
    channels = segment_data.shape[1]
    spectrum = segment_data.astype(jnp.float32).reshape(windows, channels, BANDS, 2, FB)
    scaling = lax.rsqrt(jnp.mean(spectrum * spectrum, axis=(2, 3, 4)) + 1e-05)
    live_mask = (jnp.arange(windows, dtype=jnp.int32) < counted).astype(jnp.float32)
    return (
        spectrum * scaling[:, :, None, None, None] * live_mask[:, None, None, None, None]
    ).astype(jnp.bfloat16)


def correlate(resident, visiting, weight):
    windows = resident.shape[0]
    flipped = jnp.stack([-visiting[:, :, :, 1], visiting[:, :, :, 0]], axis=3)
    both_parts = jnp.stack([visiting, flipped], axis=1)
    left_side = resident.reshape(windows, QUAD, TILE, BANDS, 2 * FB)
    right_side = both_parts.reshape(windows, 2, QUAD, TILE, BANDS, 2 * FB)
    product = jnp.einsum(
        "wqibk,wpsjbk->qsbipj", left_side, right_side, preferred_element_type=jnp.float32
    )
    return (product * weight).astype(jnp.bfloat16).reshape(QUAD * QUAD, BANDS, TILE, 2 * TILE)


def phase_matrix(phases):
    norm_factor = 1.0 / math.sqrt(TILE)
    cosine = (jnp.cos(phases) * norm_factor).astype(jnp.bfloat16)
    sine_part = (jnp.sin(phases) * norm_factor).astype(jnp.bfloat16)
    upper = jnp.concatenate([cosine, sine_part], axis=2)
    lower = jnp.concatenate([-sine_part, cosine], axis=2)
    return jnp.concatenate([upper, lower], axis=1)


def disperse(stacked, phases):
    velocity_count = phases.shape[2]
    matrix = phase_matrix(phases)
    field = jnp.einsum("nbij,bjv->nbiv", stacked, matrix, preferred_element_type=jnp.float32)
    squared = field * field
    energy = squared[..., :velocity_count] + squared[..., velocity_count:]
    return jnp.mean(energy, axis=2)


def slot_table(owner_row, segments):
    count_tiles = owner_row.shape[0]
    order_ids = jnp.arange(count_tiles, dtype=jnp.int32)
    same_owner = owner_row[:, None] == owner_row[None, :]
    earlier = order_ids[None, :] < order_ids[:, None]
    rank_of = jnp.sum(jnp.where(same_owner & earlier, 1, 0), axis=1).astype(jnp.int32)
    slot_ids = owner_row * CAP + rank_of
    grid_ids = jnp.arange(segments * CAP, dtype=jnp.int32)
    matches = grid_ids[:, None] == slot_ids[None, :]
    tile_of_slot = jnp.sum(jnp.where(matches, order_ids[None, :], 0), axis=1)
    filled = jnp.any(matches, axis=1)
    return (tile_of_slot, filled)


def my_slots(owner_row, segments):
    tile_of_slot, filled = slot_table(owner_row, segments)
    my_start = lax.axis_index("seg") * CAP
    mine = lax.dynamic_slice_in_dim(tile_of_slot, my_start, CAP, 0)
    mine_filled = lax.dynamic_slice_in_dim(filled, my_start, CAP, 0)
    return mine, mine_filled


def ring_body(spectra, window_count, tile_owner, phases):
    blocks = lax.axis_size("blk")
    segments = lax.axis_size("seg")
    counted = window_count[0]
    whitened = prepare(spectra[0], counted)
    weight = 1.0 / (counted.astype(jnp.float32) * math.sqrt(FB * segments))
    pieces = [correlate(whitened, whitened, weight)]
    moving = whitened
    for shift_step in range(1, blocks // 2 + 1):
        moving = from_behind(moving, "blk", -1)
        pieces.append(correlate(whitened, moving, weight))
    all_tiles = jnp.concatenate(pieces, axis=0)
    share_rows = (
        lax.psum_scatter(all_tiles, "seg", scatter_dimension=0, tiled=True)
        .astype(jnp.float32)
        .astype(jnp.bfloat16)
    )
    share_power = disperse(share_rows, phases)
    every_power = lax.all_gather(share_power, "seg", axis=0, tiled=True)
    mine, mine_filled = my_slots(tile_owner[0], segments)
    response = jnp.take(every_power, mine, axis=0) * mine_filled[:, None, None].astype(jnp.float32)
    return response[None, None]


CHIPS = 4
UNITS = 2 * QUAD
LAYERS = UNITS // 2
X_SWAP = [(0, 1), (1, 0), (2, 3), (3, 2)]
Y_SWAP = [(0, 2), (2, 0), (1, 3), (3, 1)]
X_EXTRA = [(1, 0), (2, 3)]
Y_EXTRA = [(2, 0), (1, 3)]
X_CORNER = [(0, 1), (2, 3)]
Y_CORNER = [(3, 1), (1, 3)]
BAND_FROM_X = [1, 0, 1, 0]
BAND_FROM_Y = [0, 0, 1, 1]
OWN_ROW, PAIR_ROW, TURNED_ROW, CORE_ROWS = 0, QUAD, 2 * QUAD, 3 * QUAD
CORNER_ROW, LAYER_ROWS = 2 * CORE_ROWS, 2 * CORE_ROWS + 8
TURNED_HOPS = [
    (UNITS * chip + n, UNITS * (chip ^ (1 if n < QUAD else 2)) + n)
    for chip in range(CHIPS)
    for n in range(UNITS)
]


def source_rows():
    table = np.full((CHIPS, UNITS, 3 * QUAD * QUAD, BANDS), -1, np.int32)

    def put(block, step, p, q, band, unit, row, corner=0):
        tile = (step * QUAD + p) * QUAD + q
        for me in range(UNITS):
            layer, other = (me // 2 - unit // 2) % LAYERS, (me ^ unit) & 1
            at = CORNER_ROW + 4 * other + row if corner else CORE_ROWS * other + row
            table[block, me, tile, band] = layer * LAYER_ROWS + at

    for chip in range(CHIPS):
        for n in range(UNITS):
            for p in range(QUAD):
                put(chip, 0, p, n % QUAD, n // QUAD, n, OWN_ROW + p)
            q = n % QUAD
            band = (BAND_FROM_X[chip], BAND_FROM_Y[chip])[n // QUAD]
            for p in range(QUAD):
                if n >= QUAD:
                    put(chip, 2, p, q, band, n, PAIR_ROW + p)
                    put(chip ^ 2, 2, q, p, band, n, TURNED_ROW + p)
                elif chip % 2 == 0:
                    put(chip, 1, p, q, band, n, PAIR_ROW + p)
                else:
                    put(chip ^ 1, 1, q, p, band, n, TURNED_ROW + p)
            for i in range(2):
                m = n - QUAD
                block = 3 if chip in (1, 2) else 1
                row = 2 * ((chip, block) in Y_CORNER) + i
                if block == 3:
                    put(3, 1, 2 * (n >> 2) + i, n & 3, chip - 1, n, row, 1)
                elif m < 0:
                    put(1, 1, (2 if chip == 3 else 0) + i, n, 0, n, row, 1)
                else:
                    put(1, 1, 2 * (m & 1) + i, (m >> 1) + (2 if chip == 0 else 0), 1, n, row, 1)
    assert table.min() >= 0
    return table


SOURCE_ROWS = source_rows()


SMALL = pl.CostEstimate(flops=1000, bytes_accessed=1000, transcendentals=0)


def in_hbm(arrays):
    return [pltpu.with_memory_space_constraint(a, pltpu.HBM) for a in arrays]


def hbm_like(shape):
    return pltpu.HBM(shape, jnp.bfloat16)


def params(limit=VMEM_LIMIT):
    return pltpu.CompilerParams(vmem_limit_bytes=limit)


def whiten_kernel(counted, spectra, whole, to_x, to_y, extra_x, extra_y):
    step = pl.program_id(0)
    half = pl.num_programs(0) // 2
    windows = spectra.shape[0]
    chip = lax.axis_index("blk")
    rows = pl.ds(pl.multiple_of(step * spectra.shape[1], spectra.shape[1]), spectra.shape[1])
    for w in range(windows):
        values = spectra[w].astype(jnp.float32)
        scaling = lax.rsqrt(jnp.mean(values * values, axis=1, keepdims=True) + 1e-05)
        scaling = scaling * jnp.where(w < counted[0], 1.0, 0.0)
        out = (values * scaling).astype(jnp.bfloat16)
        width = out.shape[1] // BANDS
        for band in range(BANDS):
            whole[band, w, rows] = out[:, band * width : (band + 1) * width]
    to_x[...] = whole[chip % 2, :, rows]
    to_y[...] = whole[1 - chip // 2, :, rows]

    @pl.when(step < half)
    def _():
        extra_x[...] = whole[chip // 2, :, rows]

    @pl.when(step >= half)
    def _():
        extra_y[...] = whole[chip // 2, :, rows]


def whiten(spectra, counted):
    windows, channels, width = spectra.shape
    band_width = width // BANDS
    steps = channels // TILE
    half = steps // 2
    block = (windows, TILE, band_width)
    full = hbm_like((windows, channels, band_width))
    part = hbm_like((windows, channels // 2, band_width))
    return pl.pallas_call(
        whiten_kernel,
        grid=(steps,),
        in_specs=[
            pl.BlockSpec(memory_space=pltpu.SMEM),
            pl.BlockSpec((windows, TILE, width), lambda i: (0, i, 0)),
        ],
        out_specs=[
            pl.BlockSpec(memory_space=pltpu.VMEM),
            pl.BlockSpec(block, lambda i: (0, i, 0)),
            pl.BlockSpec(block, lambda i: (0, i, 0)),
            pl.BlockSpec(block, lambda i: (0, jnp.minimum(i, half - 1), 0)),
            pl.BlockSpec(block, lambda i: (0, jnp.maximum(i - half, 0), 0)),
        ],
        out_shape=[
            pltpu.VMEM((BANDS, windows, channels, band_width), jnp.bfloat16),
            full,
            full,
            part,
            part,
        ],
        compiler_params=params(WHITEN_LIMIT),
        cost_estimate=SMALL,
    )(counted, *in_hbm([spectra]))


def product(left, right, weight):
    total = None
    for rows, columns in zip(left, right):
        width = columns.shape[1] // 2
        turned = jnp.concatenate([-columns[:, width:], columns[:, :width]], axis=1)
        both = jnp.concatenate([columns, turned], axis=0)
        part = lax.dot_general(
            rows, both, (((1,), (1,)), ((), ())), preferred_element_type=jnp.float32
        )
        total = part if total is None else total + part
    return (total * weight).astype(jnp.bfloat16)


def tile_rows(tile):
    return pl.ds(pl.multiple_of(tile * TILE, TILE), TILE)


def each_unit(out):
    core = lax.axis_index("seg") % 2
    for other, ref in enumerate(out):
        for layer in range(LAYERS):
            yield layer, (1 - core if other else core), ref.at[layer]


def own_kernel(weight, whole, *out):
    for layer, core, ref in each_unit(out):
        band, q = layer // 2, 2 * (layer % 2) + core
        windows = range(whole.shape[1])
        ref[...] = product(
            [whole[band, w] for w in windows],
            [whole[band, w, tile_rows(q)] for w in windows],
            weight[0],
        )


def pair_kernel(weight, whole, from_x, from_y, *out):
    chip = lax.axis_index("blk")
    bands = (1 - chip % 2, chip // 2)
    for layer, core, ref in each_unit(out):
        along = layer // 2
        arrived, q = (from_x, from_y)[along], 2 * (layer % 2) + core
        windows = range(whole.shape[1])
        ref[...] = product(
            [whole[bands[along], w] for w in windows],
            [arrived[w, tile_rows(q)] for w in windows],
            weight[0],
        )


def corner_kernel(weight, from_x, from_y, extra_x, extra_y, *out):
    chip = lax.axis_index("blk")
    windows = range(from_x.shape[0])
    half = from_x.shape[1] // 2

    def multiply(left, left_half, right, tile, ref):
        rows = pl.ds(pl.multiple_of(left_half * half, half), half)
        ref[...] = product(
            [left[w, rows] for w in windows], [right[w, tile_rows(tile)] for w in windows], weight[0]
        )

    def split(one, two, extra_one, extra_two):
        for layer, core, ref in each_unit(out):
            if layer < LAYERS // 2:
                multiply(extra_one, 0, two, 2 * layer + core, ref)
            else:
                multiply(one, core, extra_two, layer - LAYERS // 2, ref)

    def joined(one, two):
        for layer, core, ref in each_unit(out):
            multiply(one, layer // 2, two, 2 * (layer % 2) + core, ref)

    pl.when(chip == 0)(lambda: split(from_x, from_y, extra_x, extra_y))
    pl.when(chip == 1)(lambda: joined(from_y, from_x))
    pl.when(chip == 2)(lambda: joined(from_x, from_y))
    pl.when(chip == 3)(lambda: split(from_y, from_x, extra_y, extra_x))


def in_vmem(count):
    return [pl.BlockSpec(memory_space=pltpu.VMEM)] * count


def unit_call(kernel, rows, weight, *arrays):
    out = jax.ShapeDtypeStruct((LAYERS, rows, 2 * TILE), jnp.bfloat16)
    return pl.pallas_call(
        kernel,
        in_specs=[pl.BlockSpec(memory_space=pltpu.SMEM)] + in_vmem(len(arrays)),
        out_specs=in_vmem(2),
        out_shape=[out, out],
        compiler_params=params(),
        cost_estimate=SMALL,
    )(weight, *arrays)


def pair_sum_kernel(kept, got, *outs):
    layer = lax.axis_index("seg") // 2
    for r, out in enumerate(outs):
        at = lax.rem(layer + r, LAYERS)
        out[...] = (kept[at].astype(jnp.float32) + got[at].astype(jnp.float32)).astype(jnp.bfloat16)


def pair_sum(kept, got):
    shape = jax.ShapeDtypeStruct(kept.shape[1:], jnp.bfloat16)
    return pl.pallas_call(
        pair_sum_kernel,
        in_specs=in_vmem(2),
        out_specs=in_vmem(LAYERS),
        out_shape=[shape] * LAYERS,
        compiler_params=params(),
        cost_estimate=SMALL,
    )(kept, got)


def layer_sum(parts):
    total = parts[0][...].astype(jnp.float32)
    for part in parts[1:]:
        total = total + part[...].astype(jnp.float32)
    return total.astype(jnp.bfloat16)


def tile_powers(rows, table):
    velocities = table.shape[1] // 2
    field = lax.dot_general(
        rows, table, (((1,), (0,)), ((), ())), preferred_element_type=jnp.float32
    )
    squared = field * field
    energy = squared[:, :velocities] + squared[:, velocities:]
    return [
        jnp.sum(energy[t : t + TILE], axis=0, keepdims=True) * (1.0 / TILE)
        for t in range(0, rows.shape[0], TILE)
    ]


def transposed(stacked):
    rounded = stacked.astype(jnp.float32)
    turned = []
    for t in range(0, stacked.shape[0], TILE):
        tile = rounded[t : t + TILE]
        turned.append(jnp.concatenate([tile[:, :TILE].T, -tile[:, TILE:].T], axis=1))
    return jnp.concatenate(turned, axis=0).astype(jnp.bfloat16)


def power_kernel(group, matrix, *refs):
    out = refs[-1]
    chip, me = lax.axis_index("blk"), lax.axis_index("seg")
    if group == "own":
        band = me // QUAD
    elif group == "pair":
        band = jnp.where(me < QUAD, 1 - chip % 2, chip // 2)
    else:
        band = jnp.where((chip == 1) | (chip == 2), chip - 1, me // QUAD)
    stacked = layer_sum(refs[:-1])
    table = matrix[band]
    found = tile_powers(stacked, table)
    if group == "pair":
        found += tile_powers(transposed(stacked), table)
    for t, row in enumerate(found):
        out[t : t + 1, :] = row


def powers_of(group, matrix, parts):
    velocities = matrix.shape[2] // 2
    rows = parts[0].shape[0] // TILE * (2 if group == "pair" else 1)
    return pl.pallas_call(
        functools.partial(power_kernel, group),
        in_specs=in_vmem(1 + len(parts)),
        out_specs=in_vmem(1)[0],
        out_shape=jax.ShapeDtypeStruct((rows, velocities), jnp.float32),
        compiler_params=params(),
        cost_estimate=SMALL,
    )(matrix, *parts)


def across(array, hops):
    return lax.ppermute(array, "blk", hops)


def across_cores(array, hops):
    pairs = [(UNITS * a + s, UNITS * b + (s ^ 1)) for a, b in hops for s in range(UNITS)]
    return lax.ppermute(array, ("blk", "seg"), pairs)


def other_core(array):
    return lax.ppermute(array, "seg", [(i, i ^ 1) for i in range(UNITS)])


def layers_on(array, r):
    return lax.ppermute(array, "seg", [(i, (i + 2 * r) % UNITS) for i in range(UNITS)])


def from_layers(array):
    return jnp.stack([array] + [layers_on(array, r) for r in range(1, LAYERS)])


def grid_body(spectra, window_count, tile_owner, phases):
    chip = lax.axis_index("blk")
    me = lax.axis_index("seg")
    whole, to_x, to_y, extra_x, extra_y = whiten(spectra[0], window_count)
    from_x, from_y = across(to_x, X_SWAP), across(to_y, Y_SWAP)
    extra_x, extra_y = across(extra_x, X_EXTRA), across(extra_y, Y_EXTRA)
    weight = 1.0 / (window_count.astype(jnp.float32) * math.sqrt(FB * UNITS))
    matrix = phase_matrix(phases)
    mine, mine_filled = my_slots(tile_owner[0], UNITS)
    sources = jnp.asarray(SOURCE_ROWS)[chip, me][mine]
    channels = whole.shape[2]

    def reduce(kernel, rows, weight, earlier, *arrays):
        kept, sent = unit_call(kernel, rows, weight, *arrays)
        sent, *earlier = lax.optimization_barrier((sent, *earlier))
        sums = pair_sum(kept, other_core(sent))
        return [sums[0]] + [layers_on(sums[r], r) for r in range(1, LAYERS)], earlier

    own, _ = reduce(own_kernel, channels, weight, [], whole)
    own = powers_of("own", matrix, own)
    weight, own = lax.optimization_barrier((weight, own))
    pair, _ = reduce(pair_kernel, channels, weight, [], whole, from_x, from_y)
    corner, pair = reduce(
        corner_kernel, channels // 2, weight, pair, from_x, from_y, extra_x, extra_y
    )
    pair = powers_of("pair", matrix, pair)
    turned = lax.ppermute(pair[QUAD:], ("blk", "seg"), TURNED_HOPS)
    near = jnp.concatenate([own, pair[:QUAD], turned], axis=0)
    far = other_core(near)
    last = powers_of("corner", matrix, corner)
    rows = jnp.concatenate(
        [
            near,
            far,
            across(last, X_CORNER),
            across(last, Y_CORNER),
            across_cores(last, X_CORNER),
            across_cores(last, Y_CORNER),
        ],
        axis=0,
    )
    every = from_layers(rows)
    response = jnp.take(every.reshape(-1, every.shape[-1]), sources, axis=0)
    response = response * mine_filled[:, None, None].astype(jnp.float32)
    return response[None, None]


def solution(mesh):
    placed = (P("seg", None, "blk", None), P("seg"), P("blk", None), P())
    fits = mesh.shape["blk"] == CHIPS and mesh.shape["seg"] == UNITS
    return jax.shard_map(
        grid_body if fits else ring_body,
        mesh=mesh,
        in_specs=placed,
        out_specs=P("blk", "seg", None, None, None),
        check_vma=False,
    )
```

```python
import functools
import math

import jax
import jax.numpy as jnp
import numpy as np
from jax import lax
from jax.experimental import pallas as pl
from jax.experimental.pallas import tpu as pltpu
from jax.sharding import PartitionSpec as P

TILE = 128
BANDS = 2
CAP = 8
FB = 512
QUAD = 4
VMEM_LIMIT = 8 * 1024 * 1024
WHITEN_LIMIT = 16 * 1024 * 1024


def from_behind(array, axis, by):
    devices = lax.axis_size(axis)
    return lax.ppermute(array, axis, [(i, (i + by) % devices) for i in range(devices)])


def prepare(segment_data, counted):
    windows = segment_data.shape[0]
    channels = segment_data.shape[1]
    spectrum = segment_data.astype(jnp.float32).reshape(windows, channels, BANDS, 2, FB)
    scaling = lax.rsqrt(jnp.mean(spectrum * spectrum, axis=(2, 3, 4)) + 1e-05)
    live_mask = (jnp.arange(windows, dtype=jnp.int32) < counted).astype(jnp.float32)
    return (
        spectrum * scaling[:, :, None, None, None] * live_mask[:, None, None, None, None]
    ).astype(jnp.bfloat16)


def correlate(resident, visiting, weight):
    windows = resident.shape[0]
    flipped = jnp.stack([-visiting[:, :, :, 1], visiting[:, :, :, 0]], axis=3)
    both_parts = jnp.stack([visiting, flipped], axis=1)
    left_side = resident.reshape(windows, QUAD, TILE, BANDS, 2 * FB)
    right_side = both_parts.reshape(windows, 2, QUAD, TILE, BANDS, 2 * FB)
    product = jnp.einsum(
        "wqibk,wpsjbk->qsbipj", left_side, right_side, preferred_element_type=jnp.float32
    )
    return (product * weight).astype(jnp.bfloat16).reshape(QUAD * QUAD, BANDS, TILE, 2 * TILE)


def phase_matrix(phases):
    norm_factor = 1.0 / math.sqrt(TILE)
    cosine = (jnp.cos(phases) * norm_factor).astype(jnp.bfloat16)
    sine_part = (jnp.sin(phases) * norm_factor).astype(jnp.bfloat16)
    upper = jnp.concatenate([cosine, sine_part], axis=2)
    lower = jnp.concatenate([-sine_part, cosine], axis=2)
    return jnp.concatenate([upper, lower], axis=1)


def disperse(stacked, phases):
    velocity_count = phases.shape[2]
    matrix = phase_matrix(phases)
    field = jnp.einsum("nbij,bjv->nbiv", stacked, matrix, preferred_element_type=jnp.float32)
    squared = field * field
    energy = squared[..., :velocity_count] + squared[..., velocity_count:]
    return jnp.mean(energy, axis=2)


def slot_table(owner_row, segments):
    count_tiles = owner_row.shape[0]
    order_ids = jnp.arange(count_tiles, dtype=jnp.int32)
    same_owner = owner_row[:, None] == owner_row[None, :]
    earlier = order_ids[None, :] < order_ids[:, None]
    rank_of = jnp.sum(jnp.where(same_owner & earlier, 1, 0), axis=1).astype(jnp.int32)
    slot_ids = owner_row * CAP + rank_of
    grid_ids = jnp.arange(segments * CAP, dtype=jnp.int32)
    matches = grid_ids[:, None] == slot_ids[None, :]
    tile_of_slot = jnp.sum(jnp.where(matches, order_ids[None, :], 0), axis=1)
    filled = jnp.any(matches, axis=1)
    return (tile_of_slot, filled)


def my_slots(owner_row, segments):
    tile_of_slot, filled = slot_table(owner_row, segments)
    my_start = lax.axis_index("seg") * CAP
    mine = lax.dynamic_slice_in_dim(tile_of_slot, my_start, CAP, 0)
    mine_filled = lax.dynamic_slice_in_dim(filled, my_start, CAP, 0)
    return mine, mine_filled


def ring_body(spectra, window_count, tile_owner, phases):
    blocks = lax.axis_size("blk")
    segments = lax.axis_size("seg")
    counted = window_count[0]
    whitened = prepare(spectra[0], counted)
    weight = 1.0 / (counted.astype(jnp.float32) * math.sqrt(FB * segments))
    pieces = [correlate(whitened, whitened, weight)]
    moving = whitened
    for shift_step in range(1, blocks // 2 + 1):
        moving = from_behind(moving, "blk", -1)
        pieces.append(correlate(whitened, moving, weight))
    all_tiles = jnp.concatenate(pieces, axis=0)
    share_rows = (
        lax.psum_scatter(all_tiles, "seg", scatter_dimension=0, tiled=True)
        .astype(jnp.float32)
        .astype(jnp.bfloat16)
    )
    share_power = disperse(share_rows, phases)
    every_power = lax.all_gather(share_power, "seg", axis=0, tiled=True)
    mine, mine_filled = my_slots(tile_owner[0], segments)
    response = jnp.take(every_power, mine, axis=0) * mine_filled[:, None, None].astype(jnp.float32)
    return response[None, None]


CHIPS = 4
UNITS = 2 * QUAD
LAYERS = UNITS // 2
X_SWAP = [(0, 1), (1, 0), (2, 3), (3, 2)]
Y_SWAP = [(0, 2), (2, 0), (1, 3), (3, 1)]
X_EXTRA = [(1, 0), (2, 3)]
Y_EXTRA = [(2, 0), (1, 3)]
X_CORNER = [(0, 1), (2, 3)]
Y_CORNER = [(3, 1), (1, 3)]
BAND_FROM_X = [1, 0, 1, 0]
BAND_FROM_Y = [0, 0, 1, 1]
OWN_ROW, PAIR_ROW, TURNED_ROW, CORE_ROWS = 0, QUAD, 2 * QUAD, 3 * QUAD
CORNER_ROW, LAYER_ROWS = 2 * CORE_ROWS, 2 * CORE_ROWS + 8
TURNED_HOPS = [
    (UNITS * chip + n, UNITS * (chip ^ (1 if n < QUAD else 2)) + n)
    for chip in range(CHIPS)
    for n in range(UNITS)
]


def source_rows():
    table = np.full((CHIPS, UNITS, 3 * QUAD * QUAD, BANDS), -1, np.int32)

    def put(block, step, p, q, band, unit, row, corner=0):
        tile = (step * QUAD + p) * QUAD + q
        for me in range(UNITS):
            layer, other = (me // 2 - unit // 2) % LAYERS, (me ^ unit) & 1
            at = CORNER_ROW + 4 * other + row if corner else CORE_ROWS * other + row
            table[block, me, tile, band] = layer * LAYER_ROWS + at

    for chip in range(CHIPS):
        for n in range(UNITS):
            for p in range(QUAD):
                put(chip, 0, p, n % QUAD, n // QUAD, n, OWN_ROW + p)
            q = n % QUAD
            band = (BAND_FROM_X[chip], BAND_FROM_Y[chip])[n // QUAD]
            for p in range(QUAD):
                if n >= QUAD:
                    put(chip, 2, p, q, band, n, PAIR_ROW + p)
                    put(chip ^ 2, 2, q, p, band, n, TURNED_ROW + p)
                elif chip % 2 == 0:
                    put(chip, 1, p, q, band, n, PAIR_ROW + p)
                else:
                    put(chip ^ 1, 1, q, p, band, n, TURNED_ROW + p)
            for i in range(2):
                m = n - QUAD
                block = 3 if chip in (1, 2) else 1
                row = 2 * ((chip, block) in Y_CORNER) + i
                if block == 3:
                    put(3, 1, 2 * (n >> 2) + i, n & 3, chip - 1, n, row, 1)
                elif m < 0:
                    put(1, 1, (2 if chip == 3 else 0) + i, n, 0, n, row, 1)
                else:
                    put(1, 1, 2 * (m & 1) + i, (m >> 1) + (2 if chip == 0 else 0), 1, n, row, 1)
    assert table.min() >= 0
    return table


SOURCE_ROWS = source_rows()


SMALL = pl.CostEstimate(flops=1000, bytes_accessed=1000, transcendentals=0)


def in_hbm(arrays):
    return [pltpu.with_memory_space_constraint(a, pltpu.HBM) for a in arrays]


def hbm_like(shape):
    return pltpu.HBM(shape, jnp.bfloat16)


def params(limit=VMEM_LIMIT):
    return pltpu.CompilerParams(vmem_limit_bytes=limit)


def whiten_kernel(counted, spectra, whole, to_x, to_y, extra_x, extra_y):
    step = pl.program_id(0)
    half = pl.num_programs(0) // 2
    windows = spectra.shape[0]
    chip = lax.axis_index("blk")
    rows = pl.ds(pl.multiple_of(step * spectra.shape[1], spectra.shape[1]), spectra.shape[1])
    for w in range(windows):
        values = spectra[w].astype(jnp.float32)
        scaling = lax.rsqrt(jnp.mean(values * values, axis=1, keepdims=True) + 1e-05)
        scaling = scaling * jnp.where(w < counted[0], 1.0, 0.0)
        out = (values * scaling).astype(jnp.bfloat16)
        width = out.shape[1] // BANDS
        for band in range(BANDS):
            whole[band, w, rows] = out[:, band * width : (band + 1) * width]
    to_x[...] = whole[chip % 2, :, rows]
    to_y[...] = whole[1 - chip // 2, :, rows]

    @pl.when(step < half)
    def _():
        extra_x[...] = whole[chip // 2, :, rows]

    @pl.when(step >= half)
    def _():
        extra_y[...] = whole[chip // 2, :, rows]


def whiten(spectra, counted):
    windows, channels, width = spectra.shape
    band_width = width // BANDS
    steps = channels // TILE
    half = steps // 2
    block = (windows, TILE, band_width)
    full = hbm_like((windows, channels, band_width))
    part = hbm_like((windows, channels // 2, band_width))
    return pl.pallas_call(
        whiten_kernel,
        grid=(steps,),
        in_specs=[
            pl.BlockSpec(memory_space=pltpu.SMEM),
            pl.BlockSpec((windows, TILE, width), lambda i: (0, i, 0)),
        ],
        out_specs=[
            pl.BlockSpec(memory_space=pltpu.VMEM),
            pl.BlockSpec(block, lambda i: (0, i, 0)),
            pl.BlockSpec(block, lambda i: (0, i, 0)),
            pl.BlockSpec(block, lambda i: (0, jnp.minimum(i, half - 1), 0)),
            pl.BlockSpec(block, lambda i: (0, jnp.maximum(i - half, 0), 0)),
        ],
        out_shape=[
            pltpu.VMEM((BANDS, windows, channels, band_width), jnp.bfloat16),
            full,
            full,
            part,
            part,
        ],
        compiler_params=params(WHITEN_LIMIT),
        cost_estimate=SMALL,
    )(counted, *in_hbm([spectra]))


def product(left, right, weight):
    total = None
    for rows, columns in zip(left, right):
        width = columns.shape[1] // 2
        turned = jnp.concatenate([-columns[:, width:], columns[:, :width]], axis=1)
        both = jnp.concatenate([columns, turned], axis=0)
        part = lax.dot_general(
            rows, both, (((1,), (1,)), ((), ())), preferred_element_type=jnp.float32
        )
        total = part if total is None else total + part
    return (total * weight).astype(jnp.bfloat16)


def tile_rows(tile):
    return pl.ds(pl.multiple_of(tile * TILE, TILE), TILE)


def each_unit(out):
    core = lax.axis_index("seg") % 2
    for other, ref in enumerate(out):
        for layer in range(LAYERS):
            yield layer, (1 - core if other else core), ref.at[layer]


def own_kernel(weight, whole, *out):
    for layer, core, ref in each_unit(out):
        band, q = layer // 2, 2 * (layer % 2) + core
        windows = range(whole.shape[1])
        ref[...] = product(
            [whole[band, w] for w in windows],
            [whole[band, w, tile_rows(q)] for w in windows],
            weight[0],
        )


def pair_kernel(weight, whole, from_x, from_y, *out):
    chip = lax.axis_index("blk")
    bands = (1 - chip % 2, chip // 2)
    for layer, core, ref in each_unit(out):
        along = layer // 2
        arrived, q = (from_x, from_y)[along], 2 * (layer % 2) + core
        windows = range(whole.shape[1])
        ref[...] = product(
            [whole[bands[along], w] for w in windows],
            [arrived[w, tile_rows(q)] for w in windows],
            weight[0],
        )


def corner_kernel(weight, from_x, from_y, extra_x, extra_y, *out):
    chip = lax.axis_index("blk")
    windows = range(from_x.shape[0])
    half = from_x.shape[1] // 2

    def multiply(left, left_half, right, tile, ref):
        rows = pl.ds(pl.multiple_of(left_half * half, half), half)
        ref[...] = product(
            [left[w, rows] for w in windows], [right[w, tile_rows(tile)] for w in windows], weight[0]
        )

    def split(one, two, extra_one, extra_two):
        for layer, core, ref in each_unit(out):
            if layer < LAYERS // 2:
                multiply(extra_one, 0, two, 2 * layer + core, ref)
            else:
                multiply(one, core, extra_two, layer - LAYERS // 2, ref)

    def joined(one, two):
        for layer, core, ref in each_unit(out):
            multiply(one, layer // 2, two, 2 * (layer % 2) + core, ref)

    pl.when(chip == 0)(lambda: split(from_x, from_y, extra_x, extra_y))
    pl.when(chip == 1)(lambda: joined(from_y, from_x))
    pl.when(chip == 2)(lambda: joined(from_x, from_y))
    pl.when(chip == 3)(lambda: split(from_y, from_x, extra_y, extra_x))


def in_vmem(count):
    return [pl.BlockSpec(memory_space=pltpu.VMEM)] * count


def unit_call(kernel, rows, weight, *arrays):
    out = jax.ShapeDtypeStruct((LAYERS, rows, 2 * TILE), jnp.bfloat16)
    return pl.pallas_call(
        kernel,
        in_specs=[pl.BlockSpec(memory_space=pltpu.SMEM)] + in_vmem(len(arrays)),
        out_specs=in_vmem(2),
        out_shape=[out, out],
        compiler_params=params(),
        cost_estimate=SMALL,
    )(weight, *arrays)


def pair_sum_kernel(kept, got, *outs):
    layer = lax.axis_index("seg") // 2
    for r, out in enumerate(outs):
        at = lax.rem(layer + r, LAYERS)
        out[...] = (kept[at].astype(jnp.float32) + got[at].astype(jnp.float32)).astype(jnp.bfloat16)


def pair_sum(kept, got):
    shape = jax.ShapeDtypeStruct(kept.shape[1:], jnp.bfloat16)
    return pl.pallas_call(
        pair_sum_kernel,
        in_specs=in_vmem(2),
        out_specs=in_vmem(LAYERS),
        out_shape=[shape] * LAYERS,
        compiler_params=params(),
        cost_estimate=SMALL,
    )(kept, got)


def layer_sum(parts):
    total = parts[0][...].astype(jnp.float32)
    for part in parts[1:]:
        total = total + part[...].astype(jnp.float32)
    return total.astype(jnp.bfloat16)


def tile_powers(rows, table):
    velocities = table.shape[1] // 2
    field = lax.dot_general(
        rows, table, (((1,), (0,)), ((), ())), preferred_element_type=jnp.float32
    )
    squared = field * field
    energy = squared[:, :velocities] + squared[:, velocities:]
    return [
        jnp.sum(energy[t : t + TILE], axis=0, keepdims=True) * (1.0 / TILE)
        for t in range(0, rows.shape[0], TILE)
    ]


def transposed(stacked):
    rounded = stacked.astype(jnp.float32)
    turned = []
    for t in range(0, stacked.shape[0], TILE):
        tile = rounded[t : t + TILE]
        turned.append(jnp.concatenate([tile[:, :TILE].T, -tile[:, TILE:].T], axis=1))
    return jnp.concatenate(turned, axis=0).astype(jnp.bfloat16)


def matrix_kernel(phases, matrix):
    rows, velocities = phases.shape[1:]
    norm_factor = 1.0 / math.sqrt(TILE)
    for band in range(phases.shape[0]):
        cosine = (jnp.cos(phases[band]) * norm_factor).astype(jnp.bfloat16)
        sine_part = (jnp.sin(phases[band]) * norm_factor).astype(jnp.bfloat16)
        matrix[band, :rows, :velocities] = cosine
        matrix[band, :rows, velocities:] = sine_part
        matrix[band, rows:, :velocities] = -sine_part
        matrix[band, rows:, velocities:] = cosine


def matrix_of(phases):
    bands, rows, velocities = phases.shape
    return pl.pallas_call(
        matrix_kernel,
        in_specs=in_vmem(1),
        out_specs=in_vmem(1)[0],
        out_shape=jax.ShapeDtypeStruct((bands, 2 * rows, 2 * velocities), jnp.bfloat16),
        compiler_params=params(),
        cost_estimate=SMALL,
    )(phases)


def power_kernel(group, matrix, *refs):
    out = refs[-1]
    chip, me = lax.axis_index("blk"), lax.axis_index("seg")
    if group == "own":
        band = me // QUAD
    elif group == "pair":
        band = jnp.where(me < QUAD, 1 - chip % 2, chip // 2)
    else:
        band = jnp.where((chip == 1) | (chip == 2), chip - 1, me // QUAD)
    stacked = layer_sum(refs[:-1])
    table = matrix[band]
    found = tile_powers(stacked, table)
    if group == "pair":
        found += tile_powers(transposed(stacked), table)
    for t, row in enumerate(found):
        out[t : t + 1, :] = row


def powers_of(group, matrix, parts):
    velocities = matrix.shape[2] // 2
    rows = parts[0].shape[0] // TILE * (2 if group == "pair" else 1)
    return pl.pallas_call(
        functools.partial(power_kernel, group),
        in_specs=in_vmem(1 + len(parts)),
        out_specs=in_vmem(1)[0],
        out_shape=jax.ShapeDtypeStruct((rows, velocities), jnp.float32),
        compiler_params=params(),
        cost_estimate=SMALL,
    )(matrix, *parts)


def across(array, hops):
    return lax.ppermute(array, "blk", hops)


def other_core(array):
    return lax.ppermute(array, "seg", [(i, i ^ 1) for i in range(UNITS)])


def layers_on(array, r):
    return lax.ppermute(array, "seg", [(i, (i + 2 * r) % UNITS) for i in range(UNITS)])


def from_layers(array):
    return jnp.stack([array] + [layers_on(array, r) for r in range(1, LAYERS)])


def grid_body(spectra, window_count, tile_owner, phases):
    chip = lax.axis_index("blk")
    me = lax.axis_index("seg")
    whole, to_x, to_y, extra_x, extra_y = whiten(spectra[0], window_count)
    from_x, from_y = across(to_x, X_SWAP), across(to_y, Y_SWAP)
    extra_x, extra_y = across(extra_x, X_EXTRA), across(extra_y, Y_EXTRA)
    weight = 1.0 / (window_count.astype(jnp.float32) * math.sqrt(FB * UNITS))
    matrix = matrix_of(phases)
    channels = whole.shape[2]

    def sums_of(kernel, rows, weight, earlier, *arrays):
        kept, sent = unit_call(kernel, rows, weight, *arrays)
        sent, *earlier = lax.optimization_barrier((sent, *earlier))
        return pair_sum(kept, other_core(sent)), earlier

    def along_layers(sums):
        return [sums[0]] + [layers_on(sums[r], r) for r in range(1, LAYERS)]

    own = along_layers(sums_of(own_kernel, channels, weight, [], whole)[0])
    own = powers_of("own", matrix, own)
    weight, own = lax.optimization_barrier((weight, own))
    pair = along_layers(sums_of(pair_kernel, channels, weight, [], whole, from_x, from_y)[0])
    sums, pair = sums_of(
        corner_kernel, channels // 2, weight, pair, from_x, from_y, extra_x, extra_y
    )
    corner = along_layers(sums)
    owner_row, *pair = lax.optimization_barrier((tile_owner[0], *pair, *sums))[: 1 + LAYERS]
    mine, mine_filled = my_slots(owner_row, UNITS)
    sources = jnp.asarray(SOURCE_ROWS)[chip, me][mine]
    pair = powers_of("pair", matrix, pair)
    turned = lax.ppermute(pair[QUAD:], ("blk", "seg"), TURNED_HOPS)
    near = jnp.concatenate([own, pair[:QUAD], turned], axis=0)
    far = other_core(near)
    last = powers_of("corner", matrix, corner)
    corners = jnp.concatenate([across(last, X_CORNER), across(last, Y_CORNER)], axis=0)
    rows = jnp.concatenate([near, far, corners, other_core(corners)], axis=0)
    every = from_layers(rows)
    response = jnp.take(every.reshape(-1, every.shape[-1]), sources, axis=0)
    response = response * mine_filled[:, None, None].astype(jnp.float32)
    return response[None, None]


def solution(mesh):
    placed = (P("seg", None, "blk", None), P("seg"), P("blk", None), P())
    fits = mesh.shape["blk"] == CHIPS and mesh.shape["seg"] == UNITS
    return jax.shard_map(
        grid_body if fits else ring_body,
        mesh=mesh,
        in_specs=placed,
        out_specs=P("blk", "seg", None, None, None),
        check_vma=False,
    )
```

```python
import functools
import math

import jax
import jax.numpy as jnp
import numpy as np
from jax import lax
from jax.experimental import pallas as pl
from jax.experimental.pallas import tpu as pltpu
from jax.sharding import PartitionSpec as P

TILE = 128
BANDS = 2
CAP = 8
FB = 512
QUAD = 4
VMEM_LIMIT = 8 * 1024 * 1024
WHITEN_LIMIT = 16 * 1024 * 1024


def from_behind(array, axis, by):
    devices = lax.axis_size(axis)
    return lax.ppermute(array, axis, [(i, (i + by) % devices) for i in range(devices)])


def prepare(segment_data, counted):
    windows = segment_data.shape[0]
    channels = segment_data.shape[1]
    spectrum = segment_data.astype(jnp.float32).reshape(windows, channels, BANDS, 2, FB)
    scaling = lax.rsqrt(jnp.mean(spectrum * spectrum, axis=(2, 3, 4)) + 1e-05)
    live_mask = (jnp.arange(windows, dtype=jnp.int32) < counted).astype(jnp.float32)
    return (
        spectrum * scaling[:, :, None, None, None] * live_mask[:, None, None, None, None]
    ).astype(jnp.bfloat16)


def correlate(resident, visiting, weight):
    windows = resident.shape[0]
    flipped = jnp.stack([-visiting[:, :, :, 1], visiting[:, :, :, 0]], axis=3)
    both_parts = jnp.stack([visiting, flipped], axis=1)
    left_side = resident.reshape(windows, QUAD, TILE, BANDS, 2 * FB)
    right_side = both_parts.reshape(windows, 2, QUAD, TILE, BANDS, 2 * FB)
    product = jnp.einsum(
        "wqibk,wpsjbk->qsbipj", left_side, right_side, preferred_element_type=jnp.float32
    )
    return (product * weight).astype(jnp.bfloat16).reshape(QUAD * QUAD, BANDS, TILE, 2 * TILE)


def phase_matrix(phases):
    norm_factor = 1.0 / math.sqrt(TILE)
    cosine = (jnp.cos(phases) * norm_factor).astype(jnp.bfloat16)
    sine_part = (jnp.sin(phases) * norm_factor).astype(jnp.bfloat16)
    upper = jnp.concatenate([cosine, sine_part], axis=2)
    lower = jnp.concatenate([-sine_part, cosine], axis=2)
    return jnp.concatenate([upper, lower], axis=1)


def disperse(stacked, phases):
    velocity_count = phases.shape[2]
    matrix = phase_matrix(phases)
    field = jnp.einsum("nbij,bjv->nbiv", stacked, matrix, preferred_element_type=jnp.float32)
    squared = field * field
    energy = squared[..., :velocity_count] + squared[..., velocity_count:]
    return jnp.mean(energy, axis=2)


def slot_table(owner_row, segments):
    count_tiles = owner_row.shape[0]
    order_ids = jnp.arange(count_tiles, dtype=jnp.int32)
    same_owner = owner_row[:, None] == owner_row[None, :]
    earlier = order_ids[None, :] < order_ids[:, None]
    rank_of = jnp.sum(jnp.where(same_owner & earlier, 1, 0), axis=1).astype(jnp.int32)
    slot_ids = owner_row * CAP + rank_of
    grid_ids = jnp.arange(segments * CAP, dtype=jnp.int32)
    matches = grid_ids[:, None] == slot_ids[None, :]
    tile_of_slot = jnp.sum(jnp.where(matches, order_ids[None, :], 0), axis=1)
    filled = jnp.any(matches, axis=1)
    return (tile_of_slot, filled)


def my_slots(owner_row, segments):
    tile_of_slot, filled = slot_table(owner_row, segments)
    my_start = lax.axis_index("seg") * CAP
    mine = lax.dynamic_slice_in_dim(tile_of_slot, my_start, CAP, 0)
    mine_filled = lax.dynamic_slice_in_dim(filled, my_start, CAP, 0)
    return mine, mine_filled


def ring_body(spectra, window_count, tile_owner, phases):
    blocks = lax.axis_size("blk")
    segments = lax.axis_size("seg")
    counted = window_count[0]
    whitened = prepare(spectra[0], counted)
    weight = 1.0 / (counted.astype(jnp.float32) * math.sqrt(FB * segments))
    pieces = [correlate(whitened, whitened, weight)]
    moving = whitened
    for shift_step in range(1, blocks // 2 + 1):
        moving = from_behind(moving, "blk", -1)
        pieces.append(correlate(whitened, moving, weight))
    all_tiles = jnp.concatenate(pieces, axis=0)
    share_rows = (
        lax.psum_scatter(all_tiles, "seg", scatter_dimension=0, tiled=True)
        .astype(jnp.float32)
        .astype(jnp.bfloat16)
    )
    share_power = disperse(share_rows, phases)
    every_power = lax.all_gather(share_power, "seg", axis=0, tiled=True)
    mine, mine_filled = my_slots(tile_owner[0], segments)
    response = jnp.take(every_power, mine, axis=0) * mine_filled[:, None, None].astype(jnp.float32)
    return response[None, None]


CHIPS = 4
UNITS = 2 * QUAD
LAYERS = UNITS // 2
X_SWAP = [(0, 1), (1, 0), (2, 3), (3, 2)]
Y_SWAP = [(0, 2), (2, 0), (1, 3), (3, 1)]
X_EXTRA = [(1, 0), (2, 3)]
Y_EXTRA = [(2, 0), (1, 3)]
X_CORNER = [(0, 1), (2, 3)]
Y_CORNER = [(3, 1), (1, 3)]
BAND_FROM_X = [1, 0, 1, 0]
BAND_FROM_Y = [0, 0, 1, 1]
OWN_ROW, PAIR_ROW, TURNED_ROW, CORE_ROWS = 0, QUAD, 2 * QUAD, 3 * QUAD
CORNER_ROW, LAYER_ROWS = 2 * CORE_ROWS, 2 * CORE_ROWS + 8
TURNED_HOPS = [
    (UNITS * chip + n, UNITS * (chip ^ (1 if n < QUAD else 2)) + n)
    for chip in range(CHIPS)
    for n in range(UNITS)
]


def source_rows():
    table = np.full((CHIPS, UNITS, 3 * QUAD * QUAD, BANDS), -1, np.int32)

    def put(block, step, p, q, band, unit, row, corner=0):
        tile = (step * QUAD + p) * QUAD + q
        for me in range(UNITS):
            layer, other = (me // 2 - unit // 2) % LAYERS, (me ^ unit) & 1
            at = CORNER_ROW + 4 * other + row if corner else CORE_ROWS * other + row
            table[block, me, tile, band] = layer * LAYER_ROWS + at

    for chip in range(CHIPS):
        for n in range(UNITS):
            for p in range(QUAD):
                put(chip, 0, p, n % QUAD, n // QUAD, n, OWN_ROW + p)
            q = n % QUAD
            band = (BAND_FROM_X[chip], BAND_FROM_Y[chip])[n // QUAD]
            for p in range(QUAD):
                if n >= QUAD:
                    put(chip, 2, p, q, band, n, PAIR_ROW + p)
                    put(chip ^ 2, 2, q, p, band, n, TURNED_ROW + p)
                elif chip % 2 == 0:
                    put(chip, 1, p, q, band, n, PAIR_ROW + p)
                else:
                    put(chip ^ 1, 1, q, p, band, n, TURNED_ROW + p)
            for i in range(2):
                m = n - QUAD
                block = 3 if chip in (1, 2) else 1
                row = 2 * ((chip, block) in Y_CORNER) + i
                if block == 3:
                    put(3, 1, 2 * (n >> 2) + i, n & 3, chip - 1, n, row, 1)
                elif m < 0:
                    put(1, 1, (2 if chip == 3 else 0) + i, n, 0, n, row, 1)
                else:
                    put(1, 1, 2 * (m & 1) + i, (m >> 1) + (2 if chip == 0 else 0), 1, n, row, 1)
    assert table.min() >= 0
    return table


SOURCE_ROWS = source_rows()


SMALL = pl.CostEstimate(flops=1000, bytes_accessed=1000, transcendentals=0)


def in_hbm(arrays):
    return [pltpu.with_memory_space_constraint(a, pltpu.HBM) for a in arrays]


def hbm_like(shape):
    return pltpu.HBM(shape, jnp.bfloat16)


def params(limit=VMEM_LIMIT):
    return pltpu.CompilerParams(vmem_limit_bytes=limit)


def whiten_kernel(counted, spectra, whole, to_x, to_y, extra_x, extra_y):
    step = pl.program_id(0)
    half = pl.num_programs(0) // 2
    windows, count, _ = spectra.shape
    chip = lax.axis_index("blk")
    rows = pl.ds(pl.multiple_of(step * count, count), count)
    for w in range(windows):
        values = spectra[w].astype(jnp.float32)
        scaling = lax.rsqrt(jnp.mean(values * values, axis=1, keepdims=True) + 1e-05)
        scaling = scaling * jnp.where(w < counted[0], 1.0, 0.0)
        out = (values * scaling).astype(jnp.bfloat16)
        width = out.shape[1] // BANDS
        for band in range(BANDS):
            whole[band, w, rows] = out[:, band * width : (band + 1) * width]
    to_x[:, rows] = whole[chip % 2, :, rows]
    to_y[:, rows] = whole[1 - chip // 2, :, rows]

    @pl.when(step < half)
    def _():
        extra_x[:, rows] = whole[chip // 2, :, rows]

    @pl.when(step >= half)
    def _():
        at = pl.ds(pl.multiple_of((step - half) * count, count), count)
        extra_y[:, at] = whole[chip // 2, :, rows]


def whiten(spectra, counted):
    windows, channels, width = spectra.shape
    band_width = width // BANDS
    rows = 2 * TILE
    full = jax.ShapeDtypeStruct((windows, channels, band_width), jnp.bfloat16)
    part = jax.ShapeDtypeStruct((windows, channels // 2, band_width), jnp.bfloat16)
    whole = jax.ShapeDtypeStruct((BANDS, windows, channels, band_width), jnp.bfloat16)
    return pl.pallas_call(
        whiten_kernel,
        grid=(channels // rows,),
        in_specs=[
            pl.BlockSpec(memory_space=pltpu.SMEM),
            pl.BlockSpec((windows, rows, width), lambda i: (0, i, 0)),
        ],
        out_specs=in_vmem(5),
        out_shape=[whole, full, full, part, part],
        compiler_params=params(WHITEN_LIMIT),
        cost_estimate=SMALL,
    )(counted, *in_hbm([spectra]))


def product(left, right, weight):
    total = None
    for rows, columns in zip(left, right):
        width = columns.shape[1] // 2
        turned = jnp.concatenate([-columns[:, width:], columns[:, :width]], axis=1)
        both = jnp.concatenate([columns, turned], axis=0)
        part = lax.dot_general(
            rows, both, (((1,), (1,)), ((), ())), preferred_element_type=jnp.float32
        )
        total = part if total is None else total + part
    return (total * weight).astype(jnp.bfloat16)


def tile_rows(tile):
    return pl.ds(pl.multiple_of(tile * TILE, TILE), TILE)


def each_unit(out):
    core = lax.axis_index("seg") % 2
    for other, ref in enumerate(out):
        for layer in range(LAYERS):
            yield layer, (1 - core if other else core), ref.at[layer]


def own_kernel(weight, whole, *out):
    for layer, core, ref in each_unit(out):
        band, q = layer // 2, 2 * (layer % 2) + core
        windows = range(whole.shape[1])
        ref[...] = product(
            [whole[band, w] for w in windows],
            [whole[band, w, tile_rows(q)] for w in windows],
            weight[0],
        )


def pair_kernel(weight, whole, from_x, from_y, *out):
    chip = lax.axis_index("blk")
    bands = (1 - chip % 2, chip // 2)
    for layer, core, ref in each_unit(out):
        along = layer // 2
        arrived, q = (from_x, from_y)[along], 2 * (layer % 2) + core
        windows = range(whole.shape[1])
        ref[...] = product(
            [whole[bands[along], w] for w in windows],
            [arrived[w, tile_rows(q)] for w in windows],
            weight[0],
        )


def corner_kernel(weight, from_x, from_y, extra_x, extra_y, *out):
    chip = lax.axis_index("blk")
    windows = range(from_x.shape[0])
    half = from_x.shape[1] // 2

    def multiply(left, left_half, right, tile, ref):
        rows = pl.ds(pl.multiple_of(left_half * half, half), half)
        ref[...] = product(
            [left[w, rows] for w in windows], [right[w, tile_rows(tile)] for w in windows], weight[0]
        )

    def split(one, two, extra_one, extra_two):
        for layer, core, ref in each_unit(out):
            if layer < LAYERS // 2:
                multiply(extra_one, 0, two, 2 * layer + core, ref)
            else:
                multiply(one, core, extra_two, layer - LAYERS // 2, ref)

    def joined(one, two):
        for layer, core, ref in each_unit(out):
            multiply(one, layer // 2, two, 2 * (layer % 2) + core, ref)

    pl.when(chip == 0)(lambda: split(from_x, from_y, extra_x, extra_y))
    pl.when(chip == 1)(lambda: joined(from_y, from_x))
    pl.when(chip == 2)(lambda: joined(from_x, from_y))
    pl.when(chip == 3)(lambda: split(from_y, from_x, extra_y, extra_x))


def in_vmem(count):
    return [pl.BlockSpec(memory_space=pltpu.VMEM)] * count


def unit_call(kernel, rows, weight, *arrays):
    out = jax.ShapeDtypeStruct((LAYERS, rows, 2 * TILE), jnp.bfloat16)
    return pl.pallas_call(
        kernel,
        in_specs=[pl.BlockSpec(memory_space=pltpu.SMEM)] + in_vmem(len(arrays)),
        out_specs=in_vmem(2),
        out_shape=[out, out],
        compiler_params=params(),
        cost_estimate=SMALL,
    )(weight, *arrays)


def pair_sum_kernel(kept, got, *outs):
    layer = lax.axis_index("seg") // 2
    for r, out in enumerate(outs):
        at = lax.rem(layer + r, LAYERS)
        out[...] = (kept[at].astype(jnp.float32) + got[at].astype(jnp.float32)).astype(jnp.bfloat16)


def pair_sum(kept, got):
    shape = jax.ShapeDtypeStruct(kept.shape[1:], jnp.bfloat16)
    return pl.pallas_call(
        pair_sum_kernel,
        in_specs=in_vmem(2),
        out_specs=in_vmem(LAYERS),
        out_shape=[shape] * LAYERS,
        compiler_params=params(),
        cost_estimate=SMALL,
    )(kept, got)


def layer_sum(parts):
    total = parts[0][...].astype(jnp.float32)
    for part in parts[1:]:
        total = total + part[...].astype(jnp.float32)
    return total.astype(jnp.bfloat16)


def tile_powers(rows, table):
    velocities = table.shape[1] // 2
    field = lax.dot_general(
        rows, table, (((1,), (0,)), ((), ())), preferred_element_type=jnp.float32
    )
    squared = field * field
    energy = squared[:, :velocities] + squared[:, velocities:]
    return [
        jnp.sum(energy[t : t + TILE], axis=0, keepdims=True) * (1.0 / TILE)
        for t in range(0, rows.shape[0], TILE)
    ]


def transposed(stacked):
    rounded = stacked.astype(jnp.float32)
    turned = []
    for t in range(0, stacked.shape[0], TILE):
        tile = rounded[t : t + TILE]
        turned.append(jnp.concatenate([tile[:, :TILE].T, -tile[:, TILE:].T], axis=1))
    return jnp.concatenate(turned, axis=0).astype(jnp.bfloat16)


def matrix_kernel(phases, matrix):
    rows, velocities = phases.shape[1:]
    norm_factor = 1.0 / math.sqrt(TILE)
    for band in range(phases.shape[0]):
        cosine = (jnp.cos(phases[band]) * norm_factor).astype(jnp.bfloat16)
        sine_part = (jnp.sin(phases[band]) * norm_factor).astype(jnp.bfloat16)
        matrix[band, :rows, :velocities] = cosine
        matrix[band, :rows, velocities:] = sine_part
        matrix[band, rows:, :velocities] = -sine_part
        matrix[band, rows:, velocities:] = cosine


def matrix_of(phases):
    bands, rows, velocities = phases.shape
    return pl.pallas_call(
        matrix_kernel,
        in_specs=in_vmem(1),
        out_specs=in_vmem(1)[0],
        out_shape=jax.ShapeDtypeStruct((bands, 2 * rows, 2 * velocities), jnp.bfloat16),
        compiler_params=params(),
        cost_estimate=SMALL,
    )(phases)


def power_kernel(group, matrix, *refs):
    out = refs[-1]
    chip, me = lax.axis_index("blk"), lax.axis_index("seg")
    if group == "own":
        band = me // QUAD
    elif group == "pair":
        band = jnp.where(me < QUAD, 1 - chip % 2, chip // 2)
    else:
        band = jnp.where((chip == 1) | (chip == 2), chip - 1, me // QUAD)
    stacked = layer_sum(refs[:-1])
    table = matrix[band]
    found = tile_powers(stacked, table)
    if group == "pair":
        found += tile_powers(transposed(stacked), table)
    for t, row in enumerate(found):
        out[t : t + 1, :] = row


def powers_of(group, matrix, parts):
    velocities = matrix.shape[2] // 2
    rows = parts[0].shape[0] // TILE * (2 if group == "pair" else 1)
    return pl.pallas_call(
        functools.partial(power_kernel, group),
        in_specs=in_vmem(1 + len(parts)),
        out_specs=in_vmem(1)[0],
        out_shape=jax.ShapeDtypeStruct((rows, velocities), jnp.float32),
        compiler_params=params(),
        cost_estimate=SMALL,
    )(matrix, *parts)


def across(array, hops):
    return lax.ppermute(array, "blk", hops)


def other_core(array):
    return lax.ppermute(array, "seg", [(i, i ^ 1) for i in range(UNITS)])


def layers_on(array, r):
    return lax.ppermute(array, "seg", [(i, (i + 2 * r) % UNITS) for i in range(UNITS)])


def from_layers(array):
    return jnp.stack([array] + [layers_on(array, r) for r in range(1, LAYERS)])


def grid_body(spectra, window_count, tile_owner, phases):
    chip = lax.axis_index("blk")
    me = lax.axis_index("seg")
    whole, to_x, to_y, extra_x, extra_y = whiten(spectra[0], window_count)
    from_x, from_y = across(to_x, X_SWAP), across(to_y, Y_SWAP)
    extra_x, extra_y = across(extra_x, X_EXTRA), across(extra_y, Y_EXTRA)
    weight = 1.0 / (window_count.astype(jnp.float32) * math.sqrt(FB * UNITS))
    matrix = matrix_of(phases)
    channels = whole.shape[2]

    def sums_of(kernel, rows, weight, earlier, *arrays):
        kept, sent = unit_call(kernel, rows, weight, *arrays)
        sent, *earlier = lax.optimization_barrier((sent, *earlier))
        return pair_sum(kept, other_core(sent)), earlier

    def along_layers(sums):
        return [sums[0]] + [layers_on(sums[r], r) for r in range(1, LAYERS)]

    own = along_layers(sums_of(own_kernel, channels, weight, [], whole)[0])
    own = powers_of("own", matrix, own)
    weight, own = lax.optimization_barrier((weight, own))
    pair = along_layers(sums_of(pair_kernel, channels, weight, [], whole, from_x, from_y)[0])
    sums, pair = sums_of(
        corner_kernel, channels // 2, weight, pair, from_x, from_y, extra_x, extra_y
    )
    corner = along_layers(sums)
    owner_row, *pair = lax.optimization_barrier((tile_owner[0], *pair, *sums))[: 1 + LAYERS]
    mine, mine_filled = my_slots(owner_row, UNITS)
    sources = jnp.asarray(SOURCE_ROWS)[chip, me][mine]
    pair = powers_of("pair", matrix, pair)
    turned = lax.ppermute(pair[QUAD:], ("blk", "seg"), TURNED_HOPS)
    near = jnp.concatenate([own, pair[:QUAD], turned], axis=0)
    far = other_core(near)
    last = powers_of("corner", matrix, corner)
    corners = jnp.concatenate([across(last, X_CORNER), across(last, Y_CORNER)], axis=0)
    rows = jnp.concatenate([near, far, corners, other_core(corners)], axis=0)
    every = from_layers(rows)
    response = jnp.take(every.reshape(-1, every.shape[-1]), sources, axis=0)
    response = response * mine_filled[:, None, None].astype(jnp.float32)
    return response[None, None]


def solution(mesh):
    placed = (P("seg", None, "blk", None), P("seg"), P("blk", None), P())
    fits = mesh.shape["blk"] == CHIPS and mesh.shape["seg"] == UNITS
    return jax.shard_map(
        grid_body if fits else ring_body,
        mesh=mesh,
        in_specs=placed,
        out_specs=P("blk", "seg", None, None, None),
        check_vma=False,
    )
```

```python
import functools
import math

import jax
import jax.numpy as jnp
import numpy as np
from jax import lax
from jax.experimental import pallas as pl
from jax.experimental.pallas import tpu as pltpu
from jax.sharding import PartitionSpec as P

TILE = 128
BANDS = 2
CAP = 8
FB = 512
QUAD = 4
VMEM_LIMIT = 8 * 1024 * 1024
WHITEN_LIMIT = 16 * 1024 * 1024


def from_behind(array, axis, by):
    devices = lax.axis_size(axis)
    return lax.ppermute(array, axis, [(i, (i + by) % devices) for i in range(devices)])


def prepare(segment_data, counted):
    windows = segment_data.shape[0]
    channels = segment_data.shape[1]
    spectrum = segment_data.astype(jnp.float32).reshape(windows, channels, BANDS, 2, FB)
    scaling = lax.rsqrt(jnp.mean(spectrum * spectrum, axis=(2, 3, 4)) + 1e-05)
    live_mask = (jnp.arange(windows, dtype=jnp.int32) < counted).astype(jnp.float32)
    return (
        spectrum * scaling[:, :, None, None, None] * live_mask[:, None, None, None, None]
    ).astype(jnp.bfloat16)


def correlate(resident, visiting, weight):
    windows = resident.shape[0]
    flipped = jnp.stack([-visiting[:, :, :, 1], visiting[:, :, :, 0]], axis=3)
    both_parts = jnp.stack([visiting, flipped], axis=1)
    left_side = resident.reshape(windows, QUAD, TILE, BANDS, 2 * FB)
    right_side = both_parts.reshape(windows, 2, QUAD, TILE, BANDS, 2 * FB)
    product = jnp.einsum(
        "wqibk,wpsjbk->qsbipj", left_side, right_side, preferred_element_type=jnp.float32
    )
    return (product * weight).astype(jnp.bfloat16).reshape(QUAD * QUAD, BANDS, TILE, 2 * TILE)


def phase_matrix(phases):
    norm_factor = 1.0 / math.sqrt(TILE)
    cosine = (jnp.cos(phases) * norm_factor).astype(jnp.bfloat16)
    sine_part = (jnp.sin(phases) * norm_factor).astype(jnp.bfloat16)
    upper = jnp.concatenate([cosine, sine_part], axis=2)
    lower = jnp.concatenate([-sine_part, cosine], axis=2)
    return jnp.concatenate([upper, lower], axis=1)


def disperse(stacked, phases):
    velocity_count = phases.shape[2]
    matrix = phase_matrix(phases)
    field = jnp.einsum("nbij,bjv->nbiv", stacked, matrix, preferred_element_type=jnp.float32)
    squared = field * field
    energy = squared[..., :velocity_count] + squared[..., velocity_count:]
    return jnp.mean(energy, axis=2)


def slot_table(owner_row, segments):
    count_tiles = owner_row.shape[0]
    order_ids = jnp.arange(count_tiles, dtype=jnp.int32)
    same_owner = owner_row[:, None] == owner_row[None, :]
    earlier = order_ids[None, :] < order_ids[:, None]
    rank_of = jnp.sum(jnp.where(same_owner & earlier, 1, 0), axis=1).astype(jnp.int32)
    slot_ids = owner_row * CAP + rank_of
    grid_ids = jnp.arange(segments * CAP, dtype=jnp.int32)
    matches = grid_ids[:, None] == slot_ids[None, :]
    tile_of_slot = jnp.sum(jnp.where(matches, order_ids[None, :], 0), axis=1)
    filled = jnp.any(matches, axis=1)
    return (tile_of_slot, filled)


def my_slots(owner_row, segments):
    tile_of_slot, filled = slot_table(owner_row, segments)
    my_start = lax.axis_index("seg") * CAP
    mine = lax.dynamic_slice_in_dim(tile_of_slot, my_start, CAP, 0)
    mine_filled = lax.dynamic_slice_in_dim(filled, my_start, CAP, 0)
    return mine, mine_filled


def ring_body(spectra, window_count, tile_owner, phases):
    blocks = lax.axis_size("blk")
    segments = lax.axis_size("seg")
    counted = window_count[0]
    whitened = prepare(spectra[0], counted)
    weight = 1.0 / (counted.astype(jnp.float32) * math.sqrt(FB * segments))
    pieces = [correlate(whitened, whitened, weight)]
    moving = whitened
    for shift_step in range(1, blocks // 2 + 1):
        moving = from_behind(moving, "blk", -1)
        pieces.append(correlate(whitened, moving, weight))
    all_tiles = jnp.concatenate(pieces, axis=0)
    share_rows = (
        lax.psum_scatter(all_tiles, "seg", scatter_dimension=0, tiled=True)
        .astype(jnp.float32)
        .astype(jnp.bfloat16)
    )
    share_power = disperse(share_rows, phases)
    every_power = lax.all_gather(share_power, "seg", axis=0, tiled=True)
    mine, mine_filled = my_slots(tile_owner[0], segments)
    response = jnp.take(every_power, mine, axis=0) * mine_filled[:, None, None].astype(jnp.float32)
    return response[None, None]


CHIPS = 4
UNITS = 2 * QUAD
LAYERS = UNITS // 2
X_SWAP = [(0, 1), (1, 0), (2, 3), (3, 2)]
Y_SWAP = [(0, 2), (2, 0), (1, 3), (3, 1)]
X_EXTRA = [(1, 0), (2, 3)]
Y_EXTRA = [(2, 0), (1, 3)]
X_CORNER = [(0, 1), (2, 3)]
Y_CORNER = [(3, 1), (1, 3)]
BAND_FROM_X = [1, 0, 1, 0]
BAND_FROM_Y = [0, 0, 1, 1]
OWN_ROW, PAIR_ROW, TURNED_ROW, CORE_ROWS = 0, QUAD, 2 * QUAD, 3 * QUAD
CORNER_ROW, LAYER_ROWS = 2 * CORE_ROWS, 2 * CORE_ROWS + 8
TURNED_HOPS = [
    (UNITS * chip + n, UNITS * (chip ^ (1 if n < QUAD else 2)) + n)
    for chip in range(CHIPS)
    for n in range(UNITS)
]


def source_rows():
    table = np.full((CHIPS, UNITS, 3 * QUAD * QUAD, BANDS), -1, np.int32)

    def put(block, step, p, q, band, unit, row, corner=0):
        tile = (step * QUAD + p) * QUAD + q
        for me in range(UNITS):
            layer, other = (me // 2 - unit // 2) % LAYERS, (me ^ unit) & 1
            at = CORNER_ROW + 4 * other + row if corner else CORE_ROWS * other + row
            table[block, me, tile, band] = layer * LAYER_ROWS + at

    for chip in range(CHIPS):
        for n in range(UNITS):
            for p in range(QUAD):
                put(chip, 0, p, n % QUAD, n // QUAD, n, OWN_ROW + p)
            band = (BAND_FROM_X[chip], BAND_FROM_Y[chip])[n // QUAD]
            for i in range(4):
                p, q = 2 * (n % 2) + i % 2, 2 * (i // 2) + n // 2 % 2
                if n >= QUAD:
                    put(chip, 2, p, q, band, n, PAIR_ROW + i)
                    put(chip ^ 2, 2, q, p, band, n, TURNED_ROW + i)
                elif chip % 2 == 0:
                    put(chip, 1, p, q, band, n, PAIR_ROW + i)
                else:
                    put(chip ^ 1, 1, q, p, band, n, TURNED_ROW + i)
            for i in range(2):
                m = n - QUAD
                block = 3 if chip in (1, 2) else 1
                row = 2 * ((chip, block) in Y_CORNER) + i
                if block == 3:
                    put(3, 1, 2 * (n >> 2) + i, n & 3, chip - 1, n, row, 1)
                elif m < 0:
                    put(1, 1, (2 if chip == 3 else 0) + i, n, 0, n, row, 1)
                else:
                    put(1, 1, 2 * (m & 1) + i, (m >> 1) + (2 if chip == 0 else 0), 1, n, row, 1)
    assert table.min() >= 0
    return table


SOURCE_ROWS = source_rows()


SMALL = pl.CostEstimate(flops=1000, bytes_accessed=1000, transcendentals=0)


def in_hbm(arrays):
    return [pltpu.with_memory_space_constraint(a, pltpu.HBM) for a in arrays]


def hbm_like(shape):
    return pltpu.HBM(shape, jnp.bfloat16)


def params(limit=VMEM_LIMIT):
    return pltpu.CompilerParams(vmem_limit_bytes=limit)


def whiten_kernel(counted, spectra, whole, x0, y0, x1, y1, extra_x, extra_y):
    step = pl.program_id(0)
    half = pl.num_programs(0) // 2
    windows, count, _ = spectra.shape
    chip = lax.axis_index("blk")
    rows = pl.ds(pl.multiple_of(step * count, count), count)
    for w in range(windows):
        values = spectra[w].astype(jnp.float32)
        scaling = lax.rsqrt(jnp.mean(values * values, axis=1, keepdims=True) + 1e-05)
        scaling = scaling * jnp.where(w < counted[0], 1.0, 0.0)
        out = (values * scaling).astype(jnp.bfloat16)
        width = out.shape[1] // BANDS
        for band in range(BANDS):
            whole[band, w, rows] = out[:, band * width : (band + 1) * width]

    def send(to_x, to_y, extra, first):
        at = pl.ds(pl.multiple_of((step - first) * count, count), count)
        to_x[:, at] = whole[chip % 2, :, rows]
        to_y[:, at] = whole[1 - chip // 2, :, rows]
        extra[:, at] = whole[chip // 2, :, rows]

    pl.when(step < half)(lambda: send(x0, y0, extra_x, 0))
    pl.when(step >= half)(lambda: send(x1, y1, extra_y, half))


def whiten(spectra, counted):
    windows, channels, width = spectra.shape
    band_width = width // BANDS
    rows = 2 * TILE
    part = jax.ShapeDtypeStruct((windows, channels // 2, band_width), jnp.bfloat16)
    whole = jax.ShapeDtypeStruct((BANDS, windows, channels, band_width), jnp.bfloat16)
    return pl.pallas_call(
        whiten_kernel,
        grid=(channels // rows,),
        in_specs=[
            pl.BlockSpec(memory_space=pltpu.SMEM),
            pl.BlockSpec((windows, rows, width), lambda i: (0, i, 0)),
        ],
        out_specs=in_vmem(7),
        out_shape=[whole] + [part] * 6,
        compiler_params=params(WHITEN_LIMIT),
        cost_estimate=SMALL,
    )(counted, *in_hbm([spectra]))


def product(left, right, weight):
    total = None
    for rows, columns in zip(left, right):
        width = columns.shape[1] // 2
        turned = jnp.concatenate([-columns[:, width:], columns[:, :width]], axis=1)
        both = jnp.concatenate([columns, turned], axis=0)
        part = lax.dot_general(
            rows, both, (((1,), (1,)), ((), ())), preferred_element_type=jnp.float32
        )
        total = part if total is None else total + part
    return (total * weight).astype(jnp.bfloat16)


def tile_rows(tile):
    return pl.ds(pl.multiple_of(tile * TILE, TILE), TILE)


def each_unit(out):
    core = lax.axis_index("seg") % 2
    for other, ref in enumerate(out):
        for layer in range(LAYERS):
            yield layer, (1 - core if other else core), ref.at[layer]


def own_kernel(weight, whole, *out):
    for layer, core, ref in each_unit(out):
        band, q = layer // 2, 2 * (layer % 2) + core
        windows = range(whole.shape[1])
        ref[...] = product(
            [whole[band, w] for w in windows],
            [whole[band, w, tile_rows(q)] for w in windows],
            weight[0],
        )


def pair_kernel(weight, whole, from_x, from_y, *out):
    chip = lax.axis_index("blk")
    bands = (1 - chip % 2, chip // 2)
    half = from_x.shape[1]
    for layer, core, ref in each_unit(out):
        along = layer // 2
        arrived, q = (from_x, from_y)[along], layer % 2
        rows = pl.ds(pl.multiple_of(core * half, half), half)
        windows = range(whole.shape[1])
        ref[...] = product(
            [whole[bands[along], w, rows] for w in windows],
            [arrived[w, tile_rows(q)] for w in windows],
            weight[0],
        )


def corner_kernel(weight, x0, x1, y0, y1, extra_x, extra_y, *out):
    chip = lax.axis_index("blk")
    windows = range(x0.shape[0])

    def multiply(left, right, tile, ref):
        ref[...] = product(left, [right[w, tile_rows(tile)] for w in windows], weight[0])

    def split(one, two, extra_one, extra_two):
        for layer, core, ref in each_unit(out):
            if layer < LAYERS // 2:
                multiply([extra_one[w] for w in windows], two[layer], core, ref)
            else:
                left = [jnp.where(core == 0, one[0][w], one[1][w]) for w in windows]
                multiply(left, extra_two, layer - LAYERS // 2, ref)

    def joined(one, two):
        for layer, core, ref in each_unit(out):
            multiply([one[layer // 2][w] for w in windows], two[layer % 2], core, ref)

    x, y = (x0, x1), (y0, y1)
    pl.when(chip == 0)(lambda: split(x, y, extra_x, extra_y))
    pl.when(chip == 1)(lambda: joined(y, x))
    pl.when(chip == 2)(lambda: joined(x, y))
    pl.when(chip == 3)(lambda: split(y, x, extra_y, extra_x))


def in_vmem(count):
    return [pl.BlockSpec(memory_space=pltpu.VMEM)] * count


def unit_call(kernel, rows, weight, *arrays):
    out = jax.ShapeDtypeStruct((LAYERS, rows, 2 * TILE), jnp.bfloat16)
    return pl.pallas_call(
        kernel,
        in_specs=[pl.BlockSpec(memory_space=pltpu.SMEM)] + in_vmem(len(arrays)),
        out_specs=in_vmem(2),
        out_shape=[out, out],
        compiler_params=params(),
        cost_estimate=SMALL,
    )(weight, *arrays)


def pair_sum_kernel(kept, got, *outs):
    layer = lax.axis_index("seg") // 2
    for r, out in enumerate(outs):
        at = lax.rem(layer + r, LAYERS)
        out[...] = (kept[at].astype(jnp.float32) + got[at].astype(jnp.float32)).astype(jnp.bfloat16)


def pair_sum(kept, got):
    shape = jax.ShapeDtypeStruct(kept.shape[1:], jnp.bfloat16)
    return pl.pallas_call(
        pair_sum_kernel,
        in_specs=in_vmem(2),
        out_specs=in_vmem(LAYERS),
        out_shape=[shape] * LAYERS,
        compiler_params=params(),
        cost_estimate=SMALL,
    )(kept, got)


def layer_sum(parts):
    total = parts[0][...].astype(jnp.float32)
    for part in parts[1:]:
        total = total + part[...].astype(jnp.float32)
    return total.astype(jnp.bfloat16)


def tile_powers(rows, table):
    velocities = table.shape[1] // 2
    field = lax.dot_general(
        rows, table, (((1,), (0,)), ((), ())), preferred_element_type=jnp.float32
    )
    squared = field * field
    energy = squared[:, :velocities] + squared[:, velocities:]
    return [
        jnp.sum(energy[t : t + TILE], axis=0, keepdims=True) * (1.0 / TILE)
        for t in range(0, rows.shape[0], TILE)
    ]


def transposed(stacked):
    rounded = stacked.astype(jnp.float32)
    turned = []
    for t in range(0, stacked.shape[0], TILE):
        tile = rounded[t : t + TILE]
        turned.append(jnp.concatenate([tile[:, :TILE].T, -tile[:, TILE:].T], axis=1))
    return jnp.concatenate(turned, axis=0).astype(jnp.bfloat16)


def matrix_kernel(phases, matrix):
    rows, velocities = phases.shape[1:]
    norm_factor = 1.0 / math.sqrt(TILE)
    for band in range(phases.shape[0]):
        cosine = (jnp.cos(phases[band]) * norm_factor).astype(jnp.bfloat16)
        sine_part = (jnp.sin(phases[band]) * norm_factor).astype(jnp.bfloat16)
        matrix[band, :rows, :velocities] = cosine
        matrix[band, :rows, velocities:] = sine_part
        matrix[band, rows:, :velocities] = -sine_part
        matrix[band, rows:, velocities:] = cosine


def matrix_of(phases):
    bands, rows, velocities = phases.shape
    return pl.pallas_call(
        matrix_kernel,
        in_specs=in_vmem(1),
        out_specs=in_vmem(1)[0],
        out_shape=jax.ShapeDtypeStruct((bands, 2 * rows, 2 * velocities), jnp.bfloat16),
        compiler_params=params(),
        cost_estimate=SMALL,
    )(phases)


def power_kernel(group, matrix, *refs):
    out = refs[-1]
    chip, me = lax.axis_index("blk"), lax.axis_index("seg")
    if group == "own":
        band = me // QUAD
    elif group == "pair":
        band = jnp.where(me < QUAD, 1 - chip % 2, chip // 2)
    else:
        band = jnp.where((chip == 1) | (chip == 2), chip - 1, me // QUAD)
    stacked = layer_sum(refs[:-1])
    table = matrix[band]
    found = tile_powers(stacked, table)
    if group == "pair":
        found += tile_powers(transposed(stacked), table)
    for t, row in enumerate(found):
        out[t : t + 1, :] = row


def powers_of(group, matrix, parts):
    velocities = matrix.shape[2] // 2
    rows = parts[0].shape[0] // TILE * (2 if group == "pair" else 1)
    return pl.pallas_call(
        functools.partial(power_kernel, group),
        in_specs=in_vmem(1 + len(parts)),
        out_specs=in_vmem(1)[0],
        out_shape=jax.ShapeDtypeStruct((rows, velocities), jnp.float32),
        compiler_params=params(),
        cost_estimate=SMALL,
    )(matrix, *parts)


def across(array, hops):
    return lax.ppermute(array, "blk", hops)


def other_core(array):
    return lax.ppermute(array, "seg", [(i, i ^ 1) for i in range(UNITS)])


def layers_on(array, r):
    return lax.ppermute(array, "seg", [(i, (i + 2 * r) % UNITS) for i in range(UNITS)])


def from_layers(array):
    return jnp.stack([array] + [layers_on(array, r) for r in range(1, LAYERS)])


def grid_body(spectra, window_count, tile_owner, phases):
    chip = lax.axis_index("blk")
    me = lax.axis_index("seg")
    whole, x0, y0, x1, y1, extra_x, extra_y = whiten(spectra[0], window_count)
    x0, y0 = across(x0, X_SWAP), across(y0, Y_SWAP)
    x1, y1 = across(x1, X_SWAP), across(y1, Y_SWAP)
    extra_x, extra_y = across(extra_x, X_EXTRA), across(extra_y, Y_EXTRA)

    weight = 1.0 / (window_count.astype(jnp.float32) * math.sqrt(FB * UNITS))
    matrix = matrix_of(phases)
    channels = whole.shape[2]

    def sums_of(kernel, rows, weight, earlier, *arrays):
        kept, sent = unit_call(kernel, rows, weight, *arrays)
        sent, *earlier = lax.optimization_barrier((sent, *earlier))
        return pair_sum(kept, other_core(sent)), earlier

    def along_layers(sums):
        return [sums[0]] + [layers_on(sums[r], r) for r in range(1, LAYERS)]

    own = along_layers(sums_of(own_kernel, channels, weight, [], whole)[0])
    own = powers_of("own", matrix, own)
    half = channels // 2
    pair0, (own,) = sums_of(pair_kernel, half, weight, [own], whole, x0, y0)
    pair0 = along_layers(pair0)
    pair0 = powers_of("pair", matrix, pair0)
    weight, pair0 = lax.optimization_barrier((weight, pair0))
    pair1 = along_layers(sums_of(pair_kernel, half, weight, [], whole, x1, y1)[0])
    sums, pair1 = sums_of(corner_kernel, half, weight, pair1, x0, x1, y0, y1, extra_x, extra_y)
    corner = along_layers(sums)
    owner_row, *pair1 = lax.optimization_barrier((tile_owner[0], *pair1, *sums))[: 1 + LAYERS]
    mine, mine_filled = my_slots(owner_row, UNITS)
    sources = jnp.asarray(SOURCE_ROWS)[chip, me][mine]
    pair1 = powers_of("pair", matrix, pair1)
    tiles = pair0.shape[0] // 2
    turned = jnp.concatenate([pair0[tiles:], pair1[tiles:]], axis=0)
    turned = lax.ppermute(turned, ("blk", "seg"), TURNED_HOPS)
    near = jnp.concatenate([own, pair0[:tiles], pair1[:tiles], turned], axis=0)
    far = other_core(near)
    last = powers_of("corner", matrix, corner)
    corners = jnp.concatenate([across(last, X_CORNER), across(last, Y_CORNER)], axis=0)
    rows = jnp.concatenate([near, far, corners, other_core(corners)], axis=0)
    every = from_layers(rows)
    response = jnp.take(every.reshape(-1, every.shape[-1]), sources, axis=0)
    response = response * mine_filled[:, None, None].astype(jnp.float32)
    return response[None, None]


def solution(mesh):
    placed = (P("seg", None, "blk", None), P("seg"), P("blk", None), P())
    fits = mesh.shape["blk"] == CHIPS and mesh.shape["seg"] == UNITS
    return jax.shard_map(
        grid_body if fits else ring_body,
        mesh=mesh,
        in_specs=placed,
        out_specs=P("blk", "seg", None, None, None),
        check_vma=False,
    )
```

```python
import functools
import math

import jax
import jax.numpy as jnp
import numpy as np
from jax import lax
from jax.experimental import pallas as pl
from jax.experimental.pallas import tpu as pltpu
from jax.sharding import PartitionSpec as P

TILE = 128
BANDS = 2
CAP = 8
FB = 512
QUAD = 4
VMEM_LIMIT = 8 * 1024 * 1024
WHITEN_LIMIT = 16 * 1024 * 1024


def from_behind(array, axis, by):
    devices = lax.axis_size(axis)
    return lax.ppermute(array, axis, [(i, (i + by) % devices) for i in range(devices)])


def prepare(segment_data, counted):
    windows = segment_data.shape[0]
    channels = segment_data.shape[1]
    spectrum = segment_data.astype(jnp.float32).reshape(windows, channels, BANDS, 2, FB)
    scaling = lax.rsqrt(jnp.mean(spectrum * spectrum, axis=(2, 3, 4)) + 1e-05)
    live_mask = (jnp.arange(windows, dtype=jnp.int32) < counted).astype(jnp.float32)
    return (
        spectrum * scaling[:, :, None, None, None] * live_mask[:, None, None, None, None]
    ).astype(jnp.bfloat16)


def correlate(resident, visiting, weight):
    windows = resident.shape[0]
    flipped = jnp.stack([-visiting[:, :, :, 1], visiting[:, :, :, 0]], axis=3)
    both_parts = jnp.stack([visiting, flipped], axis=1)
    left_side = resident.reshape(windows, QUAD, TILE, BANDS, 2 * FB)
    right_side = both_parts.reshape(windows, 2, QUAD, TILE, BANDS, 2 * FB)
    product = jnp.einsum(
        "wqibk,wpsjbk->qsbipj", left_side, right_side, preferred_element_type=jnp.float32
    )
    return (product * weight).astype(jnp.bfloat16).reshape(QUAD * QUAD, BANDS, TILE, 2 * TILE)


def phase_matrix(phases):
    norm_factor = 1.0 / math.sqrt(TILE)
    cosine = (jnp.cos(phases) * norm_factor).astype(jnp.bfloat16)
    sine_part = (jnp.sin(phases) * norm_factor).astype(jnp.bfloat16)
    upper = jnp.concatenate([cosine, sine_part], axis=2)
    lower = jnp.concatenate([-sine_part, cosine], axis=2)
    return jnp.concatenate([upper, lower], axis=1)


def disperse(stacked, phases):
    velocity_count = phases.shape[2]
    matrix = phase_matrix(phases)
    field = jnp.einsum("nbij,bjv->nbiv", stacked, matrix, preferred_element_type=jnp.float32)
    squared = field * field
    energy = squared[..., :velocity_count] + squared[..., velocity_count:]
    return jnp.mean(energy, axis=2)


def slot_table(owner_row, segments):
    count_tiles = owner_row.shape[0]
    order_ids = jnp.arange(count_tiles, dtype=jnp.int32)
    same_owner = owner_row[:, None] == owner_row[None, :]
    earlier = order_ids[None, :] < order_ids[:, None]
    rank_of = jnp.sum(jnp.where(same_owner & earlier, 1, 0), axis=1).astype(jnp.int32)
    slot_ids = owner_row * CAP + rank_of
    grid_ids = jnp.arange(segments * CAP, dtype=jnp.int32)
    matches = grid_ids[:, None] == slot_ids[None, :]
    tile_of_slot = jnp.sum(jnp.where(matches, order_ids[None, :], 0), axis=1)
    filled = jnp.any(matches, axis=1)
    return (tile_of_slot, filled)


def my_slots(owner_row, segments):
    tile_of_slot, filled = slot_table(owner_row, segments)
    my_start = lax.axis_index("seg") * CAP
    mine = lax.dynamic_slice_in_dim(tile_of_slot, my_start, CAP, 0)
    mine_filled = lax.dynamic_slice_in_dim(filled, my_start, CAP, 0)
    return mine, mine_filled


def ring_body(spectra, window_count, tile_owner, phases):
    blocks = lax.axis_size("blk")
    segments = lax.axis_size("seg")
    counted = window_count[0]
    whitened = prepare(spectra[0], counted)
    weight = 1.0 / (counted.astype(jnp.float32) * math.sqrt(FB * segments))
    pieces = [correlate(whitened, whitened, weight)]
    moving = whitened
    for shift_step in range(1, blocks // 2 + 1):
        moving = from_behind(moving, "blk", -1)
        pieces.append(correlate(whitened, moving, weight))
    all_tiles = jnp.concatenate(pieces, axis=0)
    share_rows = (
        lax.psum_scatter(all_tiles, "seg", scatter_dimension=0, tiled=True)
        .astype(jnp.float32)
        .astype(jnp.bfloat16)
    )
    share_power = disperse(share_rows, phases)
    every_power = lax.all_gather(share_power, "seg", axis=0, tiled=True)
    mine, mine_filled = my_slots(tile_owner[0], segments)
    response = jnp.take(every_power, mine, axis=0) * mine_filled[:, None, None].astype(jnp.float32)
    return response[None, None]


CHIPS = 4
UNITS = 2 * QUAD
LAYERS = UNITS // 2
X_SWAP = [(0, 1), (1, 0), (2, 3), (3, 2)]
Y_SWAP = [(0, 2), (2, 0), (1, 3), (3, 1)]
X_EXTRA = [(1, 0), (2, 3)]
Y_EXTRA = [(2, 0), (1, 3)]
X_CORNER = [(0, 1), (2, 3)]
Y_CORNER = [(3, 1), (1, 3)]
BAND_FROM_X = [1, 0, 1, 0]
BAND_FROM_Y = [0, 0, 1, 1]
OWN_ROW, PAIR_ROW, TURNED_ROW, CORE_ROWS = 0, QUAD, 2 * QUAD, 3 * QUAD
CORNER_ROW, LAYER_ROWS = 2 * CORE_ROWS, 2 * CORE_ROWS + 8
TURNED_HOPS = [
    (UNITS * chip + n, UNITS * (chip ^ (1 if n < QUAD else 2)) + n)
    for chip in range(CHIPS)
    for n in range(UNITS)
]


def source_rows():
    table = np.full((CHIPS, UNITS, 3 * QUAD * QUAD, BANDS), -1, np.int32)

    def put(block, step, p, q, band, unit, row, corner=0):
        tile = (step * QUAD + p) * QUAD + q
        for me in range(UNITS):
            layer, other = (me // 2 - unit // 2) % LAYERS, (me ^ unit) & 1
            at = CORNER_ROW + 4 * other + row if corner else CORE_ROWS * other + row
            table[block, me, tile, band] = layer * LAYER_ROWS + at

    for chip in range(CHIPS):
        for n in range(UNITS):
            for p in range(QUAD):
                put(chip, 0, p, n % QUAD, n // QUAD, n, OWN_ROW + p)
            band = (BAND_FROM_X[chip], BAND_FROM_Y[chip])[n // QUAD]
            for i in range(4):
                p, q = 2 * (n % 2) + i % 2, 2 * (i // 2) + n // 2 % 2
                if n >= QUAD:
                    put(chip, 2, p, q, band, n, PAIR_ROW + i)
                    put(chip ^ 2, 2, q, p, band, n, TURNED_ROW + i)
                elif chip % 2 == 0:
                    put(chip, 1, p, q, band, n, PAIR_ROW + i)
                else:
                    put(chip ^ 1, 1, q, p, band, n, TURNED_ROW + i)
            for i in range(2):
                m = n - QUAD
                block = 3 if chip in (1, 2) else 1
                row = 2 * ((chip, block) in Y_CORNER) + i
                if block == 3:
                    put(3, 1, 2 * (n >> 2) + i, n & 3, chip - 1, n, row, 1)
                elif m < 0:
                    put(1, 1, (2 if chip == 3 else 0) + i, n, 0, n, row, 1)
                else:
                    put(1, 1, 2 * (m & 1) + i, (m >> 1) + (2 if chip == 0 else 0), 1, n, row, 1)
    assert table.min() >= 0
    return table


SOURCE_ROWS = source_rows()


SMALL = pl.CostEstimate(flops=1000, bytes_accessed=1000, transcendentals=0)


def in_hbm(arrays):
    return [pltpu.with_memory_space_constraint(a, pltpu.HBM) for a in arrays]


def hbm_like(shape):
    return pltpu.HBM(shape, jnp.bfloat16)


def params(limit=VMEM_LIMIT):
    return pltpu.CompilerParams(vmem_limit_bytes=limit)


def whiten_kernel(counted, spectra, whole, x0, y0, x1, y1, extra_x, extra_y):
    step = pl.program_id(0)
    half = pl.num_programs(0) // 2
    windows, count, _ = spectra.shape
    chip = lax.axis_index("blk")
    rows = pl.ds(pl.multiple_of(step * count, count), count)
    for w in range(windows):
        values = spectra[w].astype(jnp.float32)
        scaling = lax.rsqrt(jnp.mean(values * values, axis=1, keepdims=True) + 1e-05)
        scaling = scaling * jnp.where(w < counted[0], 1.0, 0.0)
        out = (values * scaling).astype(jnp.bfloat16)
        width = out.shape[1] // BANDS
        for band in range(BANDS):
            whole[band, w, rows] = out[:, band * width : (band + 1) * width]

    def send(to_x, to_y, extra, first):
        at = pl.ds(pl.multiple_of((step - first) * count, count), count)
        to_x[:, at] = whole[chip % 2, :, rows]
        to_y[:, at] = whole[1 - chip // 2, :, rows]
        extra[:, at] = whole[chip // 2, :, rows]

    pl.when(step < half)(lambda: send(x0, y0, extra_x, 0))
    pl.when(step >= half)(lambda: send(x1, y1, extra_y, half))


def whiten(spectra, counted):
    windows, channels, width = spectra.shape
    band_width = width // BANDS
    rows = 2 * TILE
    part = jax.ShapeDtypeStruct((windows, channels // 2, band_width), jnp.bfloat16)
    whole = jax.ShapeDtypeStruct((BANDS, windows, channels, band_width), jnp.bfloat16)
    return pl.pallas_call(
        whiten_kernel,
        grid=(channels // rows,),
        in_specs=[
            pl.BlockSpec(memory_space=pltpu.SMEM),
            pl.BlockSpec((windows, rows, width), lambda i: (0, i, 0)),
        ],
        out_specs=in_vmem(7),
        out_shape=[whole] + [part] * 6,
        compiler_params=params(WHITEN_LIMIT),
        cost_estimate=SMALL,
    )(counted, *in_hbm([spectra]))


def product(left, right, weight):
    total = None
    for rows, columns in zip(left, right):
        width = columns.shape[1] // 2
        turned = jnp.concatenate([-columns[:, width:], columns[:, :width]], axis=1)
        both = jnp.concatenate([columns, turned], axis=0)
        part = lax.dot_general(
            rows, both, (((1,), (1,)), ((), ())), preferred_element_type=jnp.float32
        )
        total = part if total is None else total + part
    return (total * weight).astype(jnp.bfloat16)


def tile_rows(tile):
    return pl.ds(pl.multiple_of(tile * TILE, TILE), TILE)


def each_unit(out):
    core = lax.axis_index("seg") % 2
    for other, ref in enumerate(out):
        for layer in range(LAYERS):
            yield layer, (1 - core if other else core), ref.at[layer]


def own_kernel(weight, whole, *out):
    for layer, core, ref in each_unit(out):
        band, q = layer // 2, 2 * (layer % 2) + core
        windows = range(whole.shape[1])
        ref[...] = product(
            [whole[band, w] for w in windows],
            [whole[band, w, tile_rows(q)] for w in windows],
            weight[0],
        )


def pair_kernel(weight, whole, from_x, from_y, *out):
    chip = lax.axis_index("blk")
    bands = (1 - chip % 2, chip // 2)
    half = from_x.shape[1]
    for layer, core, ref in each_unit(out):
        along = layer // 2
        arrived, q = (from_x, from_y)[along], layer % 2
        rows = pl.ds(pl.multiple_of(core * half, half), half)
        windows = range(whole.shape[1])
        ref[...] = product(
            [whole[bands[along], w, rows] for w in windows],
            [arrived[w, tile_rows(q)] for w in windows],
            weight[0],
        )


def corner_kernel(weight, x0, x1, y0, y1, extra_x, extra_y, *out):
    chip = lax.axis_index("blk")
    windows = range(x0.shape[0])

    def multiply(left, right, tile, ref):
        ref[...] = product(left, [right[w, tile_rows(tile)] for w in windows], weight[0])

    def split(one, two, extra_one, extra_two):
        for layer, core, ref in each_unit(out):
            if layer < LAYERS // 2:
                multiply([extra_one[w] for w in windows], two[layer], core, ref)
            else:
                left = [jnp.where(core == 0, one[0][w], one[1][w]) for w in windows]
                multiply(left, extra_two, layer - LAYERS // 2, ref)

    def joined(one, two):
        for layer, core, ref in each_unit(out):
            multiply([one[layer // 2][w] for w in windows], two[layer % 2], core, ref)

    x, y = (x0, x1), (y0, y1)
    pl.when(chip == 0)(lambda: split(x, y, extra_x, extra_y))
    pl.when(chip == 1)(lambda: joined(y, x))
    pl.when(chip == 2)(lambda: joined(x, y))
    pl.when(chip == 3)(lambda: split(y, x, extra_y, extra_x))


def in_vmem(count):
    return [pl.BlockSpec(memory_space=pltpu.VMEM)] * count


def unit_call(kernel, rows, weight, *arrays):
    out = jax.ShapeDtypeStruct((LAYERS, rows, 2 * TILE), jnp.bfloat16)
    return pl.pallas_call(
        kernel,
        in_specs=[pl.BlockSpec(memory_space=pltpu.SMEM)] + in_vmem(len(arrays)),
        out_specs=in_vmem(2),
        out_shape=[out, out],
        compiler_params=params(),
        cost_estimate=SMALL,
    )(weight, *arrays)


def pair_sum_kernel(kept, got, *outs):
    layer = lax.axis_index("seg") // 2
    for r, out in enumerate(outs):
        at = lax.rem(layer + r, LAYERS)
        out[...] = (kept[at].astype(jnp.float32) + got[at].astype(jnp.float32)).astype(jnp.bfloat16)


def pair_sum(kept, got):
    shape = jax.ShapeDtypeStruct(kept.shape[1:], jnp.bfloat16)
    return pl.pallas_call(
        pair_sum_kernel,
        in_specs=in_vmem(2),
        out_specs=in_vmem(LAYERS),
        out_shape=[shape] * LAYERS,
        compiler_params=params(),
        cost_estimate=SMALL,
    )(kept, got)


def halve_kernel(bit, kept, got, keep, send):
    layer = lax.axis_index("seg") // 2
    mine = lax.rem(layer // bit, 2)
    count = kept.shape[0] // 2
    for out, side in ((keep, mine), (send, 1 - mine)):
        for n in range(count):
            at = 2 * n + side if bit == 1 else side
            value = kept[at].astype(jnp.float32) + got[at].astype(jnp.float32)
            out[n] = value.astype(jnp.bfloat16)


def halve(bit, kept, got):
    shape = jax.ShapeDtypeStruct((kept.shape[0] // 2,) + kept.shape[1:], jnp.bfloat16)
    return pl.pallas_call(
        functools.partial(halve_kernel, bit),
        in_specs=in_vmem(2),
        out_specs=in_vmem(2),
        out_shape=[shape, shape],
        compiler_params=params(),
        cost_estimate=SMALL,
    )(kept, got)


def layer_sum(parts):
    total = parts[0][...].astype(jnp.float32)
    for part in parts[1:]:
        total = total + part[...].astype(jnp.float32)
    return total.astype(jnp.bfloat16)


def tile_powers(rows, table):
    velocities = table.shape[1] // 2
    field = lax.dot_general(
        rows, table, (((1,), (0,)), ((), ())), preferred_element_type=jnp.float32
    )
    squared = field * field
    energy = squared[:, :velocities] + squared[:, velocities:]
    return [
        jnp.sum(energy[t : t + TILE], axis=0, keepdims=True) * (1.0 / TILE)
        for t in range(0, rows.shape[0], TILE)
    ]


def transposed(stacked):
    rounded = stacked.astype(jnp.float32)
    turned = []
    for t in range(0, stacked.shape[0], TILE):
        tile = rounded[t : t + TILE]
        turned.append(jnp.concatenate([tile[:, :TILE].T, -tile[:, TILE:].T], axis=1))
    return jnp.concatenate(turned, axis=0).astype(jnp.bfloat16)


def matrix_kernel(phases, matrix):
    rows, velocities = phases.shape[1:]
    norm_factor = 1.0 / math.sqrt(TILE)
    for band in range(phases.shape[0]):
        cosine = (jnp.cos(phases[band]) * norm_factor).astype(jnp.bfloat16)
        sine_part = (jnp.sin(phases[band]) * norm_factor).astype(jnp.bfloat16)
        matrix[band, :rows, :velocities] = cosine
        matrix[band, :rows, velocities:] = sine_part
        matrix[band, rows:, :velocities] = -sine_part
        matrix[band, rows:, velocities:] = cosine


def matrix_of(phases):
    bands, rows, velocities = phases.shape
    return pl.pallas_call(
        matrix_kernel,
        in_specs=in_vmem(1),
        out_specs=in_vmem(1)[0],
        out_shape=jax.ShapeDtypeStruct((bands, 2 * rows, 2 * velocities), jnp.bfloat16),
        compiler_params=params(),
        cost_estimate=SMALL,
    )(phases)


def power_kernel(group, matrix, *refs):
    out = refs[-1]
    chip, me = lax.axis_index("blk"), lax.axis_index("seg")
    if group == "own":
        band = me // QUAD
    elif group == "pair":
        band = jnp.where(me < QUAD, 1 - chip % 2, chip // 2)
    else:
        band = jnp.where((chip == 1) | (chip == 2), chip - 1, me // QUAD)
    stacked = layer_sum(refs[:-1])
    table = matrix[band]
    found = tile_powers(stacked, table)
    if group == "pair":
        found += tile_powers(transposed(stacked), table)
    for t, row in enumerate(found):
        out[t : t + 1, :] = row


def powers_of(group, matrix, parts):
    velocities = matrix.shape[2] // 2
    rows = parts[0].shape[0] // TILE * (2 if group == "pair" else 1)
    return pl.pallas_call(
        functools.partial(power_kernel, group),
        in_specs=in_vmem(1 + len(parts)),
        out_specs=in_vmem(1)[0],
        out_shape=jax.ShapeDtypeStruct((rows, velocities), jnp.float32),
        compiler_params=params(),
        cost_estimate=SMALL,
    )(matrix, *parts)


def across(array, hops):
    return lax.ppermute(array, "blk", hops)


def other_core(array):
    return lax.ppermute(array, "seg", [(i, i ^ 1) for i in range(UNITS)])


def layers_on(array, r):
    return lax.ppermute(array, "seg", [(i, (i + 2 * r) % UNITS) for i in range(UNITS)])


def from_layers(array):
    return jnp.stack([array] + [layers_on(array, r) for r in range(1, LAYERS)])


def grid_body(spectra, window_count, tile_owner, phases):
    chip = lax.axis_index("blk")
    me = lax.axis_index("seg")
    whole, x0, y0, x1, y1, extra_x, extra_y = whiten(spectra[0], window_count)
    x0, y0 = across(x0, X_SWAP), across(y0, Y_SWAP)
    x1, y1 = across(x1, X_SWAP), across(y1, Y_SWAP)
    extra_x, extra_y = across(extra_x, X_EXTRA), across(extra_y, Y_EXTRA)

    weight = 1.0 / (window_count.astype(jnp.float32) * math.sqrt(FB * UNITS))
    matrix = matrix_of(phases)
    channels = whole.shape[2]

    def sums_of(kernel, rows, weight, earlier, *arrays):
        kept, sent = unit_call(kernel, rows, weight, *arrays)
        sent, *earlier = lax.optimization_barrier((sent, *earlier))
        return pair_sum(kept, other_core(sent)), earlier

    def along_layers(sums):
        return [sums[0]] + [layers_on(sums[r], r) for r in range(1, LAYERS)]

    kept, sent = unit_call(own_kernel, channels, weight, whole)
    got = other_core(sent)
    for bit in (1, 2):
        kept, sent = halve(bit, kept, got)
        got = lax.ppermute(sent, "seg", [(i, i ^ (2 * bit)) for i in range(UNITS)])
    own = [kept[0], got[0]]
    own = powers_of("own", matrix, own)
    half = channels // 2
    pair0, (own,) = sums_of(pair_kernel, half, weight, [own], whole, x0, y0)
    pair0 = along_layers(pair0)
    pair0 = powers_of("pair", matrix, pair0)
    weight, pair0 = lax.optimization_barrier((weight, pair0))
    pair1 = along_layers(sums_of(pair_kernel, half, weight, [], whole, x1, y1)[0])
    sums, pair1 = sums_of(corner_kernel, half, weight, pair1, x0, x1, y0, y1, extra_x, extra_y)
    corner = along_layers(sums)
    owner_row, *pair1 = lax.optimization_barrier((tile_owner[0], *pair1, *sums))[: 1 + LAYERS]
    mine, mine_filled = my_slots(owner_row, UNITS)
    sources = jnp.asarray(SOURCE_ROWS)[chip, me][mine]
    pair1 = powers_of("pair", matrix, pair1)
    tiles = pair0.shape[0] // 2
    turned = jnp.concatenate([pair0[tiles:], pair1[tiles:]], axis=0)
    turned = lax.ppermute(turned, ("blk", "seg"), TURNED_HOPS)
    near = jnp.concatenate([own, pair0[:tiles], pair1[:tiles], turned], axis=0)
    far = other_core(near)
    last = powers_of("corner", matrix, corner)
    corners = jnp.concatenate([across(last, X_CORNER), across(last, Y_CORNER)], axis=0)
    rows = jnp.concatenate([near, far, corners, other_core(corners)], axis=0)
    every = from_layers(rows)
    response = jnp.take(every.reshape(-1, every.shape[-1]), sources, axis=0)
    response = response * mine_filled[:, None, None].astype(jnp.float32)
    return response[None, None]


def solution(mesh):
    placed = (P("seg", None, "blk", None), P("seg"), P("blk", None), P())
    fits = mesh.shape["blk"] == CHIPS and mesh.shape["seg"] == UNITS
    return jax.shard_map(
        grid_body if fits else ring_body,
        mesh=mesh,
        in_specs=placed,
        out_specs=P("blk", "seg", None, None, None),
        check_vma=False,
    )
```

```python
import functools
import math

import jax
import jax.numpy as jnp
import numpy as np
from jax import lax
from jax.experimental import pallas as pl
from jax.experimental.pallas import tpu as pltpu
from jax.sharding import PartitionSpec as P

TILE = 128
BANDS = 2
CAP = 8
FB = 512
QUAD = 4
VMEM_LIMIT = 8 * 1024 * 1024
WHITEN_LIMIT = 16 * 1024 * 1024


def from_behind(array, axis, by):
    devices = lax.axis_size(axis)
    return lax.ppermute(array, axis, [(i, (i + by) % devices) for i in range(devices)])


def prepare(segment_data, counted):
    windows = segment_data.shape[0]
    channels = segment_data.shape[1]
    spectrum = segment_data.astype(jnp.float32).reshape(windows, channels, BANDS, 2, FB)
    scaling = lax.rsqrt(jnp.mean(spectrum * spectrum, axis=(2, 3, 4)) + 1e-05)
    live_mask = (jnp.arange(windows, dtype=jnp.int32) < counted).astype(jnp.float32)
    return (
        spectrum * scaling[:, :, None, None, None] * live_mask[:, None, None, None, None]
    ).astype(jnp.bfloat16)


def correlate(resident, visiting, weight):
    windows = resident.shape[0]
    flipped = jnp.stack([-visiting[:, :, :, 1], visiting[:, :, :, 0]], axis=3)
    both_parts = jnp.stack([visiting, flipped], axis=1)
    left_side = resident.reshape(windows, QUAD, TILE, BANDS, 2 * FB)
    right_side = both_parts.reshape(windows, 2, QUAD, TILE, BANDS, 2 * FB)
    product = jnp.einsum(
        "wqibk,wpsjbk->qsbipj", left_side, right_side, preferred_element_type=jnp.float32
    )
    return (product * weight).astype(jnp.bfloat16).reshape(QUAD * QUAD, BANDS, TILE, 2 * TILE)


def phase_matrix(phases):
    norm_factor = 1.0 / math.sqrt(TILE)
    cosine = (jnp.cos(phases) * norm_factor).astype(jnp.bfloat16)
    sine_part = (jnp.sin(phases) * norm_factor).astype(jnp.bfloat16)
    upper = jnp.concatenate([cosine, sine_part], axis=2)
    lower = jnp.concatenate([-sine_part, cosine], axis=2)
    return jnp.concatenate([upper, lower], axis=1)


def disperse(stacked, phases):
    velocity_count = phases.shape[2]
    matrix = phase_matrix(phases)
    field = jnp.einsum("nbij,bjv->nbiv", stacked, matrix, preferred_element_type=jnp.float32)
    squared = field * field
    energy = squared[..., :velocity_count] + squared[..., velocity_count:]
    return jnp.mean(energy, axis=2)


def slot_table(owner_row, segments):
    count_tiles = owner_row.shape[0]
    order_ids = jnp.arange(count_tiles, dtype=jnp.int32)
    same_owner = owner_row[:, None] == owner_row[None, :]
    earlier = order_ids[None, :] < order_ids[:, None]
    rank_of = jnp.sum(jnp.where(same_owner & earlier, 1, 0), axis=1).astype(jnp.int32)
    slot_ids = owner_row * CAP + rank_of
    grid_ids = jnp.arange(segments * CAP, dtype=jnp.int32)
    matches = grid_ids[:, None] == slot_ids[None, :]
    tile_of_slot = jnp.sum(jnp.where(matches, order_ids[None, :], 0), axis=1)
    filled = jnp.any(matches, axis=1)
    return (tile_of_slot, filled)


def my_slots(owner_row, segments):
    tile_of_slot, filled = slot_table(owner_row, segments)
    my_start = lax.axis_index("seg") * CAP
    mine = lax.dynamic_slice_in_dim(tile_of_slot, my_start, CAP, 0)
    mine_filled = lax.dynamic_slice_in_dim(filled, my_start, CAP, 0)
    return mine, mine_filled


def ring_body(spectra, window_count, tile_owner, phases):
    blocks = lax.axis_size("blk")
    segments = lax.axis_size("seg")
    counted = window_count[0]
    whitened = prepare(spectra[0], counted)
    weight = 1.0 / (counted.astype(jnp.float32) * math.sqrt(FB * segments))
    pieces = [correlate(whitened, whitened, weight)]
    moving = whitened
    for shift_step in range(1, blocks // 2 + 1):
        moving = from_behind(moving, "blk", -1)
        pieces.append(correlate(whitened, moving, weight))
    all_tiles = jnp.concatenate(pieces, axis=0)
    share_rows = (
        lax.psum_scatter(all_tiles, "seg", scatter_dimension=0, tiled=True)
        .astype(jnp.float32)
        .astype(jnp.bfloat16)
    )
    share_power = disperse(share_rows, phases)
    every_power = lax.all_gather(share_power, "seg", axis=0, tiled=True)
    mine, mine_filled = my_slots(tile_owner[0], segments)
    response = jnp.take(every_power, mine, axis=0) * mine_filled[:, None, None].astype(jnp.float32)
    return response[None, None]


CHIPS = 4
UNITS = 2 * QUAD
LAYERS = UNITS // 2
X_SWAP = [(0, 1), (1, 0), (2, 3), (3, 2)]
Y_SWAP = [(0, 2), (2, 0), (1, 3), (3, 1)]
X_EXTRA = [(1, 0), (2, 3)]
Y_EXTRA = [(2, 0), (1, 3)]
X_CORNER = [(0, 1), (2, 3)]
Y_CORNER = [(3, 1), (1, 3)]
BAND_FROM_X = [1, 0, 1, 0]
BAND_FROM_Y = [0, 0, 1, 1]
OWN_ROW, PAIR_ROW, TURNED_ROW, CORE_ROWS = 0, QUAD, 2 * QUAD, 3 * QUAD
CORNER_ROW, LAYER_ROWS = 2 * CORE_ROWS, 2 * CORE_ROWS + 8
TURNED_HOPS = [
    (UNITS * chip + n, UNITS * (chip ^ (1 if n < QUAD else 2)) + n)
    for chip in range(CHIPS)
    for n in range(UNITS)
]


def source_rows():
    table = np.full((CHIPS, UNITS, 3 * QUAD * QUAD, BANDS), -1, np.int32)

    def put(block, step, p, q, band, unit, row, corner=0):
        tile = (step * QUAD + p) * QUAD + q
        for me in range(UNITS):
            layer, other = (me // 2 - unit // 2) % LAYERS, (me ^ unit) & 1
            at = CORNER_ROW + 4 * other + row if corner else CORE_ROWS * other + row
            table[block, me, tile, band] = layer * LAYER_ROWS + at

    for chip in range(CHIPS):
        for n in range(UNITS):
            for p in range(QUAD):
                put(chip, 0, p, n % QUAD, n // QUAD, n, OWN_ROW + p)
            band = (BAND_FROM_X[chip], BAND_FROM_Y[chip])[n // QUAD]
            for i in range(4):
                p, q = 2 * (n % 2) + i % 2, 2 * (i // 2) + n // 2 % 2
                if n >= QUAD:
                    put(chip, 2, p, q, band, n, PAIR_ROW + i)
                    put(chip ^ 2, 2, q, p, band, n, TURNED_ROW + i)
                elif chip % 2 == 0:
                    put(chip, 1, p, q, band, n, PAIR_ROW + i)
                else:
                    put(chip ^ 1, 1, q, p, band, n, TURNED_ROW + i)
            for i in range(2):
                m = n - QUAD
                block = 3 if chip in (1, 2) else 1
                row = 2 * ((chip, block) in Y_CORNER) + i
                if block == 3:
                    put(3, 1, 2 * (n >> 2) + i, n & 3, chip - 1, n, row, 1)
                elif m < 0:
                    put(1, 1, (2 if chip == 3 else 0) + i, n, 0, n, row, 1)
                else:
                    put(1, 1, 2 * (m & 1) + i, (m >> 1) + (2 if chip == 0 else 0), 1, n, row, 1)
    assert table.min() >= 0
    return table


SOURCE_ROWS = source_rows()


SMALL = pl.CostEstimate(flops=1000, bytes_accessed=1000, transcendentals=0)


def in_hbm(arrays):
    return [pltpu.with_memory_space_constraint(a, pltpu.HBM) for a in arrays]


def hbm_like(shape):
    return pltpu.HBM(shape, jnp.bfloat16)


def params(limit=VMEM_LIMIT):
    return pltpu.CompilerParams(vmem_limit_bytes=limit)


def whiten_kernel(counted, spectra, whole, x0, y0, x1, y1, extra_x, extra_y):
    step = pl.program_id(0)
    half = pl.num_programs(0) // 2
    windows, count, _ = spectra.shape
    chip = lax.axis_index("blk")
    rows = pl.ds(pl.multiple_of(step * count, count), count)
    for w in range(windows):
        values = spectra[w].astype(jnp.float32)
        scaling = lax.rsqrt(jnp.mean(values * values, axis=1, keepdims=True) + 1e-05)
        scaling = scaling * jnp.where(w < counted[0], 1.0, 0.0)
        out = (values * scaling).astype(jnp.bfloat16)
        width = out.shape[1] // BANDS
        for band in range(BANDS):
            whole[band, w, rows] = out[:, band * width : (band + 1) * width]

    def send(to_x, to_y, extra, first):
        at = pl.ds(pl.multiple_of((step - first) * count, count), count)
        to_x[:, at] = whole[chip % 2, :, rows]
        to_y[:, at] = whole[1 - chip // 2, :, rows]
        extra[:, at] = whole[chip // 2, :, rows]

    pl.when(step < half)(lambda: send(x0, y0, extra_x, 0))
    pl.when(step >= half)(lambda: send(x1, y1, extra_y, half))


def whiten(spectra, counted):
    windows, channels, width = spectra.shape
    band_width = width // BANDS
    rows = 2 * TILE
    part = jax.ShapeDtypeStruct((windows, channels // 2, band_width), jnp.bfloat16)
    whole = jax.ShapeDtypeStruct((BANDS, windows, channels, band_width), jnp.bfloat16)
    return pl.pallas_call(
        whiten_kernel,
        grid=(channels // rows,),
        in_specs=[
            pl.BlockSpec(memory_space=pltpu.SMEM),
            pl.BlockSpec((windows, rows, width), lambda i: (0, i, 0)),
        ],
        out_specs=in_vmem(7),
        out_shape=[whole] + [part] * 6,
        compiler_params=params(WHITEN_LIMIT),
        cost_estimate=SMALL,
    )(counted, *in_hbm([spectra]))


def product(left, right, weight):
    total = None
    for rows, columns in zip(left, right):
        width = columns.shape[1] // 2
        turned = jnp.concatenate([-columns[:, width:], columns[:, :width]], axis=1)
        both = jnp.concatenate([columns, turned], axis=0)
        part = lax.dot_general(
            rows, both, (((1,), (1,)), ((), ())), preferred_element_type=jnp.float32
        )
        total = part if total is None else total + part
    return (total * weight).astype(jnp.bfloat16)


def tile_rows(tile):
    return pl.ds(pl.multiple_of(tile * TILE, TILE), TILE)


def each_unit(out):
    core = lax.axis_index("seg") % 2
    for other, ref in enumerate(out):
        for layer in range(LAYERS):
            yield layer, (1 - core if other else core), ref.at[layer]


def own_kernel(weight, whole, *out):
    for layer, core, ref in each_unit(out):
        band, q = layer // 2, 2 * (layer % 2) + core
        windows = range(whole.shape[1])
        ref[...] = product(
            [whole[band, w] for w in windows],
            [whole[band, w, tile_rows(q)] for w in windows],
            weight[0],
        )


def pair_kernel(weight, whole, from_x, from_y, *out):
    chip = lax.axis_index("blk")
    bands = (1 - chip % 2, chip // 2)
    half = from_x.shape[1]
    for layer, core, ref in each_unit(out):
        along = layer // 2
        arrived, q = (from_x, from_y)[along], layer % 2
        rows = pl.ds(pl.multiple_of(core * half, half), half)
        windows = range(whole.shape[1])
        ref[...] = product(
            [whole[bands[along], w, rows] for w in windows],
            [arrived[w, tile_rows(q)] for w in windows],
            weight[0],
        )


def corner_kernel(weight, x0, x1, y0, y1, extra_x, extra_y, *out):
    chip = lax.axis_index("blk")
    windows = range(x0.shape[0])

    def multiply(left, right, tile, ref):
        ref[...] = product(left, [right[w, tile_rows(tile)] for w in windows], weight[0])

    def split(one, two, extra_one, extra_two):
        for layer, core, ref in each_unit(out):
            if layer < LAYERS // 2:
                multiply([extra_one[w] for w in windows], two[layer], core, ref)
            else:
                left = [jnp.where(core == 0, one[0][w], one[1][w]) for w in windows]
                multiply(left, extra_two, layer - LAYERS // 2, ref)

    def joined(one, two):
        for layer, core, ref in each_unit(out):
            multiply([one[layer // 2][w] for w in windows], two[layer % 2], core, ref)

    x, y = (x0, x1), (y0, y1)
    pl.when(chip == 0)(lambda: split(x, y, extra_x, extra_y))
    pl.when(chip == 1)(lambda: joined(y, x))
    pl.when(chip == 2)(lambda: joined(x, y))
    pl.when(chip == 3)(lambda: split(y, x, extra_y, extra_x))


def in_vmem(count):
    return [pl.BlockSpec(memory_space=pltpu.VMEM)] * count


def unit_call(kernel, rows, weight, *arrays):
    out = jax.ShapeDtypeStruct((LAYERS, rows, 2 * TILE), jnp.bfloat16)
    return pl.pallas_call(
        kernel,
        in_specs=[pl.BlockSpec(memory_space=pltpu.SMEM)] + in_vmem(len(arrays)),
        out_specs=in_vmem(2),
        out_shape=[out, out],
        compiler_params=params(),
        cost_estimate=SMALL,
    )(weight, *arrays)


def pair_sum_kernel(kept, got, *outs):
    layer = lax.axis_index("seg") // 2
    for r, out in enumerate(outs):
        at = lax.rem(layer + r, LAYERS)
        out[...] = (kept[at].astype(jnp.float32) + got[at].astype(jnp.float32)).astype(jnp.bfloat16)


def pair_sum(kept, got):
    shape = jax.ShapeDtypeStruct(kept.shape[1:], jnp.bfloat16)
    return pl.pallas_call(
        pair_sum_kernel,
        in_specs=in_vmem(2),
        out_specs=in_vmem(LAYERS),
        out_shape=[shape] * LAYERS,
        compiler_params=params(),
        cost_estimate=SMALL,
    )(kept, got)


def halve_kernel(bit, kept, got, keep, send):
    layer = lax.axis_index("seg") // 2
    mine = lax.rem(layer // bit, 2)
    count = kept.shape[0] // 2
    for out, side in ((keep, mine), (send, 1 - mine)):
        for n in range(count):
            at = 2 * n + side if bit == 1 else side
            value = kept[at].astype(jnp.float32) + got[at].astype(jnp.float32)
            out[n] = value.astype(out.dtype)


def halve(bit, kept, got):
    shape = (kept.shape[0] // 2,) + kept.shape[1:]
    return pl.pallas_call(
        functools.partial(halve_kernel, bit),
        in_specs=in_vmem(2),
        out_specs=in_vmem(2),
        out_shape=[jax.ShapeDtypeStruct(shape, t) for t in (jnp.float32, jnp.bfloat16)],
        compiler_params=params(),
        cost_estimate=SMALL,
    )(kept, got)


def layer_sum(parts):
    total = parts[0][...].astype(jnp.float32)
    for part in parts[1:]:
        total = total + part[...].astype(jnp.float32)
    return total.astype(jnp.bfloat16)


def tile_powers(rows, table):
    velocities = table.shape[1] // 2
    field = lax.dot_general(
        rows, table, (((1,), (0,)), ((), ())), preferred_element_type=jnp.float32
    )
    squared = field * field
    energy = squared[:, :velocities] + squared[:, velocities:]
    return [
        jnp.sum(energy[t : t + TILE], axis=0, keepdims=True) * (1.0 / TILE)
        for t in range(0, rows.shape[0], TILE)
    ]


def transposed(stacked):
    rounded = stacked.astype(jnp.float32)
    turned = []
    for t in range(0, stacked.shape[0], TILE):
        tile = rounded[t : t + TILE]
        turned.append(jnp.concatenate([tile[:, :TILE].T, -tile[:, TILE:].T], axis=1))
    return jnp.concatenate(turned, axis=0).astype(jnp.bfloat16)


def matrix_kernel(phases, matrix):
    rows, velocities = phases.shape[1:]
    norm_factor = 1.0 / math.sqrt(TILE)
    for band in range(phases.shape[0]):
        cosine = (jnp.cos(phases[band]) * norm_factor).astype(jnp.bfloat16)
        sine_part = (jnp.sin(phases[band]) * norm_factor).astype(jnp.bfloat16)
        matrix[band, :rows, :velocities] = cosine
        matrix[band, :rows, velocities:] = sine_part
        matrix[band, rows:, :velocities] = -sine_part
        matrix[band, rows:, velocities:] = cosine


def matrix_of(phases):
    bands, rows, velocities = phases.shape
    return pl.pallas_call(
        matrix_kernel,
        in_specs=in_vmem(1),
        out_specs=in_vmem(1)[0],
        out_shape=jax.ShapeDtypeStruct((bands, 2 * rows, 2 * velocities), jnp.bfloat16),
        compiler_params=params(),
        cost_estimate=SMALL,
    )(phases)


def power_kernel(group, matrix, *refs):
    out = refs[-1]
    chip, me = lax.axis_index("blk"), lax.axis_index("seg")
    if group == "own":
        band = me // QUAD
    elif group == "pair":
        band = jnp.where(me < QUAD, 1 - chip % 2, chip // 2)
    else:
        band = jnp.where((chip == 1) | (chip == 2), chip - 1, me // QUAD)
    stacked = layer_sum(refs[:-1])
    table = matrix[band]
    found = tile_powers(stacked, table)
    if group == "pair":
        found += tile_powers(transposed(stacked), table)
    for t, row in enumerate(found):
        out[t : t + 1, :] = row


def powers_of(group, matrix, parts):
    velocities = matrix.shape[2] // 2
    rows = parts[0].shape[0] // TILE * (2 if group == "pair" else 1)
    return pl.pallas_call(
        functools.partial(power_kernel, group),
        in_specs=in_vmem(1 + len(parts)),
        out_specs=in_vmem(1)[0],
        out_shape=jax.ShapeDtypeStruct((rows, velocities), jnp.float32),
        compiler_params=params(),
        cost_estimate=SMALL,
    )(matrix, *parts)


def across(array, hops):
    return lax.ppermute(array, "blk", hops)


def other_core(array):
    return lax.ppermute(array, "seg", [(i, i ^ 1) for i in range(UNITS)])


def layers_on(array, r):
    return lax.ppermute(array, "seg", [(i, (i + 2 * r) % UNITS) for i in range(UNITS)])


def from_layers(array):
    return jnp.stack([array] + [layers_on(array, r) for r in range(1, LAYERS)])


def grid_body(spectra, window_count, tile_owner, phases):
    chip = lax.axis_index("blk")
    me = lax.axis_index("seg")
    whole, x0, y0, x1, y1, extra_x, extra_y = whiten(spectra[0], window_count)
    x0, y0 = across(x0, X_SWAP), across(y0, Y_SWAP)
    x1, y1 = across(x1, X_SWAP), across(y1, Y_SWAP)
    extra_x, extra_y = across(extra_x, X_EXTRA), across(extra_y, Y_EXTRA)

    weight = 1.0 / (window_count.astype(jnp.float32) * math.sqrt(FB * UNITS))
    matrix = matrix_of(phases)
    channels = whole.shape[2]

    def sums_of(kernel, rows, weight, earlier, *arrays):
        kept, sent = unit_call(kernel, rows, weight, *arrays)
        sent, *earlier = lax.optimization_barrier((sent, *earlier))
        return pair_sum(kept, other_core(sent)), earlier

    def along_layers(sums):
        return [sums[0]] + [layers_on(sums[r], r) for r in range(1, LAYERS)]

    kept, sent = unit_call(own_kernel, channels, weight, whole)
    got = other_core(sent)
    for bit in (1, 2):
        kept, sent = halve(bit, kept, got)
        got = lax.ppermute(sent, "seg", [(i, i ^ (2 * bit)) for i in range(UNITS)])
    own = [kept[0], got[0]]
    own = powers_of("own", matrix, own)
    half = channels // 2
    pair0, (own,) = sums_of(pair_kernel, half, weight, [own], whole, x0, y0)
    pair0 = along_layers(pair0)
    pair0 = powers_of("pair", matrix, pair0)
    weight, pair0 = lax.optimization_barrier((weight, pair0))
    pair1 = along_layers(sums_of(pair_kernel, half, weight, [], whole, x1, y1)[0])
    sums, pair1 = sums_of(corner_kernel, half, weight, pair1, x0, x1, y0, y1, extra_x, extra_y)
    corner = along_layers(sums)
    owner_row, *pair1 = lax.optimization_barrier((tile_owner[0], *pair1, *sums))[: 1 + LAYERS]
    mine, mine_filled = my_slots(owner_row, UNITS)
    sources = jnp.asarray(SOURCE_ROWS)[chip, me][mine]
    pair1 = powers_of("pair", matrix, pair1)
    tiles = pair0.shape[0] // 2
    turned = jnp.concatenate([pair0[tiles:], pair1[tiles:]], axis=0)
    turned = lax.ppermute(turned, ("blk", "seg"), TURNED_HOPS)
    near = jnp.concatenate([own, pair0[:tiles], pair1[:tiles], turned], axis=0)
    far = other_core(near)
    last = powers_of("corner", matrix, corner)
    corners = jnp.concatenate([across(last, X_CORNER), across(last, Y_CORNER)], axis=0)
    rows = jnp.concatenate([near, far, corners, other_core(corners)], axis=0)
    every = from_layers(rows)
    response = jnp.take(every.reshape(-1, every.shape[-1]), sources, axis=0)
    response = response * mine_filled[:, None, None].astype(jnp.float32)
    return response[None, None]


def solution(mesh):
    placed = (P("seg", None, "blk", None), P("seg"), P("blk", None), P())
    fits = mesh.shape["blk"] == CHIPS and mesh.shape["seg"] == UNITS
    return jax.shard_map(
        grid_body if fits else ring_body,
        mesh=mesh,
        in_specs=placed,
        out_specs=P("blk", "seg", None, None, None),
        check_vma=False,
    )
```

```python
import functools
import math

import jax
import jax.numpy as jnp
import numpy as np
from jax import lax
from jax.experimental import pallas as pl
from jax.experimental.pallas import tpu as pltpu
from jax.sharding import PartitionSpec as P

TILE = 128
BANDS = 2
CAP = 8
FB = 512
QUAD = 4
VMEM_LIMIT = 8 * 1024 * 1024
WHITEN_LIMIT = 16 * 1024 * 1024


def from_behind(array, axis, by):
    devices = lax.axis_size(axis)
    return lax.ppermute(array, axis, [(i, (i + by) % devices) for i in range(devices)])


def prepare(segment_data, counted):
    windows = segment_data.shape[0]
    channels = segment_data.shape[1]
    spectrum = segment_data.astype(jnp.float32).reshape(windows, channels, BANDS, 2, FB)
    scaling = lax.rsqrt(jnp.mean(spectrum * spectrum, axis=(2, 3, 4)) + 1e-05)
    live_mask = (jnp.arange(windows, dtype=jnp.int32) < counted).astype(jnp.float32)
    return (
        spectrum * scaling[:, :, None, None, None] * live_mask[:, None, None, None, None]
    ).astype(jnp.bfloat16)


def correlate(resident, visiting, weight):
    windows = resident.shape[0]
    flipped = jnp.stack([-visiting[:, :, :, 1], visiting[:, :, :, 0]], axis=3)
    both_parts = jnp.stack([visiting, flipped], axis=1)
    left_side = resident.reshape(windows, QUAD, TILE, BANDS, 2 * FB)
    right_side = both_parts.reshape(windows, 2, QUAD, TILE, BANDS, 2 * FB)
    product = jnp.einsum(
        "wqibk,wpsjbk->qsbipj", left_side, right_side, preferred_element_type=jnp.float32
    )
    return (product * weight).astype(jnp.bfloat16).reshape(QUAD * QUAD, BANDS, TILE, 2 * TILE)


def phase_matrix(phases):
    norm_factor = 1.0 / math.sqrt(TILE)
    cosine = (jnp.cos(phases) * norm_factor).astype(jnp.bfloat16)
    sine_part = (jnp.sin(phases) * norm_factor).astype(jnp.bfloat16)
    upper = jnp.concatenate([cosine, sine_part], axis=2)
    lower = jnp.concatenate([-sine_part, cosine], axis=2)
    return jnp.concatenate([upper, lower], axis=1)


def disperse(stacked, phases):
    velocity_count = phases.shape[2]
    matrix = phase_matrix(phases)
    field = jnp.einsum("nbij,bjv->nbiv", stacked, matrix, preferred_element_type=jnp.float32)
    squared = field * field
    energy = squared[..., :velocity_count] + squared[..., velocity_count:]
    return jnp.mean(energy, axis=2)


def slot_table(owner_row, segments):
    count_tiles = owner_row.shape[0]
    order_ids = jnp.arange(count_tiles, dtype=jnp.int32)
    same_owner = owner_row[:, None] == owner_row[None, :]
    earlier = order_ids[None, :] < order_ids[:, None]
    rank_of = jnp.sum(jnp.where(same_owner & earlier, 1, 0), axis=1).astype(jnp.int32)
    slot_ids = owner_row * CAP + rank_of
    grid_ids = jnp.arange(segments * CAP, dtype=jnp.int32)
    matches = grid_ids[:, None] == slot_ids[None, :]
    tile_of_slot = jnp.sum(jnp.where(matches, order_ids[None, :], 0), axis=1)
    filled = jnp.any(matches, axis=1)
    return (tile_of_slot, filled)


def my_slots(owner_row, segments):
    tile_of_slot, filled = slot_table(owner_row, segments)
    my_start = lax.axis_index("seg") * CAP
    mine = lax.dynamic_slice_in_dim(tile_of_slot, my_start, CAP, 0)
    mine_filled = lax.dynamic_slice_in_dim(filled, my_start, CAP, 0)
    return mine, mine_filled


def ring_body(spectra, window_count, tile_owner, phases):
    blocks = lax.axis_size("blk")
    segments = lax.axis_size("seg")
    counted = window_count[0]
    whitened = prepare(spectra[0], counted)
    weight = 1.0 / (counted.astype(jnp.float32) * math.sqrt(FB * segments))
    pieces = [correlate(whitened, whitened, weight)]
    moving = whitened
    for shift_step in range(1, blocks // 2 + 1):
        moving = from_behind(moving, "blk", -1)
        pieces.append(correlate(whitened, moving, weight))
    all_tiles = jnp.concatenate(pieces, axis=0)
    share_rows = (
        lax.psum_scatter(all_tiles, "seg", scatter_dimension=0, tiled=True)
        .astype(jnp.float32)
        .astype(jnp.bfloat16)
    )
    share_power = disperse(share_rows, phases)
    every_power = lax.all_gather(share_power, "seg", axis=0, tiled=True)
    mine, mine_filled = my_slots(tile_owner[0], segments)
    response = jnp.take(every_power, mine, axis=0) * mine_filled[:, None, None].astype(jnp.float32)
    return response[None, None]


CHIPS = 4
UNITS = 2 * QUAD
LAYERS = UNITS // 2
X_SWAP = [(0, 1), (1, 0), (2, 3), (3, 2)]
Y_SWAP = [(0, 2), (2, 0), (1, 3), (3, 1)]
X_EXTRA = [(1, 0), (2, 3)]
Y_EXTRA = [(2, 0), (1, 3)]
X_CORNER = [(0, 1), (2, 3)]
Y_CORNER = [(3, 1), (1, 3)]
BAND_FROM_X = [1, 0, 1, 0]
BAND_FROM_Y = [0, 0, 1, 1]
OWN_ROW, PAIR_ROW, TURNED_ROW, CORE_ROWS = 0, QUAD, 2 * QUAD, 3 * QUAD
CORNER_ROW, LAYER_ROWS = 2 * CORE_ROWS, 2 * CORE_ROWS + 8
TURNED_HOPS = [
    (UNITS * chip + n, UNITS * (chip ^ (1 if n < QUAD else 2)) + n)
    for chip in range(CHIPS)
    for n in range(UNITS)
]


def source_rows():
    table = np.full((CHIPS, UNITS, 3 * QUAD * QUAD, BANDS), -1, np.int32)

    def put(block, step, p, q, band, unit, row, corner=0):
        tile = (step * QUAD + p) * QUAD + q
        for me in range(UNITS):
            layer, other = (me // 2 - unit // 2) % LAYERS, (me ^ unit) & 1
            at = CORNER_ROW + 4 * other + row if corner else CORE_ROWS * other + row
            table[block, me, tile, band] = layer * LAYER_ROWS + at

    for chip in range(CHIPS):
        for n in range(UNITS):
            for p in range(QUAD):
                put(chip, 0, p, n % QUAD, n // QUAD, n, OWN_ROW + p)
            band = (BAND_FROM_X[chip], BAND_FROM_Y[chip])[n // QUAD]
            for i in range(4):
                p, q = 2 * (n % 2) + i % 2, 2 * (i // 2) + n // 2 % 2
                if n >= QUAD:
                    put(chip, 2, p, q, band, n, PAIR_ROW + i)
                    put(chip ^ 2, 2, q, p, band, n, TURNED_ROW + i)
                elif chip % 2 == 0:
                    put(chip, 1, p, q, band, n, PAIR_ROW + i)
                else:
                    put(chip ^ 1, 1, q, p, band, n, TURNED_ROW + i)
            for i in range(2):
                m = n - QUAD
                block = 3 if chip in (1, 2) else 1
                row = 2 * ((chip, block) in Y_CORNER) + i
                if block == 3:
                    put(3, 1, 2 * (n >> 2) + i, n & 3, chip - 1, n, row, 1)
                elif m < 0:
                    put(1, 1, (2 if chip == 3 else 0) + i, n, 0, n, row, 1)
                else:
                    put(1, 1, 2 * (m & 1) + i, (m >> 1) + (2 if chip == 0 else 0), 1, n, row, 1)
    assert table.min() >= 0
    return table


SOURCE_ROWS = source_rows()


SMALL = pl.CostEstimate(flops=1000, bytes_accessed=1000, transcendentals=0)


def in_hbm(arrays):
    return [pltpu.with_memory_space_constraint(a, pltpu.HBM) for a in arrays]


def hbm_like(shape):
    return pltpu.HBM(shape, jnp.bfloat16)


def params(limit=VMEM_LIMIT):
    return pltpu.CompilerParams(vmem_limit_bytes=limit)


def whiten_kernel(counted, spectra, whole, x0, y0, x1, y1, extra_x, extra_y):
    step = pl.program_id(0)
    half = pl.num_programs(0) // 2
    windows, count, _ = spectra.shape
    chip = lax.axis_index("blk")
    rows = pl.ds(pl.multiple_of(step * count, count), count)
    for w in range(windows):
        values = spectra[w].astype(jnp.float32)
        scaling = lax.rsqrt(jnp.mean(values * values, axis=1, keepdims=True) + 1e-05)
        scaling = scaling * jnp.where(w < counted[0], 1.0, 0.0)
        out = (values * scaling).astype(jnp.bfloat16)
        width = out.shape[1] // BANDS
        for band in range(BANDS):
            whole[band, w, rows] = out[:, band * width : (band + 1) * width]

    def send(to_x, to_y, extra, first):
        at = pl.ds(pl.multiple_of((step - first) * count, count), count)
        to_x[:, at] = whole[chip % 2, :, rows]
        to_y[:, at] = whole[1 - chip // 2, :, rows]
        extra[:, at] = whole[chip // 2, :, rows]

    pl.when(step < half)(lambda: send(x0, y0, extra_x, 0))
    pl.when(step >= half)(lambda: send(x1, y1, extra_y, half))


def whiten(spectra, counted):
    windows, channels, width = spectra.shape
    band_width = width // BANDS
    rows = 2 * TILE
    part = jax.ShapeDtypeStruct((windows, channels // 2, band_width), jnp.bfloat16)
    whole = jax.ShapeDtypeStruct((BANDS, windows, channels, band_width), jnp.bfloat16)
    return pl.pallas_call(
        whiten_kernel,
        grid=(channels // rows,),
        in_specs=[
            pl.BlockSpec(memory_space=pltpu.SMEM),
            pl.BlockSpec((windows, rows, width), lambda i: (0, i, 0)),
        ],
        out_specs=in_vmem(7),
        out_shape=[whole] + [part] * 6,
        compiler_params=params(WHITEN_LIMIT),
        cost_estimate=SMALL,
    )(counted, *in_hbm([spectra]))


def product(left, right, weight):
    total = None
    for rows, columns in zip(left, right):
        width = columns.shape[1] // 2
        turned = jnp.concatenate([-columns[:, width:], columns[:, :width]], axis=1)
        both = jnp.concatenate([columns, turned], axis=0)
        part = lax.dot_general(
            rows, both, (((1,), (1,)), ((), ())), preferred_element_type=jnp.float32
        )
        total = part if total is None else total + part
    return (total * weight).astype(jnp.bfloat16)


def tile_rows(tile):
    return pl.ds(pl.multiple_of(tile * TILE, TILE), TILE)


def each_unit(out):
    core = lax.axis_index("seg") % 2
    kept, *sent = out
    span = LAYERS // len(sent)
    for layer in range(LAYERS):
        yield layer, core, kept.at[layer]
    for layer in range(LAYERS):
        yield layer, 1 - core, sent[layer // span].at[layer % span]


def own_kernel(weight, whole, *out):
    for layer, core, ref in each_unit(out):
        band, q = layer // 2, 2 * (layer % 2) + core
        windows = range(whole.shape[1])
        ref[...] = product(
            [whole[band, w] for w in windows],
            [whole[band, w, tile_rows(q)] for w in windows],
            weight[0],
        )


def pair_kernel(weight, whole, from_x, from_y, *out):
    chip = lax.axis_index("blk")
    bands = (1 - chip % 2, chip // 2)
    half = from_x.shape[1]
    for layer, core, ref in each_unit(out):
        along = layer // 2
        arrived, q = (from_x, from_y)[along], layer % 2
        rows = pl.ds(pl.multiple_of(core * half, half), half)
        windows = range(whole.shape[1])
        ref[...] = product(
            [whole[bands[along], w, rows] for w in windows],
            [arrived[w, tile_rows(q)] for w in windows],
            weight[0],
        )


def corner_kernel(weight, x0, x1, y0, y1, extra_x, extra_y, *out):
    chip = lax.axis_index("blk")
    windows = range(x0.shape[0])

    def multiply(left, right, tile, ref):
        ref[...] = product(left, [right[w, tile_rows(tile)] for w in windows], weight[0])

    def split(one, two, extra_one, extra_two):
        for layer, core, ref in each_unit(out):
            if layer < LAYERS // 2:
                multiply([extra_one[w] for w in windows], two[layer], core, ref)
            else:
                left = [jnp.where(core == 0, one[0][w], one[1][w]) for w in windows]
                multiply(left, extra_two, layer - LAYERS // 2, ref)

    def joined(one, two):
        for layer, core, ref in each_unit(out):
            multiply([one[layer // 2][w] for w in windows], two[layer % 2], core, ref)

    x, y = (x0, x1), (y0, y1)
    pl.when(chip == 0)(lambda: split(x, y, extra_x, extra_y))
    pl.when(chip == 1)(lambda: joined(y, x))
    pl.when(chip == 2)(lambda: joined(x, y))
    pl.when(chip == 3)(lambda: split(y, x, extra_y, extra_x))


def in_vmem(count):
    return [pl.BlockSpec(memory_space=pltpu.VMEM)] * count


def unit_call(kernel, rows, weight, *arrays, pieces=1):
    shapes = [(LAYERS, rows, 2 * TILE)] + [(LAYERS // pieces, rows, 2 * TILE)] * pieces
    return pl.pallas_call(
        kernel,
        in_specs=[pl.BlockSpec(memory_space=pltpu.SMEM)] + in_vmem(len(arrays)),
        out_specs=in_vmem(1 + pieces),
        out_shape=[jax.ShapeDtypeStruct(shape, jnp.bfloat16) for shape in shapes],
        compiler_params=params(),
        cost_estimate=SMALL,
    )(weight, *arrays)


def pair_sum_kernel(kept, got, *outs):
    layer = lax.axis_index("seg") // 2
    for r, out in enumerate(outs):
        at = lax.rem(layer + r, LAYERS)
        out[...] = (kept[at].astype(jnp.float32) + got[at].astype(jnp.float32)).astype(jnp.bfloat16)


def pair_sum(kept, got):
    shape = jax.ShapeDtypeStruct(kept.shape[1:], jnp.bfloat16)
    return pl.pallas_call(
        pair_sum_kernel,
        in_specs=in_vmem(2),
        out_specs=in_vmem(LAYERS),
        out_shape=[shape] * LAYERS,
        compiler_params=params(),
        cost_estimate=SMALL,
    )(kept, got)


def halve_kernel(bit, kept, *refs):
    layer = lax.axis_index("seg") // 2
    mine = lax.rem(layer // bit, 2)
    *got, keep, send = refs
    count = kept.shape[0] // 2
    for out, side in ((keep, mine), (send, 1 - mine)):
        for n in range(count):
            at = 2 * n + side if bit == 1 else side
            theirs = got[n][side] if bit == 1 else got[0][side]
            value = kept[at].astype(jnp.float32) + theirs.astype(jnp.float32)
            out[n] = value.astype(out.dtype)


def halve(bit, kept, got):
    shape = (kept.shape[0] // 2,) + kept.shape[1:]
    return pl.pallas_call(
        functools.partial(halve_kernel, bit),
        in_specs=in_vmem(1 + len(got)),
        out_specs=in_vmem(2),
        out_shape=[jax.ShapeDtypeStruct(shape, t) for t in (jnp.float32, jnp.bfloat16)],
        compiler_params=params(),
        cost_estimate=SMALL,
    )(kept, *got)


def layer_sum(parts):
    total = parts[0][...].astype(jnp.float32)
    for part in parts[1:]:
        total = total + part[...].astype(jnp.float32)
    return total.astype(jnp.bfloat16)


def tile_powers(rows, table):
    velocities = table.shape[1] // 2
    field = lax.dot_general(
        rows, table, (((1,), (0,)), ((), ())), preferred_element_type=jnp.float32
    )
    squared = field * field
    energy = squared[:, :velocities] + squared[:, velocities:]
    return [
        jnp.sum(energy[t : t + TILE], axis=0, keepdims=True) * (1.0 / TILE)
        for t in range(0, rows.shape[0], TILE)
    ]


def transposed(stacked):
    rounded = stacked.astype(jnp.float32)
    turned = []
    for t in range(0, stacked.shape[0], TILE):
        tile = rounded[t : t + TILE]
        turned.append(jnp.concatenate([tile[:, :TILE].T, -tile[:, TILE:].T], axis=1))
    return jnp.concatenate(turned, axis=0).astype(jnp.bfloat16)


def matrix_kernel(phases, matrix):
    rows, velocities = phases.shape[1:]
    norm_factor = 1.0 / math.sqrt(TILE)
    for band in range(phases.shape[0]):
        cosine = (jnp.cos(phases[band]) * norm_factor).astype(jnp.bfloat16)
        sine_part = (jnp.sin(phases[band]) * norm_factor).astype(jnp.bfloat16)
        matrix[band, :rows, :velocities] = cosine
        matrix[band, :rows, velocities:] = sine_part
        matrix[band, rows:, :velocities] = -sine_part
        matrix[band, rows:, velocities:] = cosine


def matrix_of(phases):
    bands, rows, velocities = phases.shape
    return pl.pallas_call(
        matrix_kernel,
        in_specs=in_vmem(1),
        out_specs=in_vmem(1)[0],
        out_shape=jax.ShapeDtypeStruct((bands, 2 * rows, 2 * velocities), jnp.bfloat16),
        compiler_params=params(),
        cost_estimate=SMALL,
    )(phases)


def power_kernel(group, matrix, *refs):
    out = refs[-1]
    chip, me = lax.axis_index("blk"), lax.axis_index("seg")
    if group == "own":
        band = me // QUAD
    elif group == "pair":
        band = jnp.where(me < QUAD, 1 - chip % 2, chip // 2)
    else:
        band = jnp.where((chip == 1) | (chip == 2), chip - 1, me // QUAD)
    stacked = layer_sum(refs[:-1])
    table = matrix[band]
    found = tile_powers(stacked, table)
    if group == "pair":
        found += tile_powers(transposed(stacked), table)
    for t, row in enumerate(found):
        out[t : t + 1, :] = row


def powers_of(group, matrix, parts):
    velocities = matrix.shape[2] // 2
    rows = parts[0].shape[0] // TILE * (2 if group == "pair" else 1)
    return pl.pallas_call(
        functools.partial(power_kernel, group),
        in_specs=in_vmem(1 + len(parts)),
        out_specs=in_vmem(1)[0],
        out_shape=jax.ShapeDtypeStruct((rows, velocities), jnp.float32),
        compiler_params=params(),
        cost_estimate=SMALL,
    )(matrix, *parts)


def across(array, hops):
    return lax.ppermute(array, "blk", hops)


def other_core(array):
    return lax.ppermute(array, "seg", [(i, i ^ 1) for i in range(UNITS)])


def layers_on(array, r):
    return lax.ppermute(array, "seg", [(i, (i + 2 * r) % UNITS) for i in range(UNITS)])


def from_layers(array):
    return jnp.stack([array] + [layers_on(array, r) for r in range(1, LAYERS)])


def grid_body(spectra, window_count, tile_owner, phases):
    chip = lax.axis_index("blk")
    me = lax.axis_index("seg")
    whole, x0, y0, x1, y1, extra_x, extra_y = whiten(spectra[0], window_count)
    x0, y0 = across(x0, X_SWAP), across(y0, Y_SWAP)
    x1, y1 = across(x1, X_SWAP), across(y1, Y_SWAP)
    extra_x, extra_y = across(extra_x, X_EXTRA), across(extra_y, Y_EXTRA)

    weight = 1.0 / (window_count.astype(jnp.float32) * math.sqrt(FB * UNITS))
    matrix = matrix_of(phases)
    channels = whole.shape[2]

    def sums_of(kernel, rows, weight, earlier, *arrays):
        kept, sent = unit_call(kernel, rows, weight, *arrays)
        sent, *earlier = lax.optimization_barrier((sent, *earlier))
        return pair_sum(kept, other_core(sent)), earlier

    def along_layers(sums):
        return [sums[0]] + [layers_on(sums[r], r) for r in range(1, LAYERS)]

    kept, *sent = unit_call(own_kernel, channels, weight, whole, pieces=2)
    got = [other_core(piece) for piece in sent]
    for bit in (1, 2):
        kept, sent = halve(bit, kept, got)
        got = [lax.ppermute(sent, "seg", [(i, i ^ (2 * bit)) for i in range(UNITS)])]
    own = [kept[0], got[0][0]]
    own = powers_of("own", matrix, own)
    half = channels // 2
    pair0, (own,) = sums_of(pair_kernel, half, weight, [own], whole, x0, y0)
    pair0 = along_layers(pair0)
    pair0 = powers_of("pair", matrix, pair0)
    weight, pair0 = lax.optimization_barrier((weight, pair0))
    pair1 = along_layers(sums_of(pair_kernel, half, weight, [], whole, x1, y1)[0])
    sums, pair1 = sums_of(corner_kernel, half, weight, pair1, x0, x1, y0, y1, extra_x, extra_y)
    corner = along_layers(sums)
    owner_row, *pair1 = lax.optimization_barrier((tile_owner[0], *pair1, *sums))[: 1 + LAYERS]
    mine, mine_filled = my_slots(owner_row, UNITS)
    sources = jnp.asarray(SOURCE_ROWS)[chip, me][mine]
    pair1 = powers_of("pair", matrix, pair1)
    tiles = pair0.shape[0] // 2
    turned = jnp.concatenate([pair0[tiles:], pair1[tiles:]], axis=0)
    turned = lax.ppermute(turned, ("blk", "seg"), TURNED_HOPS)
    near = jnp.concatenate([own, pair0[:tiles], pair1[:tiles], turned], axis=0)
    far = other_core(near)
    last = powers_of("corner", matrix, corner)
    corners = jnp.concatenate([across(last, X_CORNER), across(last, Y_CORNER)], axis=0)
    rows = jnp.concatenate([near, far, corners, other_core(corners)], axis=0)
    every = from_layers(rows)
    response = jnp.take(every.reshape(-1, every.shape[-1]), sources, axis=0)
    response = response * mine_filled[:, None, None].astype(jnp.float32)
    return response[None, None]


def solution(mesh):
    placed = (P("seg", None, "blk", None), P("seg"), P("blk", None), P())
    fits = mesh.shape["blk"] == CHIPS and mesh.shape["seg"] == UNITS
    return jax.shard_map(
        grid_body if fits else ring_body,
        mesh=mesh,
        in_specs=placed,
        out_specs=P("blk", "seg", None, None, None),
        check_vma=False,
    )
```
